32 devices in a mesh: section: 2 (over y), tensor: 4 (over x, core), dp: 4 (over z).
Axes of the slice: x: 2, y: 2, z: 4, core: 2. Of those that a mesh axis runs over, the one named last changes fastest.
Arguments:
- block_input: bfloat16 [2, 1024, 4, 767], P(None, 'tensor', 'dp'), may hold values from -6 to 6
- segments: int32 [2, 4, 1024], P(None, 'dp'), may hold values from 0 to 3, as said below
- cotangent: bfloat16 [2, 1024, 4, 767], P(None, 'tensor', 'dp'), may hold values from -6 to 6
- attn_gain: bfloat16 [2, 768], P('section'), may hold values from 0.5 to 1.5
- qkv_weight: bfloat16 [2, 768, 3, 768], P('section', None, None, 'tensor'), may hold values from -0.21875 to 0.21875
- qv_bias: bfloat16 [2, 2, 768], P('section', None, 'tensor'), may hold values from -0.59765625 to 0.59765625
- out_weight: bfloat16 [2, 768, 768], P('section', 'tensor'), may hold values from -1.25 to 1.25
- out_bias: bfloat16 [2, 768], P('section'), may hold values from -1.796875 to 1.796875
- mlp_gain: bfloat16 [2, 768], P('section'), may hold values from 0.5 to 1.5
- up_projection_weight: bfloat16 [2, 768, 3072], P('section', None, 'tensor'), may hold values from -0.21875 to 0.21875
- up_bias: bfloat16 [2, 3072], P('section', 'tensor'), may hold values from -1.796875 to 1.796875
- down_projection_weight: bfloat16 [2, 768, 3072], P('section', None, 'tensor'), may hold values from -0.109375 to 0.109375
- down_bias: bfloat16 [2, 768], P('section'), may hold values from -1.796875 to 1.796875
Outputs:
- activations: bfloat16 [2, 2, 1024, 4, 767], P('section', None, 'tensor', 'dp')
- entry_grads: float32 [2, 2, 1024, 4, 767], P('section', None, 'tensor', 'dp')
- attn_gain_grad: float32 [2, 768], P('section')
- qkv_weight_grad: float32 [2, 768, 3, 768], P('section', None, None, 'tensor')
- qv_bias_grad: float32 [2, 2, 768], P('section', None, 'tensor')
- out_weight_grad: float32 [2, 768, 768], P('section', 'tensor')
- out_bias_grad: float32 [2, 768], P('section')
- mlp_gain_grad: float32 [2, 768], P('section')
- up_weight_grad: float32 [2, 768, 3072], P('section', None, 'tensor')
- up_bias_grad: float32 [2, 3072], P('section', 'tensor')
- down_weight_grad: float32 [2, 768, 3072], P('section', None, 'tensor')
- down_bias_grad: float32 [2, 768], P('section')
The draws below stay inside these ranges and needn't reach their ends.
Inputs may be any that keep to these rules, and one draw needn't show every extreme that they name: `segments`: along each packed row of 1024 positions the segment numbers start at 0, never fall, and rise by one at each document boundary.
All inputs are finite; a program needn't handle non-finite values.
Results may differ from the reference program's by a relative error of at most 0.035.
Values may be sent and summed in bfloat16 or wider, within the bound.
A program may use at most 192 MiB of HBM per device.

```python
import jax
import jax.numpy as jnp
from jax import lax

D = 768
HD = 64
FF = 3072
LEN = 1024
MICRO = 2
DS = 767
LAYERS = 2
SHARE = 256
SEQ_ALL = 4


def draw_segments(key, part):
    key = jax.random.fold_in(key, 7)
    row_count = MICRO * SEQ_ALL
    longest = max(1, (SHARE - 1) // 3)
    length_key, split_key = jax.random.split(key)
    lengths = jax.random.randint(length_key, (row_count, 3), 1, longest + 1)
    before = jax.random.randint(split_key, (row_count, 1), 0, 4)
    column = jnp.arange(3)[None, :]
    ahead = jnp.cumsum(lengths, axis=1)
    behind = jnp.cumsum(lengths[:, ::-1], axis=1)[:, ::-1]
    bounds = jnp.where(column < before, ahead, LEN - behind)
    places = jnp.arange(LEN)
    numbers = jnp.sum((bounds[:, :, None] <= places[None, None, :]).astype(jnp.int32), axis=1)
    return numbers.reshape(MICRO, SEQ_ALL, LEN).astype(jnp.int32)


def shard_levels(rng, dims, pieces, least, largest):
    factor_of = 1.0
    for position, blocks in pieces:
        steps = jax.random.uniform(jax.random.fold_in(jax.random.fold_in(rng, 6), position), (blocks,), jnp.float32, least / len(pieces), largest / len(pieces))
        factor_of = factor_of * jnp.repeat(jnp.exp(steps), dims[position] // blocks).reshape((-1,) + (1,) * (len(dims) - 1 - position))
    return factor_of


def bell_draw(own_key, dims, scale, reach, shards=(), dtype=jnp.bfloat16):
    result = jax.random.normal(own_key, dims, jnp.float32) * scale
    if len(shards) > 0:
        result = shard_levels(own_key, dims, shards, -0.22, 0.18) * result
    return jnp.clip(result, min=-reach, max=reach).astype(dtype)


def setup_inputs(seed: int = 0) -> dict:
    arg_keys = jax.random.split(jax.random.key(seed), 14)
    return {
        "block_input": bell_draw(arg_keys[0], (MICRO, LEN, SEQ_ALL, DS), 1.0, 6.0, ((1, 4), (2, 4))),
        "segments": draw_segments(jax.random.fold_in(arg_keys[13], 71), 0),
        "cotangent": bell_draw(arg_keys[2], (MICRO, LEN, SEQ_ALL, DS), 1.0, 6.0, ((1, 4), (2, 4))),
        "attn_gain": jnp.clip(1.0 + 0.1 * jax.random.normal(arg_keys[3], (LAYERS, D), jnp.float32), 0.5, 1.5).astype(jnp.bfloat16),
        "qkv_weight": bell_draw(arg_keys[4], (LAYERS, D, 3, D), D ** -0.5, 0.21875, ((0, 2), (3, 4))),
        "qv_bias": bell_draw(arg_keys[5], (LAYERS, 2, D), 0.1, 0.59765625, ((0, 2), (2, 4))),
        "out_weight": bell_draw(arg_keys[6], (LAYERS, D, D), (D // 32) ** -0.5, 1.25, ((0, 2), (1, 4))),
        "out_bias": bell_draw(arg_keys[7], (LAYERS, D), 0.3, 1.796875, ((0, 2),)),
        "mlp_gain": jnp.clip(1.0 + 0.1 * jax.random.normal(arg_keys[8], (LAYERS, D), jnp.float32), 0.5, 1.5).astype(jnp.bfloat16),
        "up_projection_weight": bell_draw(arg_keys[9], (LAYERS, D, FF), D ** -0.5, 0.21875, ((0, 2), (2, 4))),
        "up_bias": bell_draw(arg_keys[10], (LAYERS, FF), 0.3, 1.796875, ((0, 2), (1, 4))),
        "down_projection_weight": bell_draw(arg_keys[11], (LAYERS, D, FF), FF ** -0.5, 0.109375, ((0, 2), (2, 4))),
        "down_bias": bell_draw(arg_keys[12], (LAYERS, D), 0.3, 1.796875, ((0, 2),)),
    }


@jax.custom_vjp
def low(v):
    return lax.optimization_barrier(v.astype(jnp.bfloat16)).astype(jnp.float32)

@jax.custom_vjp
def low_back(v):
    return v

def low_keep(v):
    return (low(v), None)

def low_pass(kept, grad):
    return (grad,)

def back_keep(v):
    return (v, None)

def back_low(kept, grad):
    return (low(grad),)
low.defvjp(low_keep, low_pass)
low_back.defvjp(back_keep, back_low)
EPS = 1e-05
SCALE = 0.125
NEGATIVE = -1e+30
HIGHEST = lax.Precision.HIGHEST

def rounded_both(value):
    return low_back(low(value))

def expand(residual):
    return jnp.concatenate([residual, -lax.optimization_barrier(jnp.sum(residual, axis=-1, keepdims=True))], axis=-1)

def shrink(branch):
    return branch[..., :-1] - lax.optimization_barrier(jnp.mean(branch, axis=-1, keepdims=True))

def crms(residual, gain):
    full = expand(residual)
    factor = lax.rsqrt(lax.optimization_barrier(jnp.mean(full * full, axis=-1, keepdims=True)) + EPS)
    return full * factor * gain

def attend(query, keys, values, segment):
    places = jnp.arange(segment.shape[0])
    allowed = (segment[:, None] == segment[None, :]) & (places[None, :] <= places[:, None])
    scores = low_back(jnp.einsum('qhd,khd->hqk', query, keys, precision=HIGHEST) * SCALE)
    probs = jax.nn.softmax(jnp.where(allowed[None], scores, NEGATIVE), axis=-1)
    return jnp.einsum('hqk,khd->qhd', low(probs), values, precision=HIGHEST)

def to_rows(array):
    micro, length, seqs, width = array.shape
    return array.transpose(0, 2, 1, 3).reshape(micro * seqs, length, width // HD, HD)

def from_rows(array, micro, seqs):
    count, length, heads, depth = array.shape
    return array.reshape(micro, seqs, length, heads * depth).transpose(0, 2, 1, 3)

def layer(residual, segment_rows, params):
    attn_gain, qkv_weight, qv_bias, out_weight, out_bias, mlp_gain, up_projection_weight, up_bias, down_projection_weight, down_bias = params
    micro = residual.shape[0]
    seqs = residual.shape[2]
    normed = low(crms(residual, attn_gain))
    query = rounded_both(jnp.einsum('mlsd,de->mlse', normed, qkv_weight[:, 0], precision=HIGHEST) + qv_bias[0])
    keys = rounded_both(jnp.einsum('mlsd,de->mlse', normed, qkv_weight[:, 1], precision=HIGHEST))
    values = rounded_both(jnp.einsum('mlsd,de->mlse', normed, qkv_weight[:, 2], precision=HIGHEST) + qv_bias[1])
    checked = jax.checkpoint(attend)
    context = lax.map(lambda items: checked(items[0], items[1], items[2], items[3]), (to_rows(query), to_rows(keys), to_rows(values), segment_rows))
    context = rounded_both(from_rows(context, micro, seqs))
    attn_out = low_back(jnp.einsum('mlse,ed->mlsd', context, out_weight, precision=HIGHEST) + out_bias)
    middle = residual + shrink(attn_out)
    normed2 = low(crms(middle, mlp_gain))
    pre = low_back(jnp.einsum('mlsd,df->mlsf', normed2, up_projection_weight, precision=HIGHEST) + up_bias)
    hidden_state = low(jax.nn.gelu(pre, approximate=True))
    mlp_out = low_back(jnp.einsum('mlsf,df->mlsd', hidden_state, down_projection_weight, precision=HIGHEST) + down_bias)
    return middle + shrink(mlp_out)

def reference(block_input, segments, cotangent, attn_gain, qkv_weight, qv_bias, out_weight, out_bias, mlp_gain, up_projection_weight, up_bias, down_projection_weight, down_bias):
    weights = tuple((weight.astype(jnp.float32) for weight in (attn_gain, qkv_weight, qv_bias, out_weight, out_bias, mlp_gain, up_projection_weight, up_bias, down_projection_weight, down_bias)))
    segment_rows = segments.reshape(-1, segments.shape[-1]).astype(jnp.int32)

    def forward(residual, bridge, *params):
        first = layer(residual, segment_rows, tuple((param[0] for param in params)))
        inner = low(first)
        last = layer(low_back(inner + bridge), segment_rows, tuple((param[1] for param in params)))
        return (inner, last)
    residual = block_input.astype(jnp.float32)
    bridge = jnp.zeros_like(residual)
    (inner, last), pull = jax.vjp(forward, residual, bridge, *weights)
    grads = pull((jnp.zeros_like(inner), cotangent.astype(jnp.float32)))
    activations = jnp.stack([inner, last]).astype(jnp.bfloat16)
    entry_grads = jnp.stack([grads[0], grads[1]])
    return (activations, entry_grads, grads[2], grads[3], grads[4], grads[5], grads[6], grads[7], grads[8], grads[9], grads[10], grads[11])
```

```python
import jax
import jax.numpy as jnp
from jax import lax
from jax.experimental import pallas as pl
from jax.experimental.pallas import tpu as pltpu
from jax.sharding import PartitionSpec as P

HD = 64
EPS = 1e-05
SCALE = 0.125
NEGATIVE = -1e30
CHUNK = 128
MESH = pl.DeviceIdType.MESH
F32 = jnp.float32
BF16 = jnp.bfloat16
NN = (((1,), (0,)), ((), ()))
NT = (((1,), (1,)), ((), ()))
TN = (((0,), (0,)), ((), ()))
GELU_C = 0.7978845608028654
GELU_A = 0.044715


def dot(left, right, dims=NN):
    return lax.dot_general(left, right, dims, preferred_element_type=F32)


def lane_sum(value):
    return jnp.sum(value, axis=-1, keepdims=True)


def row_sum(value):
    return jnp.sum(value, axis=0, keepdims=True)


def expanded(block):
    value = block.astype(F32)
    lane = lax.broadcasted_iota(jnp.int32, value.shape, 1)
    return jnp.where(lane == value.shape[1] - 1, -lane_sum(value), value)


def norm_factor(full):
    return lax.rsqrt(lane_sum(full * full) * (1.0 / full.shape[1]) + EPS)


def centred(value):
    return value - lane_sum(value) * (1.0 / value.shape[1])


def norm_back(grad, full, gain):
    factor = norm_factor(full)
    weighted = grad * gain
    inner = lane_sum(weighted * full) * (1.0 / full.shape[1])
    gain_grad = row_sum(grad * full * factor)
    return centred(factor * weighted - full * (factor * factor * factor * inner)), gain_grad


def make_kernel(names, count):
    def kernel(*refs):
        r = dict(zip(names, refs, strict=True))
        xin, cot = r["xin"], r["cot"]
        vec, segc, segr = r["vec"], r["segc"], r["segr"]
        act, eg, grads, small = r["act"], r["eg"], r["grads"], r["small"]
        wq, wo, wu, wd, bc, ub = r["wq"], r["wo"], r["wu"], r["wd"], r["bc"], r["ub"]
        xbuf, cotb, hop, resb = r["xbuf"], r["cotb"], r["hop"], r["resb"]
        pool, nrm, n2t = r["pool"], r["nrm"], r["n2t"]
        qt, kt, vt, ctx, lse = r["qt"], r["kt"], r["vt"], r["ctx"], r["lse"]
        gp, hid, gpre, gmt, gat = r["gp"], r["hid"], r["gpre"], r["gmt"], r["gat"]
        dot_, dqkv, dk, dv = r["dot"], r["dqkv"], r["dk"], r["dv"]
        ex, xrec, cin, fin = r["ex"], r["xrec"], r["cin"], r["fin"]
        sown, soth, srec, scin, sfin = r["sown"], r["soth"], r["srec"], r["scin"], r["sfin"]
        sl, sg, se, sh, so, sr, sc, ss, credit = (
            r["sl"], r["sg"], r["se"], r["sh"], r["so"], r["sr"], r["sc"], r["ss"], r["credit"])
        blocks, rows, width = xbuf.shape
        length = blocks * rows
        slots, hs = wq.shape[0], wo.shape[1] // HD
        heads = slots * hs
        part = wo.shape[1]
        units = wu.shape[2]

        s = lax.axis_index("section")
        t = lax.axis_index("tensor")
        d = lax.axis_index("dp")
        core, xh = lax.rem(t, 2), lax.div(t, 2)
        t_core = 2 * xh + 1 - core
        t_x = 2 * (1 - xh) + core
        to_core = (s, t_core, d)
        to_x = (s, t_x, d)
        to_y = (1 - s, t, d)
        parity = lax.rem(d, 2)
        to_pair = (s, t, d + 1 - 2 * parity)
        left, right = (s, t, d - 1), (s, t, d + 1)

        def send(src, dst, sems, at, device):
            return pltpu.make_async_remote_copy(
                src_ref=src, dst_ref=dst, send_sem=sems.at[(0, *at)], recv_sem=sems.at[(1, *at)],
                device_id=device, device_id_type=MESH)

        def loop(stop, body):
            def step(i, carry):
                body(i)
                return carry

            lax.fori_loop(0, stop, step, 0)

        barrier = pltpu.get_barrier_semaphore()
        for device in (to_core, to_x, to_y):
            pl.semaphore_signal(barrier, inc=1, device_id=device, device_id_type=MESH)

        @pl.when(d > 0)
        def _():
            pl.semaphore_signal(barrier, inc=1, device_id=left, device_id_type=MESH)

        @pl.when(d < count - 1)
        def _():
            pl.semaphore_signal(barrier, inc=1, device_id=right, device_id_type=MESH)

        ends = jnp.where(d > 0, 1, 0) + jnp.where(d < count - 1, 1, 0)
        pl.semaphore_wait(barrier, 3 + ends)

        def rows_in(source, target, which):
            return (
                pltpu.make_async_copy(source.at[xh], target.at[t], sl.at[which]),
                send(source.at[1 - xh], target.at[t], sg, (which,), to_x),
                send(source.at[xh], target.at[t], sg, (which + 2,), to_core),
                send(target.at[t_x], target.at[t_x], sg, (which + 4,), to_core),
            )

        def rows_wait(copies):
            local, across, core_own, core_other = copies
            local.wait()
            across.wait_recv()
            core_other.start()
            core_own.wait()
            core_other.wait()
            across.wait_send()

        x_copies = rows_in(xin, xbuf, 0)
        cot_copies = rows_in(cot, cotb, 1)
        for copy in x_copies[:3]:
            copy.start()

        bias_copies = []
        for which, (source, target) in enumerate(((r["bch"], bc), (r["ubh"], ub))):
            bias_copies.append(pltpu.make_async_copy(source, target.at[0], sl.at[2 + which]))
            bias_copies.append(send(source, target.at[1], sg, (6 + which,), to_x))
        weights = []
        for which, (source, target) in enumerate(((r["wqh"], wq), (r["woh"], wo), (r["wuh"], wu), (r["wdh"], wd))):
            half = source.shape[0] // 2
            mine = pl.ds(pl.multiple_of(parity * half, 16), half)
            weights.append((
                pltpu.make_async_copy(source, target.at[0], sl.at[4 + which]),
                send(source.at[mine], target.at[1, mine], sg, (8 + which,), to_x),
                send(target.at[1, mine], target.at[1, mine], sg, (12 + which,), to_pair),
            ))
        for copy in bias_copies:
            copy.start()
        for local, across, _ in weights:
            local.start()
            across.start()
        for copy in cot_copies[:3]:
            copy.start()

        def pass_on(which):
            _, across, pair = weights[which]
            across.wait_recv()
            pair.start()

        def have(which):
            local, across, pair = weights[which]
            local.wait()
            across.wait_send()
            pair.wait()

        sown[...] = jnp.zeros_like(sown)
        soth[...] = jnp.zeros_like(soth)

        attn_gain, mlp_gain, out_bias, down_bias = (vec[i : i + 1, :] for i in range(4))

        def at_row(i):
            return pl.ds(pl.multiple_of(i * rows, rows), rows)

        def mid_at(i):
            return at_row(i)

        def grad_at(i):
            return pl.ds(pl.multiple_of(length + i * rows, rows), rows)

        def ex_at(kind, i):
            return pl.ds(pl.multiple_of(kind * length + i * rows, rows), rows)

        def pair_copy(kind, i):
            return send(ex.at[ex_at(2 * kind, i)], ex.at[ex_at(2 * kind + 1, i)], se, (kind, i), to_core)

        def pair_send(kind, i, value):
            ex[ex_at(2 * kind, i), :] = value.astype(BF16)
            pair_copy(kind, i).start()

        def pair_sum(kind, i):
            pair_copy(kind, i).wait()
            return ex[ex_at(2 * kind, i), :].astype(F32) + ex[ex_at(2 * kind + 1, i), :].astype(F32)

        half_rows = rows // 2
        own_half = pl.ds(pl.multiple_of(core * half_rows, half_rows), half_rows)

        def hop_copy(i):
            return send(resb.at[i, own_half], hop.at[i, own_half], sh, (0, i), to_y)

        def hop_core(i):
            return send(hop.at[i, own_half], hop.at[i, own_half], sh, (1, i), to_core)

        def hop_receive():
            def first(i):
                hop_copy(i).wait_recv()
                hop_core(i).start()

            def second(i):
                hop_copy(i).wait_send()
                hop_core(i).wait()

            loop(blocks, first)
            loop(blocks, second)

        def masked(scores, i, j0, j1, diagonal):
            same = segc[j0:j1, :]
            same = jnp.concatenate([same] * (rows // same.shape[1]), axis=1)
            allowed = same == segr[0:1, i * rows : (i + 1) * rows]
            if diagonal:
                key = lax.broadcasted_iota(jnp.int32, scores.shape, 0)
                query = lax.broadcasted_iota(jnp.int32, scores.shape, 1)
                allowed = allowed & (key <= query)
            return jnp.where(allowed, scores, NEGATIVE)

        def key_parts(i):
            parts = [(i * rows, (i + 1) * rows, True)]
            if i > 0:
                parts.append((0, i * rows, False))
            return parts

        def forward(p):
            @pl.when(p == 0)
            def _():
                rows_wait(x_copies)

            @pl.when(p == 1)
            def _():
                hop_receive()

                @pl.when(s == 1)
                def _():
                    xbuf[...] = hop[...]

                pl.semaphore_signal(credit, inc=1, device_id=to_y, device_id_type=MESH)

            def norm_rows(i):
                full = expanded(xbuf[i])
                nrm[i] = (full * norm_factor(full) * attn_gain).astype(BF16)

            loop(blocks, norm_rows)

            @pl.when(p == 0)
            def _():
                pass_on(0)
                for copy in bias_copies:
                    copy.wait()
                have(0)

            def project(i):
                normed = nrm[i]
                cols = at_row(i)
                for slot in range(slots):
                    three = dot(wq[slot], normed, NT)
                    bias = bc[slot].astype(F32)
                    bias = jnp.concatenate([bias] * (rows // bias.shape[1]), axis=1)
                    query = (three[:part] + bias[:part]).astype(BF16) * SCALE
                    key = three[part : 2 * part].astype(BF16)
                    value = (three[2 * part :] + bias[part:]).astype(BF16)
                    for h in range(hs):
                        at = slice(h * HD, (h + 1) * HD)
                        qt[i, slot * hs + h] = query[at].astype(BF16)
                        kt[slot * hs + h, :, cols] = key[at]
                        vt[slot * hs + h, :, cols] = value[at]

            loop(blocks, project)

            @pl.when(p == 0)
            def _():
                pass_on(1)
                pass_on(2)

            def attend(h):
                key = kt[h].astype(F32).T.astype(BF16)
                for i in range(blocks):
                    cols = slice(i * rows, (i + 1) * rows)
                    parts = key_parts(i)
                    query = qt[i, h]
                    scores = [masked(dot(key[a:b], query), i, a, b, g) for a, b, g in parts]
                    highest = scores[0].max(axis=0, keepdims=True)
                    for score in scores[1:]:
                        highest = jnp.maximum(highest, score.max(axis=0, keepdims=True))
                    total, context = 0.0, 0.0
                    for score, (a, b, _) in zip(scores, parts, strict=True):
                        power = jnp.exp(score - highest)
                        total = total + row_sum(power)
                        context = context + dot(vt[h, :, a:b], power.astype(BF16))
                    ctx[h, :, cols] = (context / total).astype(BF16)
                    lse[i, h] = highest + jnp.log(total)

            loop(heads, attend)

            @pl.when(p == 0)
            def _():
                pass_on(3)
                have(1)

            def out_rows(i):
                context = ctx[:, :, at_row(i)].reshape(heads * HD, rows)
                pair_send(0, i, dot(context, wo[...].reshape(heads * HD, width), TN))

            loop(blocks, out_rows)

            @pl.when(p == 0)
            def _():
                have(2)

            def up_rows(i):
                branch = pair_sum(0, i) + out_bias
                middle = expanded(xbuf[i]) + centred(branch)
                pool[mid_at(i), :] = middle
                normed = middle * norm_factor(middle) * mlp_gain
                n2t[:, at_row(i)] = normed.T.astype(BF16)
                normed = normed.astype(BF16)
                for slot in range(slots):
                    pre = dot(normed, wu[slot]) + ub[slot, 0:1, :].astype(F32)
                    square = pre * pre
                    bend = jnp.tanh(GELU_C * pre * (1.0 + GELU_A * square))
                    grow = 0.5 * (1.0 + bend)
                    hid[slot, i] = (pre * grow).astype(BF16)
                    slope = GELU_C * (1.0 + 3.0 * GELU_A * square)
                    gp[slot, i] = (grow + 0.5 * pre * (1.0 - bend * bend) * slope).astype(BF16)

            loop(blocks, up_rows)

            @pl.when(p == 0)
            def _():
                have(3)

            def down_rows(i):
                branch = dot(hid[0, i], wd[0], NT)
                for slot in range(1, slots):
                    branch = branch + dot(hid[slot, i], wd[slot], NT)
                pair_send(1, i, branch)

            loop(blocks, down_rows)

            def result_rows(i):
                result = pool[mid_at(i), :] + centred(pair_sum(1, i) + down_bias)
                lane = lax.broadcasted_iota(jnp.int32, result.shape, 1)
                resb[i] = jnp.where(lane == width - 1, 0.0, result).astype(BF16)

                @pl.when(p == 0)
                def _():
                    hop_copy(i).start()

            loop(blocks, result_rows)

        def rows_out(target, which):
            return (
                pltpu.make_async_copy(resb.at[t], target.at[xh], sl.at[8 + which]),
                send(resb.at[t_x], target.at[xh], so, (which,), to_x),
            )

        loop(2, forward)
        act_copies = rows_out(act, 0)
        for copy in act_copies:
            copy.start()
        rows_wait(cot_copies)

        def backward(p):
            @pl.when(p == 0)
            def _():
                pl.semaphore_wait(credit, 1)

            @pl.when(p == 1)
            def _():
                hop_receive()

                @pl.when(s == 0)
                def _():
                    cotb[...] = hop[...]

            sown[...] = jnp.zeros_like(sown)
            soth[...] = jnp.zeros_like(soth)

            def down_back(i):
                grad = centred(cotb[i].astype(F32))
                pool[grad_at(i), :] = grad
                gmt[:, at_row(i)] = grad.T.astype(BF16)
                grad = grad.astype(BF16)
                sown[3:4, :] += row_sum(grad.astype(F32))
                branch = 0.0
                for slot, sums in ((0, sown), (1, soth)):
                    before = (dot(grad, wd[slot]) * gp[slot, i].astype(F32)).astype(BF16)
                    gpre[slot, i] = before
                    sums[4:5, :] += row_sum(before.astype(F32))
                    branch = branch + dot(before, wu[slot], NT)
                pair_send(0, i, branch)

            loop(blocks, down_back)

            def out_back(i):
                grad, gain_grad = norm_back(pair_sum(0, i), pool[mid_at(i), :], mlp_gain)
                sown[2:3, :] += gain_grad
                grad = grad + pool[grad_at(i), :]
                pool[grad_at(i), :] = grad
                grad = grad.astype(BF16)
                gat[i] = grad
                sown[1:2, :] += row_sum(grad.astype(F32))
                back = dot(wo[...].reshape(heads * HD, width), grad, NT).astype(BF16)
                for h in range(heads):
                    dot_[i, h] = back[h * HD : (h + 1) * HD]

            loop(blocks, out_back)

            def attend_back(h):
                key_t = kt[h]
                key = key_t.astype(F32).T.astype(BF16)
                value = vt[h].astype(F32).T.astype(BF16)
                slot, place = lax.div(h, hs), lax.rem(h, hs)
                for i in reversed(range(blocks)):
                    query, back = qt[i, h], dot_[i, h]
                    parts = key_parts(i)
                    probs, g_probs = [], []
                    centre = 0.0
                    for a, b, g in parts:
                        prob = jnp.exp(masked(dot(key[a:b], query), i, a, b, g) - lse[i, h])
                        g_prob = dot(value[a:b], back)
                        centre = centre + row_sum(prob * g_prob)
                        probs.append(prob)
                        g_probs.append(g_prob)
                    g_query = 0.0
                    for prob, g_prob, (a, b, _) in zip(probs, g_probs, parts, strict=True):
                        g_score = (prob * (g_prob - centre)).astype(BF16)
                        g_value = dot(back, prob.astype(BF16), NT)
                        g_key = dot(query, g_score, NT)
                        g_query = g_query + dot(key_t[:, a:b], g_score)
                        if i == blocks - 1:
                            dv[:, a:b] = g_value
                            dk[:, a:b] = g_key
                        else:
                            dv[:, a:b] += g_value
                            dk[:, a:b] += g_key
                    dqkv[slot, 0, place, :, i * rows : (i + 1) * rows] = (g_query * SCALE).astype(BF16)
                dqkv[slot, 1, place] = dk[...].astype(BF16)
                dqkv[slot, 2, place] = dv[...].astype(BF16)

            loop(heads, attend_back)

            def qkv_back(i):
                branch = 0.0
                for slot in range(slots):
                    three = dqkv[slot, :, :, :, at_row(i)].reshape(3 * part, rows)
                    branch = branch + dot(three, wq[slot], TN)
                pair_send(1, i, branch)

            loop(blocks, qkv_back)

            @pl.when(p == 0)
            def _():
                for copy in act_copies:
                    copy.wait()

            def in_back(i):
                grad, gain_grad = norm_back(pair_sum(1, i), expanded(xbuf[i]), attn_gain)
                sown[0:1, :] += gain_grad
                grad = grad + pool[grad_at(i), :]
                resb[i] = (grad - grad[:, width - 1 :]).astype(BF16)

                @pl.when(p == 0)
                def _():
                    hop_copy(i).start()

            loop(blocks, in_back)

        loop(2, backward)
        eg_copies = rows_out(eg, 1)
        for copy in eg_copies:
            copy.start()

        chunks = grads.shape[0]

        def x_copy(k):
            return send(ex.at[pl.ds(pl.multiple_of(k * CHUNK, CHUNK), CHUNK)], xrec.at[k], sr, (k,), to_x)

        ones = jnp.ones((8, length), BF16)
        sown[5:6, : 3 * part] = dot(ones, dqkv[0].reshape(3 * part, length), NT)[0:1]
        soth[5:6, : 3 * part] = dot(ones, dqkv[1].reshape(3 * part, length), NT)[0:1]
        soth[0:4, :] = sown[0:4, :]
        small_x = send(soth, srec, ss, (0,), to_x)
        small_x.start()

        def weight_grads(turn):
            slot = 1 - turn

            def put(at, value):
                @pl.when(turn == 0)
                def _():
                    ex[at, :] = value.astype(BF16)

                @pl.when(turn == 1)
                def _():
                    pool[at, :] = value

            def start(first, number):
                @pl.when(turn == 0)
                def _():
                    loop(number, lambda k: x_copy(first + k).start())

            tile = 256
            tiles = width // tile

            def down_part(k):
                at = pl.ds(pl.multiple_of(k * tile, tile), tile)
                put(at, dot(gmt[at, :], hid[slot].reshape(length, units)))

            loop(tiles, down_part)
            start(0, width // CHUNK)

            def up_part(k):
                at = pl.ds(pl.multiple_of(k * tile, tile), tile)
                here = pl.ds(pl.multiple_of(width + k * tile, tile), tile)
                put(here, dot(n2t[at, :], gpre[slot].reshape(length, units)))

            loop(tiles, up_part)
            start(width // CHUNK, width // CHUNK)

            def qkv_part(k):
                here = pl.ds(pl.multiple_of(2 * width + k * part, 64), part)
                put(here, dot(dqkv[slot, k].reshape(part, length), nrm[...].reshape(length, width)))

            loop(3, qkv_part)
            here = pl.ds(2 * width + 3 * part, part)
            context = ctx[pl.ds(slot * hs, hs)].reshape(part, length)
            put(here, dot(context, gat[...].reshape(length, width)))
            start(2 * (width // CHUNK), chunks - 2 * (width // CHUNK))

        loop(2, weight_grads)

        middle = count // 2
        on_left = d < middle
        depth = jnp.where(on_left, d, count - 1 - d)
        has_outer = depth > 0
        is_mid = depth == middle - 1
        side = jnp.where(on_left, 0, 1)
        inner = (s, t, jnp.where(on_left, d + 1, d - 1))
        outer = (s, t, jnp.where(on_left, d - 1, d + 1))
        lag = 2
        lag_in = lag * depth
        lag_mid = lag * middle
        lag_out = lag_mid + lag * (middle - depth)
        lag_all = lag_mid + lag * middle

        def in_copy(k):
            return send(xrec.at[k], cin.at[k], sc, (0, k), inner)

        def cross_copy(k):
            return send(xrec.at[k], fin.at[k], sc, (1, k), inner)

        def back_copy(k):
            return send(fin.at[k], fin.at[k], sc, (2, k), inner)

        def out_copy(k):
            return send(fin.at[k], fin.at[k], sc, (3, k), outer)

        def grads_copy(k):
            return pltpu.make_async_copy(fin.at[k], grads.at[k], so.at[0, 2 + k])

        def reduce(it):
            @pl.when(it < chunks)
            def _():
                k = it
                x_copy(k).wait()
                here = pl.ds(pl.multiple_of(k * CHUNK, CHUNK), CHUNK)
                xrec[k] = (pool[here, :] + xrec[k].astype(F32)).astype(BF16)

            k_in = it - lag_in

            @pl.when((k_in >= 0) & (k_in < chunks))
            def _():
                k = k_in
                owner = lax.rem(k, 2) == side

                @pl.when(has_outer)
                def _():
                    in_copy(k).wait_recv()
                    xrec[k] = (xrec[k].astype(F32) + cin[k].astype(F32)).astype(BF16)

                @pl.when(jnp.logical_not(is_mid))
                def _():
                    in_copy(k).start()

                @pl.when(is_mid & jnp.logical_not(owner))
                def _():
                    cross_copy(k).start()

            k_mid = it - lag_mid

            @pl.when((k_mid >= 0) & (k_mid < chunks) & is_mid)
            def _():
                k = k_mid

                @pl.when(lax.rem(k, 2) == side)
                def _():
                    cross_copy(k).wait_recv()
                    fin[k] = (xrec[k].astype(F32) + fin[k].astype(F32)).astype(BF16)
                    back_copy(k).start()

                    @pl.when(has_outer)
                    def _():
                        out_copy(k).start()

                    grads_copy(k).start()

            k_out = it - lag_out

            @pl.when((k_out >= 0) & (k_out < chunks))
            def _():
                k = k_out
                owner = lax.rem(k, 2) == side

                @pl.when(is_mid & jnp.logical_not(owner))
                def _():
                    back_copy(k).wait_recv()

                @pl.when(jnp.logical_not(is_mid))
                def _():
                    out_copy(k).wait_recv()

                @pl.when(jnp.logical_not(is_mid & owner))
                def _():
                    @pl.when(has_outer)
                    def _():
                        out_copy(k).start()

                    grads_copy(k).start()

        loop(chunks + lag_all, reduce)

        small_x.wait()
        sown[...] = sown[...] + srec[...]
        s_in = send(sown, scin, ss, (1,), inner)
        s_cross = send(sown, sfin, ss, (2,), inner)
        s_back = send(sfin, sfin, ss, (3,), inner)
        s_out = send(sfin, sfin, ss, (4,), outer)
        owner = side == 0

        @pl.when(has_outer)
        def _():
            s_in.wait_recv()
            sown[...] = sown[...] + scin[...]

        @pl.when(jnp.logical_not(is_mid))
        def _():
            s_in.start()
            s_in.wait_send()
            s_out.wait_recv()

        @pl.when(is_mid & jnp.logical_not(owner))
        def _():
            s_cross.start()
            s_cross.wait_send()
            s_back.wait_recv()

        @pl.when(is_mid & owner)
        def _():
            s_cross.wait_recv()
            sfin[...] = sfin[...] + sown[...]
            s_back.start()
            s_back.wait_send()

        @pl.when(has_outer)
        def _():
            s_out.start()
            s_out.wait_send()

        small[...] = sfin[...]

        def drain(k):
            owner = lax.rem(k, 2) == side

            @pl.when(jnp.logical_not(is_mid))
            def _():
                in_copy(k).wait_send()

            @pl.when(is_mid & jnp.logical_not(owner))
            def _():
                cross_copy(k).wait_send()

            @pl.when(is_mid & owner)
            def _():
                back_copy(k).wait_send()

            @pl.when(has_outer)
            def _():
                out_copy(k).wait_send()

            grads_copy(k).wait()

        loop(chunks, drain)
        for copy in eg_copies:
            copy.wait()

    return kernel


def per_device(
    block_input,
    segments,
    cotangent,
    attn_gain,
    qkv_weight,
    qv_bias,
    out_weight,
    out_bias,
    mlp_gain,
    up_projection_weight,
    up_bias,
    down_projection_weight,
    down_bias,
):
    micros, rows, _, kept = block_input.shape
    width = qkv_weight.shape[1]
    part = qkv_weight.shape[3]
    units = up_projection_weight.shape[2]
    blocks = lax.axis_size("tensor")
    count = lax.axis_size("dp")
    length = blocks * rows
    slots = 2
    hs = part // HD
    heads = slots * hs
    chunks = (2 * width + 4 * part) // CHUNK

    def padded(array):
        return jnp.pad(array[:, :, 0, :], ((0, 0), (0, 0), (0, width - kept)))

    micro = lax.axis_index("tensor") // 2
    segment = lax.dynamic_index_in_dim(segments[:, 0, :], micro, 0, keepdims=False)
    vec = jnp.concatenate([attn_gain, mlp_gain, out_bias, down_bias] * 2).astype(F32)
    inputs = {
        "xin": padded(block_input),
        "cot": padded(cotangent),
        "wqh": qkv_weight[0].transpose(1, 2, 0).reshape(3 * part, width),
        "woh": out_weight[0],
        "wuh": up_projection_weight[0],
        "wdh": down_projection_weight[0],
        "bch": jnp.broadcast_to(qv_bias[0].reshape(2 * part, 1), (2 * part, 128)),
        "ubh": jnp.broadcast_to(up_bias, (16, units)),
        "vec": vec,
        "segc": jnp.broadcast_to(segment[:, None], (length, 128)),
        "segr": jnp.broadcast_to(segment[None, :], (8, length)),
    }
    outputs = {
        "act": ((micros, rows, width), BF16),
        "eg": ((micros, rows, width), BF16),
        "grads": ((chunks, CHUNK, width), BF16),
        "small": ((8, width), F32),
    }
    scratch = {
        "wq": ((slots, 3 * part, width), BF16),
        "wo": ((slots, part, width), BF16),
        "wu": ((slots, width, units), BF16),
        "wd": ((slots, width, units), BF16),
        "bc": ((slots, 2 * part, 128), BF16),
        "ub": ((slots, 16, units), BF16),
        "xbuf": ((blocks, rows, width), BF16),
        "cotb": ((blocks, rows, width), BF16),
        "hop": ((blocks, rows, width), BF16),
        "resb": ((blocks, rows, width), BF16),
        "pool": ((max(2 * length, chunks * CHUNK), width), F32),
        "nrm": ((blocks, rows, width), BF16),
        "n2t": ((width, length), BF16),
        "qt": ((blocks, heads, HD, rows), BF16),
        "kt": ((heads, HD, length), BF16),
        "vt": ((heads, HD, length), BF16),
        "ctx": ((heads, HD, length), BF16),
        "lse": ((blocks, heads, 1, rows), F32),
        "gp": ((slots, blocks, rows, units), BF16),
        "hid": ((slots, blocks, rows, units), BF16),
        "gpre": ((slots, blocks, rows, units), BF16),
        "gmt": ((width, length), BF16),
        "gat": ((blocks, rows, width), BF16),
        "dot": ((blocks, heads, HD, rows), BF16),
        "dqkv": ((slots, 3, hs, HD, length), BF16),
        "dk": ((HD, length), F32),
        "dv": ((HD, length), F32),
        "ex": ((4 * length, width), BF16),
        "xrec": ((chunks, CHUNK, width), BF16),
        "cin": ((chunks, CHUNK, width), BF16),
        "fin": ((chunks, CHUNK, width), BF16),
        "sown": ((8, width), F32),
        "soth": ((8, width), F32),
        "srec": ((8, width), F32),
        "scin": ((8, width), F32),
        "sfin": ((8, width), F32),
    }
    dma = pltpu.SemaphoreType.DMA
    semaphores = {
        "sl": dma((10,)),
        "sg": dma((2, 16)),
        "se": dma((2, 2, blocks)),
        "sh": dma((2, 2, blocks)),
        "so": dma((2, 2 + chunks)),
        "sr": dma((2, chunks)),
        "sc": dma((2, 4, chunks)),
        "ss": dma((2, 5)),
        "credit": pltpu.SemaphoreType.REGULAR,
    }
    in_vmem = {"vec", "segc", "segr", "small"}

    def spec(name):
        return pl.BlockSpec(memory_space=pltpu.VMEM if name in in_vmem else pl.ANY)

    names = [*inputs, *outputs, *scratch, *semaphores]
    act, eg, grads, small = pl.pallas_call(
        make_kernel(names, count),
        out_shape=[jax.ShapeDtypeStruct(*item) for item in outputs.values()],
        in_specs=[spec(name) for name in inputs],
        out_specs=[spec(name) for name in outputs],
        scratch_shapes=[pltpu.VMEM(*item) for item in scratch.values()] + list(semaphores.values()),
        compiler_params=pltpu.CompilerParams(
            collective_id=0, has_side_effects=True, vmem_limit_bytes=63 * 1024 * 1024
        ),
        name="layers",
    )(*inputs.values())

    grads = grads.reshape(chunks * CHUNK, width).astype(F32)
    down, up, qkv, out = jnp.split(grads, [width, 2 * width, 2 * width + 3 * part])
    qv = small[5, : 3 * part].reshape(3, part)
    return (
        act[None, :, :, None, :kept],
        eg[None, :, :, None, :kept].astype(F32),
        small[0:1],
        qkv.reshape(3, part, width).transpose(2, 0, 1)[None],
        qv[0::2][None],
        out[None],
        small[1:2],
        small[2:3],
        up[None],
        small[4:5, :units],
        down[None],
        small[3:4],
    )


def solution(mesh):
    in_specs = (
        P(None, "tensor", "dp", None),
        P(None, "dp", None),
        P(None, "tensor", "dp", None),
        P("section", None),
        P("section", None, None, "tensor"),
        P("section", None, "tensor"),
        P("section", "tensor", None),
        P("section", None),
        P("section", None),
        P("section", None, "tensor"),
        P("section", "tensor"),
        P("section", None, "tensor"),
        P("section", None),
    )
    out_specs = (
        P("section", None, "tensor", "dp", None),
        P("section", None, "tensor", "dp", None),
        P("section", None),
        P("section", None, None, "tensor"),
        P("section", None, "tensor"),
        P("section", "tensor", None),
        P("section", None),
        P("section", None),
        P("section", None, "tensor"),
        P("section", "tensor"),
        P("section", None, "tensor"),
        P("section", None),
    )
    return jax.shard_map(
        per_device, mesh=mesh, in_specs=in_specs, out_specs=out_specs, check_vma=False
    )
```

```python
import jax
import jax.numpy as jnp
from jax import lax
from jax.experimental import pallas as pl
from jax.experimental.pallas import tpu as pltpu
from jax.sharding import PartitionSpec as P

HD = 64
EPS = 1e-05
SCALE = 0.125
NEGATIVE = -1e30
CHUNK = 64
MESH = pl.DeviceIdType.MESH
F32 = jnp.float32
BF16 = jnp.bfloat16
NN = (((1,), (0,)), ((), ()))
NT = (((1,), (1,)), ((), ()))
TN = (((0,), (0,)), ((), ()))
GELU_C = 0.7978845608028654
GELU_A = 0.044715


def dot(left, right, dims=NN):
    return lax.dot_general(left, right, dims, preferred_element_type=F32)


def lane_sum(value):
    return jnp.sum(value, axis=-1, keepdims=True)


def row_sum(value):
    return jnp.sum(value, axis=0, keepdims=True)


def expanded(block):
    value = block.astype(F32)
    lane = lax.broadcasted_iota(jnp.int32, value.shape, 1)
    return jnp.where(lane == value.shape[1] - 1, -lane_sum(value), value)


def norm_factor(full):
    return lax.rsqrt(lane_sum(full * full) * (1.0 / full.shape[1]) + EPS)


def centred(value):
    return value - lane_sum(value) * (1.0 / value.shape[1])


def norm_back(grad, full, gain):
    factor = norm_factor(full)
    weighted = grad * gain
    inner = lane_sum(weighted * full) * (1.0 / full.shape[1])
    gain_grad = row_sum(grad * full * factor)
    return centred(factor * weighted - full * (factor * factor * factor * inner)), gain_grad


def make_kernel(names, count):
    def kernel(*refs):
        r = dict(zip(names, refs, strict=True))
        xin, cot, misc, seg = r["xin"], r["cot"], r["misc"], r["seg"]
        act, eg, small = r["act"], r["eg"], r["small"]
        wq, wo, wu, wd, mc = r["wq"], r["wo"], r["wu"], r["wd"], r["mc"]
        xbuf, cotb, resb, outt = r["xbuf"], r["cotb"], r["resb"], r["outt"]
        pool, nrm, n2t = r["pool"], r["nrm"], r["n2t"]
        qt, kt, vt, kn, vn = r["qt"], r["kt"], r["vt"], r["kn"], r["vn"]
        ctx, lse, segc = r["ctx"], r["lse"], r["segc"]
        gp, hid, gmt, gat = r["gp"], r["hid"], r["gmt"], r["gat"]
        dot_, dqkv, dk, dv = r["dot"], r["dqkv"], r["dk"], r["dv"]
        ex, xrec, cin, fin = r["ex"], r["xrec"], r["cin"], r["fin"]
        sown, soth, srec, scin, sfin = r["sown"], r["soth"], r["srec"], r["scin"], r["sfin"]
        sl, sg, sw, se, sh, so, sr, sc, ss = (
            r[name] for name in ("sl", "sg", "sw", "se", "sh", "so", "sr", "sc", "ss"))
        blocks, rows, width = xbuf.shape
        length = blocks * rows
        slots, hs = wq.shape[0], wo.shape[1] // HD
        heads = slots * hs
        part = wo.shape[1]
        units = wu.shape[2]
        chunks = xrec.shape[0]

        s = lax.axis_index("section")
        t = lax.axis_index("tensor")
        d = lax.axis_index("dp")
        core, xh = lax.rem(t, 2), lax.div(t, 2)
        t_core = 2 * xh + 1 - core
        t_x = 2 * (1 - xh) + core
        to_core = (s, t_core, d)
        to_x = (s, t_x, d)
        to_y = (1 - s, t, d)
        to_xy = (1 - s, t_x, d)
        parity = lax.rem(d, 2)
        to_pair = (s, t, d + 1 - 2 * parity)
        left, right = (s, t, d - 1), (s, t, d + 1)
        first_section, last_section = s == 0, s == 1

        def send(src, dst, sems, at, device):
            return pltpu.make_async_remote_copy(
                src_ref=src, dst_ref=dst, send_sem=sems.at[(0, *at)], recv_sem=sems.at[(1, *at)],
                device_id=device, device_id_type=MESH)

        def loop(stop, body):
            def step(i, carry):
                body(i)
                return carry

            lax.fori_loop(0, stop, step, 0)

        barrier = pltpu.get_barrier_semaphore()
        for device in (to_core, to_x, to_y, to_xy):
            pl.semaphore_signal(barrier, inc=1, device_id=device, device_id_type=MESH)

        @pl.when(d > 0)
        def _():
            pl.semaphore_signal(barrier, inc=1, device_id=left, device_id_type=MESH)

        @pl.when(d < count - 1)
        def _():
            pl.semaphore_signal(barrier, inc=1, device_id=right, device_id_type=MESH)

        ends = jnp.where(d > 0, 1, 0) + jnp.where(d < count - 1, 1, 0)
        pl.semaphore_wait(barrier, 4 + ends)

        def at_row(i):
            return pl.ds(pl.multiple_of(i * rows, rows), rows)

        mid_at = at_row

        def grad_at(i):
            return pl.ds(pl.multiple_of(length + i * rows, rows), rows)

        def rows_in(source, device):
            mine, other = gmt.at[:, at_row(t)], gmt.at[:, at_row(t_x)]
            return (
                pltpu.make_async_copy(source.at[xh], mine, sl.at[0]),
                send(source.at[xh], mine, sg, (1,), to_core),
                send(source.at[1 - xh], mine, sg, (0,), device),
                send(other, other, sg, (2,), to_core),
            )

        def rows_wait(copies, target):
            local, core_own, across, core_other = copies
            across.wait_recv()
            core_other.start()
            local.wait()
            core_own.wait()
            core_other.wait()

            def turn(i):
                target[i] = gmt[:, at_row(i)].astype(F32).T.astype(BF16)

            loop(blocks, turn)

        @pl.when(first_section)
        def _():
            for copy in rows_in(xin, to_xy)[:2]:
                copy.start()

        @pl.when(last_section)
        def _():
            rows_in(xin, to_xy)[2].start()

        misc_local = pltpu.make_async_copy(misc, mc.at[0], sl.at[1])
        misc_x = send(misc, mc.at[1], sg, (3,), to_x)
        misc_local.start()
        misc_x.start()
        locals_, pieces = [], []
        for which, (name, target, cuts) in enumerate((("wqh", wq, 2), ("woh", wo, 1), ("wuh", wu, 2), ("wdh", wd, 3))):
            source = r[name]
            locals_.append(pltpu.make_async_copy(source, target.at[0], sl.at[4 + which]))
            half = source.shape[0] // 2
            step = half // cuts
            group = []
            for cut in range(cuts):
                at = pl.ds(pl.multiple_of(parity * half + cut * step, 16), step)
                place = 3 * which + cut
                group.append((
                    send(source.at[at], target.at[1, at], sw, (0, place), to_x),
                    send(target.at[1, at], target.at[1, at], sw, (1, place), to_pair),
                ))
            pieces.append(group)
        for local, group in zip(locals_, pieces, strict=True):
            local.start()
            for across, _ in group:
                across.start()

        @pl.when(last_section)
        def _():
            for copy in rows_in(cot, to_x)[:3]:
                copy.start()

        def pass_on(which, *cuts):
            for cut in cuts:
                across, pair = pieces[which][cut]
                across.wait_recv()
                pair.start()

        def have(which):
            locals_[which].wait()
            for across, pair in pieces[which]:
                across.wait_send()
                pair.wait()

        sown[...] = jnp.zeros_like(sown)
        soth[...] = jnp.zeros_like(soth)
        segment = seg[pl.ds(xh, 1), :]
        segc[...] = jnp.broadcast_to(segment.astype(F32), (128, length)).T

        def ex_at(kind, i):
            return pl.ds(pl.multiple_of(kind * length + i * rows, rows), rows)

        def pair_copy(kind, i):
            return send(ex.at[ex_at(2 * kind, i)], ex.at[ex_at(2 * kind + 1, i)], se, (kind, i), to_core)

        def pair_send(kind, i, value):
            ex[ex_at(2 * kind, i), :] = value.astype(BF16)
            pair_copy(kind, i).start()

        def pair_sum(kind, i):
            pair_copy(kind, i).wait()
            return ex[ex_at(2 * kind, i), :].astype(F32) + ex[ex_at(2 * kind + 1, i), :].astype(F32)

        half_rows = rows // 2
        own_half = pl.ds(pl.multiple_of(core * half_rows, half_rows), half_rows)

        def hop_copy(i, target):
            return send(resb.at[lax.rem(i, 2), own_half], target.at[i, own_half], sh, (0, i), to_y)

        def hop_core(i, target):
            return send(target.at[i, own_half], target.at[i, own_half], sh, (1, i), to_core)

        pass_on(0, 0, 1)

        @pl.when(first_section)
        def _():
            rows_wait(rows_in(xin, to_xy), xbuf)
            pass_on(1, 0)

        @pl.when(last_section)
        def _():
            pass_on(1, 0)
            pass_on(2, 0, 1)
            pass_on(3, 0, 1, 2)
            copies = rows_in(cot, to_x)
            rows_wait(copies, cotb)
            copies[2].wait_send()
            rows_in(xin, to_xy)[2].wait_send()

        misc_local.wait()
        misc_x.wait()
        attn_gain, mlp_gain, out_bias, down_bias = (mc[0, i : i + 1, :] for i in range(4))
        have(0)

        def masked(scores, i, j0, j1, diagonal):
            same = segc[j0:j1, :]
            same = jnp.concatenate([same] * (rows // same.shape[1]), axis=1)
            cols = slice(i * rows, (i + 1) * rows)
            allowed = same == seg[pl.ds(xh, 1), cols].astype(F32)
            if diagonal:
                key = lax.broadcasted_iota(jnp.int32, scores.shape, 0)
                query = lax.broadcasted_iota(jnp.int32, scores.shape, 1)
                allowed = allowed & (key <= query)
            return jnp.where(allowed, scores, NEGATIVE)

        def key_parts(i):
            parts = [(i * rows, (i + 1) * rows, True)]
            if i > 0:
                parts.append((0, i * rows, False))
            return parts

        def project(i):
            full = expanded(xbuf[i])
            normed = (full * norm_factor(full) * attn_gain).astype(BF16)
            nrm[i] = normed
            cols = at_row(i)
            for slot in range(slots):
                three = dot(wq[slot], normed, NT)
                bias = jnp.broadcast_to(mc[slot, 5:6, : 2 * part], (8, 2 * part)).T[:, 0:1]
                query = (three[:part] + bias[:part]).astype(BF16) * SCALE
                key = three[part : 2 * part]
                value = (three[2 * part :] + bias[part:]).astype(BF16).astype(F32)
                for h in range(hs):
                    at = slice(h * HD, (h + 1) * HD)
                    head = slot * hs + h
                    qt[i, head] = query[at].astype(BF16)
                    kt[head, :, cols] = key[at].astype(BF16)
                    vt[head, :, cols] = value[at].astype(BF16)
                    kn[head, cols, :] = key[at].T.astype(BF16)
                    vn[head, cols, :] = value[at].T.astype(BF16)

        def attend(i, h):
            cols = slice(i * rows, (i + 1) * rows)
            parts = key_parts(i)
            query = qt[i, h]
            scores = [masked(dot(kn[h, a:b], query), i, a, b, g) for a, b, g in parts]
            highest = scores[0].max(axis=0, keepdims=True)
            for score in scores[1:]:
                highest = jnp.maximum(highest, score.max(axis=0, keepdims=True))
            total, context = 0.0, 0.0
            for score, (a, b, _) in zip(scores, parts, strict=True):
                power = jnp.exp(score - highest)
                total = total + row_sum(power)
                context = context + dot(vt[h, :, a:b], power.astype(BF16))
            ctx[h, :, cols] = (context / total).astype(BF16)
            lse[i, h] = highest + jnp.log(total)

        def each_block(i, body):
            for block in range(blocks):

                @pl.when(i == block)
                def _():
                    loop(heads, lambda h: body(block, h))

        def attention_rows(i):
            @pl.when(last_section & (i == 0))
            def _():
                hop_copy(0, xbuf).wait_recv()
                hop_core(0, xbuf).start()

            @pl.when(last_section)
            def _():
                hop_core(i, xbuf).wait()

            project(i)
            each_block(i, attend)

            @pl.when(i == 0)
            def _():
                have(1)

            context = ctx[:, :, at_row(i)].reshape(heads * HD, rows)
            pair_send(0, i, dot(context, wo[...].reshape(heads * HD, width), TN))

            for step, (which, cut) in enumerate(((2, 0), (2, 1), (3, 0), (3, 1))):

                @pl.when((i == step) & first_section)
                def _():
                    pass_on(which, cut)

            @pl.when(last_section & (i < blocks - 1))
            def _():
                hop_copy(i + 1, xbuf).wait_recv()
                hop_core(i + 1, xbuf).start()

        def mlp_rows(i):
            @pl.when(i == 0)
            def _():
                have(2)

            branch = pair_sum(0, i) + out_bias
            middle = expanded(xbuf[i]) + centred(branch)
            pool[mid_at(i), :] = middle
            normed = middle * norm_factor(middle) * mlp_gain
            n2t[:, at_row(i)] = normed.T.astype(BF16)
            normed = normed.astype(BF16)
            for slot in range(slots):
                pre = dot(normed, wu[slot]) + mc[slot, 4:5, :]
                square = pre * pre
                bend = jnp.tanh(GELU_C * pre * (1.0 + GELU_A * square))
                grow = 0.5 * (1.0 + bend)
                hid[slot, i] = (pre * grow).astype(BF16)
                slope = GELU_C * (1.0 + 3.0 * GELU_A * square)
                gp[slot, i] = (grow + 0.5 * pre * (1.0 - bend * bend) * slope).astype(BF16)

            @pl.when(i == 0)
            def _():
                @pl.when(first_section)
                def _():
                    pass_on(3, 2)

                have(3)

            branch = dot(hid[0, i], wd[0], NT)
            for slot in range(1, slots):
                branch = branch + dot(hid[slot, i], wd[slot], NT)
            pair_send(1, i, branch)

        def keep_out(i, value):
            @pl.when((i == t) | (i == t_x))
            def _():
                outt[jnp.where(i == t, 0, 1)] = value.T.astype(BF16)

        def result_rows(i):
            result = pool[mid_at(i), :] + centred(pair_sum(1, i) + down_bias)
            keep_out(i, result)

            @pl.when(first_section)
            def _():
                @pl.when(i >= 2)
                def _():
                    hop_copy(i - 2, xbuf).wait_send()

                lane = lax.broadcasted_iota(jnp.int32, result.shape, 1)
                resb[lax.rem(i, 2)] = jnp.where(lane == width - 1, 0.0, result).astype(BF16)
                hop_copy(i, xbuf).start()

        def forward(step):
            i_mlp = jnp.where(first_section, step - blocks, step - 1)
            i_res = i_mlp - 1
            some_res = (i_res >= 0) & (i_res < blocks)

            @pl.when(step < blocks)
            def _():
                attention_rows(step)

            @pl.when(last_section & some_res)
            def _():
                result_rows(i_res)

            @pl.when((i_mlp >= 0) & (i_mlp < blocks))
            def _():
                mlp_rows(i_mlp)

            @pl.when(first_section & some_res)
            def _():
                result_rows(i_res)

        loop(2 * blocks + 1, forward)

        def rows_out(target, which):
            return (
                pltpu.make_async_copy(outt.at[0], target.at[xh], sl.at[2]),
                send(outt.at[1], target.at[xh], so, (which,), to_x),
            )

        act_copies = rows_out(act, 0)
        for copy in act_copies:
            copy.start()

        @pl.when(first_section)
        def _():
            loop(2, lambda i: hop_copy(blocks - 2 + i, xbuf).wait_send())

        def other_at(k):
            row = k * CHUNK
            early = lax.div(row, 2 * rows) * length + 2 * rows + lax.rem(row, 2 * rows)
            return pl.ds(pl.multiple_of(jnp.where(row < 8 * rows, early, row - 8 * rows), CHUNK), CHUNK)

        def own_at(k):
            row = k * CHUNK
            late = jnp.where(row < 7 * rows, row - 6 * rows, row - 3 * rows)
            late = jnp.where(row < 6 * rows, row + 3 * rows, late)
            return pl.ds(pl.multiple_of(jnp.where(row < 3 * rows, row + rows, late), CHUNK), CHUNK)

        def x_copy(k):
            return send(ex.at[other_at(k)], xrec.at[k], sr, (k,), to_x)

        def put(turn, first, value):
            @pl.when(turn == 0)
            def _():
                for k in range(value.shape[0] // CHUNK):
                    ex[other_at(first + k), :] = value[k * CHUNK : (k + 1) * CHUNK].astype(BF16)

            @pl.when(turn == 1)
            def _():
                for k in range(value.shape[0] // CHUNK):
                    pool[own_at(first + k), :] = value[k * CHUNK : (k + 1) * CHUNK]

        def start(turn, first, number):
            @pl.when(turn == 0)
            def _():
                loop(number, lambda k: x_copy(first + k).start())

        def mlp_grads(turn):
            slot = 1 - turn
            tile = 256
            tiles = width // tile

            def down_part(k):
                at = pl.ds(pl.multiple_of(k * tile, tile), tile)
                put(turn, k * (tile // CHUNK), dot(gmt[at, :], hid[slot].reshape(length, units)))

            loop(tiles, down_part)
            start(turn, 0, width // CHUNK)

            def up_part(k):
                at = pl.ds(pl.multiple_of(k * tile, tile), tile)
                first = width // CHUNK + k * (tile // CHUNK)
                put(turn, first, dot(n2t[at, :], gp[slot].reshape(length, units)))

            loop(tiles, up_part)
            start(turn, width // CHUNK, width // CHUNK)

        def down_back(i):
            @pl.when(first_section)
            def _():
                hop_copy(i, cotb).wait_recv()
                hop_core(i, cotb).start()
                hop_core(i, cotb).wait()

            grad = centred(cotb[i].astype(F32))
            pool[grad_at(i), :] = grad
            gmt[:, at_row(i)] = grad.T.astype(BF16)
            grad = grad.astype(BF16)
            sown[3:4, :] += row_sum(grad.astype(F32))
            branch = 0.0
            for slot, sums in ((0, sown), (1, soth)):
                before = (dot(grad, wd[slot]) * gp[slot, i].astype(F32)).astype(BF16)
                gp[slot, i] = before
                sums[4:5, :] += row_sum(before.astype(F32))
                branch = branch + dot(before, wu[slot], NT)
            pair_send(0, i, branch)

        def out_back(i):
            grad, gain_grad = norm_back(pair_sum(0, i), pool[mid_at(i), :], mlp_gain)
            sown[2:3, :] += gain_grad
            grad = grad + pool[grad_at(i), :]
            pool[grad_at(i), :] = grad
            grad = grad.astype(BF16)
            gat[i] = grad
            sown[1:2, :] += row_sum(grad.astype(F32))
            back = dot(wo[...].reshape(heads * HD, width), grad, NT).astype(BF16)
            for h in range(heads):
                dot_[i, h] = back[h * HD : (h + 1) * HD]

        def attend_back(i, h):
            slot, place = lax.div(h, hs), lax.rem(h, hs)
            query, back = qt[i, h], dot_[i, h]
            parts = key_parts(i)
            cols = slice(i * rows, (i + 1) * rows)
            probs, g_probs = [], []
            centre = 0.0
            for a, b, g in parts:
                prob = jnp.exp(masked(dot(kn[h, a:b], query), i, a, b, g) - lse[i, h])
                g_prob = dot(vn[h, a:b], back)
                centre = centre + row_sum(prob * g_prob)
                probs.append(prob)
                g_probs.append(g_prob)
            g_query = 0.0
            for prob, g_prob, (a, b, _) in zip(probs, g_probs, parts, strict=True):
                g_score = (prob * (g_prob - centre)).astype(BF16)
                g_value = dot(back, prob.astype(BF16), NT)
                g_key = dot(query, g_score, NT)
                g_query = g_query + dot(kt[h, :, a:b], g_score)
                if i == blocks - 1:
                    dv[h, :, a:b] = g_value
                    dk[h, :, a:b] = g_key
                else:
                    dv[h, :, a:b] += g_value
                    dk[h, :, a:b] += g_key
            dqkv[slot, 0, place, :, cols] = (g_query * SCALE).astype(BF16)
            dqkv[slot, 1, place, :, cols] = dk[h, :, cols].astype(BF16)
            dqkv[slot, 2, place, :, cols] = dv[h, :, cols].astype(BF16)

        def qkv_back(i):
            branch = 0.0
            for slot in range(slots):
                three = dqkv[slot, :, :, :, at_row(i)].reshape(3 * part, rows)
                branch = branch + dot(three, wq[slot], TN)
            pair_send(1, i, branch)

        def in_back(i):
            grad, gain_grad = norm_back(pair_sum(1, i), expanded(xbuf[i]), attn_gain)
            sown[0:1, :] += gain_grad
            grad = grad + pool[grad_at(i), :]
            grad = grad - grad[:, width - 1 :]
            keep_out(i, grad)

            @pl.when(last_section)
            def _():
                @pl.when(i < blocks - 2)
                def _():
                    hop_copy(i + 2, cotb).wait_send()

                resb[lax.rem(i, 2)] = grad.astype(BF16)
                hop_copy(i, cotb).start()

        def backward(step):
            behind = jnp.where(first_section, 0, 1)
            n_rest = step - behind
            n_in = n_rest - 1
            last = blocks - 1

            @pl.when(step < blocks)
            def _():
                down_back(last - step)

            @pl.when(step == jnp.where(first_section, blocks - 1, blocks + 2))
            def _():
                loop(2, mlp_grads)

            @pl.when(n_in == 0)
            def _():
                for copy in act_copies:
                    copy.wait()

            @pl.when((n_in >= 0) & (n_in < blocks))
            def _():
                in_back(last - n_in)

            @pl.when((n_rest >= 0) & (n_rest < blocks))
            def _():
                i = last - n_rest
                out_back(i)
                each_block(i, attend_back)
                qkv_back(i)

        loop(blocks + 3, backward)

        ones = jnp.ones((8, length), BF16)
        sown[5:6, : 3 * part] = dot(ones, dqkv[0].reshape(3 * part, length), NT)[0:1]
        soth[5:6, : 3 * part] = dot(ones, dqkv[1].reshape(3 * part, length), NT)[0:1]
        soth[0:4, :] = sown[0:4, :]
        small_x = send(soth, srec, ss, (0,), to_x)
        small_x.start()

        def attention_grads(turn):
            slot = 1 - turn

            def qkv_part(k):
                first = (2 * width) // CHUNK + k * (part // CHUNK)
                put(turn, first, dot(dqkv[slot, k].reshape(part, length), nrm[...].reshape(length, width)))

            loop(3, qkv_part)
            first = (2 * width + 3 * part) // CHUNK
            context = ctx[pl.ds(slot * hs, hs)].reshape(part, length)
            put(turn, first, dot(context, gat[...].reshape(length, width)))
            start(turn, 2 * (width // CHUNK), chunks - 2 * (width // CHUNK))

        loop(2, attention_grads)
        eg_copies = rows_out(eg, 1)
        for copy in eg_copies:
            copy.start()

        middle = count // 2
        on_left = d < middle
        depth = jnp.where(on_left, d, count - 1 - d)
        has_outer = depth > 0
        is_mid = depth == middle - 1
        side = jnp.where(on_left, 0, 1)
        inner = (s, t, jnp.where(on_left, d + 1, d - 1))
        outer = (s, t, jnp.where(on_left, d - 1, d + 1))
        lag = 3
        lag_in = lag * depth
        lag_mid = lag * middle
        lag_out = lag_mid + lag * (middle - depth)
        lag_all = lag_mid + lag * middle

        def in_copy(k):
            return send(xrec.at[k], cin.at[k], sc, (0, k), inner)

        def cross_copy(k):
            return send(xrec.at[k], fin.at[k], sc, (1, k), inner)

        def back_copy(k):
            return send(fin.at[k], fin.at[k], sc, (2, k), inner)

        def out_copy(k):
            return send(fin.at[k], fin.at[k], sc, (3, k), outer)

        def chunk_out(k):
            place = 0
            for name in ("down", "up", "qkv", "out"):
                number = r[name].shape[0] // CHUNK

                @pl.when((k >= place) & (k < place + number))
                def _():
                    at = pl.ds(pl.multiple_of((k - place) * CHUNK, CHUNK), CHUNK)
                    pltpu.make_async_copy(fin.at[k], r[name].at[at], so.at[0, 2 + k]).start()

                place += number

        s_in = send(sown, scin, ss, (1,), inner)
        s_cross = send(sown, sfin, ss, (2,), inner)
        s_back = send(sfin, sfin, ss, (3,), inner)
        s_out = send(sfin, sfin, ss, (4,), outer)

        def reduce_small(it):
            small_owner = side == 0
            begin = chunks - 4

            @pl.when(it == begin)
            def _():
                small_x.wait()
                sown[...] = sown[...] + srec[...]

            @pl.when(it == begin + lag_in)
            def _():
                @pl.when(has_outer)
                def _():
                    s_in.wait_recv()
                    sown[...] = sown[...] + scin[...]

                @pl.when(jnp.logical_not(is_mid))
                def _():
                    s_in.start()

                @pl.when(is_mid & jnp.logical_not(small_owner))
                def _():
                    s_cross.start()

            @pl.when((it == begin + lag_mid) & is_mid & small_owner)
            def _():
                s_cross.wait_recv()
                sfin[...] = sfin[...] + sown[...]
                s_back.start()

            @pl.when(it == begin + lag_out)
            def _():
                @pl.when(is_mid & jnp.logical_not(small_owner))
                def _():
                    s_back.wait_recv()

                @pl.when(jnp.logical_not(is_mid))
                def _():
                    s_out.wait_recv()

                @pl.when(has_outer)
                def _():
                    s_out.start()

        def reduce(it):
            @pl.when(it < chunks)
            def _():
                k = it
                x_copy(k).wait()
                xrec[k] = (pool[own_at(k), :] + xrec[k].astype(F32)).astype(BF16)

            k_in = it - lag_in

            @pl.when((k_in >= 0) & (k_in < chunks))
            def _():
                k = k_in
                owner = lax.rem(k, 2) == side

                @pl.when(has_outer)
                def _():
                    in_copy(k).wait_recv()
                    xrec[k] = (xrec[k].astype(F32) + cin[k].astype(F32)).astype(BF16)

                @pl.when(jnp.logical_not(is_mid))
                def _():
                    in_copy(k).start()

                @pl.when(is_mid & jnp.logical_not(owner))
                def _():
                    cross_copy(k).start()

            k_mid = it - lag_mid

            @pl.when((k_mid >= 0) & (k_mid < chunks) & is_mid)
            def _():
                k = k_mid

                @pl.when(lax.rem(k, 2) == side)
                def _():
                    cross_copy(k).wait_recv()
                    fin[k] = (xrec[k].astype(F32) + fin[k].astype(F32)).astype(BF16)
                    back_copy(k).start()

                    @pl.when(has_outer)
                    def _():
                        out_copy(k).start()

                    chunk_out(k)

            k_out = it - lag_out

            @pl.when((k_out >= 0) & (k_out < chunks))
            def _():
                k = k_out
                owner = lax.rem(k, 2) == side

                @pl.when(is_mid & jnp.logical_not(owner))
                def _():
                    back_copy(k).wait_recv()

                @pl.when(jnp.logical_not(is_mid))
                def _():
                    out_copy(k).wait_recv()

                @pl.when(jnp.logical_not(is_mid & owner))
                def _():
                    @pl.when(has_outer)
                    def _():
                        out_copy(k).start()

                    chunk_out(k)

            reduce_small(it)

        loop(chunks + lag_all, reduce)
        small[...] = sfin[...]

        @pl.when(jnp.logical_not(is_mid))
        def _():
            s_in.wait_send()

        @pl.when(is_mid & (side == 1))
        def _():
            s_cross.wait_send()

        @pl.when(is_mid & (side == 0))
        def _():
            s_back.wait_send()

        @pl.when(has_outer)
        def _():
            s_out.wait_send()

        def drain(k):
            owner = lax.rem(k, 2) == side

            @pl.when(jnp.logical_not(is_mid))
            def _():
                in_copy(k).wait_send()

            @pl.when(is_mid & jnp.logical_not(owner))
            def _():
                cross_copy(k).wait_send()

            @pl.when(is_mid & owner)
            def _():
                back_copy(k).wait_send()

            @pl.when(has_outer)
            def _():
                out_copy(k).wait_send()

            pltpu.make_async_copy(fin.at[k], r["down"].at[pl.ds(0, CHUNK)], so.at[0, 2 + k]).wait()

        loop(chunks, drain)

        @pl.when(last_section)
        def _():
            loop(2, lambda i: hop_copy(i, cotb).wait_send())

        for copy in eg_copies:
            copy.wait()

    return kernel


def per_device(
    block_input,
    segments,
    cotangent,
    attn_gain,
    qkv_weight,
    qv_bias,
    out_weight,
    out_bias,
    mlp_gain,
    up_projection_weight,
    up_bias,
    down_projection_weight,
    down_bias,
):
    micros, rows, _, kept = block_input.shape
    width = qkv_weight.shape[1]
    part = qkv_weight.shape[3]
    units = up_projection_weight.shape[2]
    blocks = lax.axis_size("tensor")
    count = lax.axis_size("dp")
    length = blocks * rows
    slots = 2
    hs = part // HD
    heads = slots * hs
    chunks = (2 * width + 4 * part) // CHUNK

    def features_first(array):
        return jnp.pad(array[:, :, 0, :].transpose(0, 2, 1), ((0, 0), (0, width - kept), (0, 0)))

    qv_row = jnp.pad(qv_bias.reshape(1, 2 * part), ((0, 0), (0, width - 2 * part)))
    rows_of = [attn_gain, mlp_gain, out_bias, down_bias, up_bias, qv_row, up_bias, qv_row]
    inputs = {
        "xin": features_first(block_input),
        "cot": features_first(cotangent),
        "wqh": qkv_weight[0].transpose(1, 2, 0).reshape(3 * part, width),
        "woh": out_weight[0],
        "wuh": up_projection_weight[0],
        "wdh": down_projection_weight[0],
        "misc": jnp.concatenate(rows_of).astype(F32),
        "seg": segments[:, 0, :],
    }
    outputs = {
        "act": ((micros, width, rows), BF16),
        "eg": ((micros, width, rows), BF16),
        "down": ((width, units), BF16),
        "up": ((width, units), BF16),
        "qkv": ((3 * part, width), BF16),
        "out": ((part, width), BF16),
        "small": ((8, width), F32),
    }
    scratch = {
        "wq": ((slots, 3 * part, width), BF16),
        "wo": ((slots, part, width), BF16),
        "wu": ((slots, width, units), BF16),
        "wd": ((slots, width, units), BF16),
        "mc": ((slots, 8, width), F32),
        "xbuf": ((blocks, rows, width), BF16),
        "cotb": ((blocks, rows, width), BF16),
        "resb": ((2, rows, width), BF16),
        "outt": ((2, width, rows), BF16),
        "pool": ((max(2 * length, chunks * CHUNK), width), F32),
        "nrm": ((blocks, rows, width), BF16),
        "n2t": ((width, length), BF16),
        "qt": ((blocks, heads, HD, rows), BF16),
        "kt": ((heads, HD, length), BF16),
        "vt": ((heads, HD, length), BF16),
        "kn": ((heads, length, HD), BF16),
        "vn": ((heads, length, HD), BF16),
        "ctx": ((heads, HD, length), BF16),
        "lse": ((blocks, heads, 1, rows), F32),
        "segc": ((length, 128), F32),
        "gp": ((slots, blocks, rows, units), BF16),
        "hid": ((slots, blocks, rows, units), BF16),
        "gmt": ((width, length), BF16),
        "gat": ((blocks, rows, width), BF16),
        "dot": ((blocks, heads, HD, rows), BF16),
        "dqkv": ((slots, 3, hs, HD, length), BF16),
        "dk": ((heads, HD, length), F32),
        "dv": ((heads, HD, length), F32),
        "ex": ((4 * length, width), BF16),
        "xrec": ((chunks, CHUNK, width), BF16),
        "cin": ((chunks, CHUNK, width), BF16),
        "fin": ((chunks, CHUNK, width), BF16),
        "sown": ((8, width), F32),
        "soth": ((8, width), F32),
        "srec": ((8, width), F32),
        "scin": ((8, width), F32),
        "sfin": ((8, width), F32),
    }
    dma = pltpu.SemaphoreType.DMA
    semaphores = {
        "sl": dma((8,)),
        "sg": dma((2, 4)),
        "sw": dma((2, 2, 12)),
        "se": dma((2, 2, blocks)),
        "sh": dma((2, 2, blocks)),
        "so": dma((2, 2 + chunks)),
        "sr": dma((2, chunks)),
        "sc": dma((2, 4, chunks)),
        "ss": dma((2, 5)),
    }
    in_vmem = {"seg", "small"}

    def spec(name):
        return pl.BlockSpec(memory_space=pltpu.VMEM if name in in_vmem else pl.ANY)

    names = [*inputs, *outputs, *scratch, *semaphores]
    act, eg, down, up, qkv, out, small = pl.pallas_call(
        make_kernel(names, count),
        out_shape=[jax.ShapeDtypeStruct(*item) for item in outputs.values()],
        in_specs=[spec(name) for name in inputs],
        out_specs=[spec(name) for name in outputs],
        scratch_shapes=[pltpu.VMEM(*item) for item in scratch.values()] + list(semaphores.values()),
        compiler_params=pltpu.CompilerParams(
            collective_id=0, has_side_effects=True, vmem_limit_bytes=63 * 1024 * 1024
        ),
        name="layers",
    )(*inputs.values())

    def positions_first(array):
        return array[:, :kept, :].transpose(0, 2, 1)[None, :, :, None, :]

    qv = small[5, : 3 * part].reshape(3, part)
    return (
        positions_first(act),
        positions_first(eg).astype(F32),
        small[0:1],
        qkv.reshape(3, part, width).transpose(2, 0, 1).astype(F32)[None],
        qv[0::2][None],
        out.astype(F32)[None],
        small[1:2],
        small[2:3],
        up.astype(F32)[None],
        small[4:5, :units],
        down.astype(F32)[None],
        small[3:4],
    )


def solution(mesh):
    in_specs = (
        P(None, "tensor", "dp", None),
        P(None, "dp", None),
        P(None, "tensor", "dp", None),
        P("section", None),
        P("section", None, None, "tensor"),
        P("section", None, "tensor"),
        P("section", "tensor", None),
        P("section", None),
        P("section", None),
        P("section", None, "tensor"),
        P("section", "tensor"),
        P("section", None, "tensor"),
        P("section", None),
    )
    out_specs = (
        P("section", None, "tensor", "dp", None),
        P("section", None, "tensor", "dp", None),
        P("section", None),
        P("section", None, None, "tensor"),
        P("section", None, "tensor"),
        P("section", "tensor", None),
        P("section", None),
        P("section", None),
        P("section", None, "tensor"),
        P("section", "tensor"),
        P("section", None, "tensor"),
        P("section", None),
    )
    return jax.shard_map(
        per_device, mesh=mesh, in_specs=in_specs, out_specs=out_specs, check_vma=False
    )
```

```python
import jax
import jax.numpy as jnp
from jax import lax
from jax.experimental import pallas as pl
from jax.experimental.pallas import tpu as pltpu
from jax.sharding import PartitionSpec as P

HD = 64
EPS = 1e-05
SCALE = 0.125
NEGATIVE = -1e30
CHUNK = 64
EARLY = ({3: (0, 1), 4: (5, 6)}, {3: (1, 4), 4: (6, 7)}, {3: (4, 5), 4: (7, 8)})
MESH = pl.DeviceIdType.MESH
F32 = jnp.float32
BF16 = jnp.bfloat16
NN = (((1,), (0,)), ((), ()))
NT = (((1,), (1,)), ((), ()))
TN = (((0,), (0,)), ((), ()))
GELU_C = 0.7978845608028654
GELU_A = 0.044715


def dot(left, right, dims=NN):
    return lax.dot_general(left, right, dims, preferred_element_type=F32)


def lane_sum(value):
    return jnp.sum(value, axis=-1, keepdims=True)


def row_sum(value):
    return jnp.sum(value, axis=0, keepdims=True)


def expanded(block):
    value = block.astype(F32)
    lane = lax.broadcasted_iota(jnp.int32, value.shape, 1)
    return jnp.where(lane == value.shape[1] - 1, -lane_sum(value), value)


def norm_factor(full):
    return lax.rsqrt(lane_sum(full * full) * (1.0 / full.shape[1]) + EPS)


def centred(value):
    return value - lane_sum(value) * (1.0 / value.shape[1])


def norm_back(grad, full, gain):
    factor = norm_factor(full)
    weighted = grad * gain
    inner = lane_sum(weighted * full) * (1.0 / full.shape[1])
    gain_grad = row_sum(grad * full * factor)
    return centred(factor * weighted - full * (factor * factor * factor * inner)), gain_grad


def make_kernel(names, count):
    def kernel(*refs):
        r = dict(zip(names, refs, strict=True))
        xin, cot, misc, seg = r["xin"], r["cot"], r["misc"], r["seg"]
        act, eg, small = r["act"], r["eg"], r["small"]
        wq, wo, wu, wd, mc = r["wq"], r["wo"], r["wu"], r["wd"], r["mc"]
        xbuf, cotb, resb, outt = r["xbuf"], r["cotb"], r["resb"], r["outt"]
        pool, nrm, n2t = r["pool"], r["nrm"], r["n2t"]
        qt, kt, vt, kn, vn = r["qt"], r["kt"], r["vt"], r["kn"], r["vn"]
        ctx, lse, segc = r["ctx"], r["lse"], r["segc"]
        gp, hid, gmt, gat = r["gp"], r["hid"], r["gmt"], r["gat"]
        dot_, dqkv, dk, dv = r["dot"], r["dqkv"], r["dk"], r["dv"]
        ex, xrec, cin, fin = r["ex"], r["xrec"], r["cin"], r["fin"]
        sown, soth, srec, scin, sfin = r["sown"], r["soth"], r["srec"], r["scin"], r["sfin"]
        sl, sg, sw, se, sh, so, sr, sc, ss = (
            r[name] for name in ("sl", "sg", "sw", "se", "sh", "so", "sr", "sc", "ss"))
        blocks, rows, width = xbuf.shape
        length = blocks * rows
        slots, hs = wq.shape[0], wo.shape[1] // HD
        heads = slots * hs
        part = wo.shape[1]
        units = wu.shape[2]
        chunks = xrec.shape[0]

        s = lax.axis_index("section")
        t = lax.axis_index("tensor")
        d = lax.axis_index("dp")
        core, xh = lax.rem(t, 2), lax.div(t, 2)
        t_core = 2 * xh + 1 - core
        t_x = 2 * (1 - xh) + core
        to_core = (s, t_core, d)
        to_x = (s, t_x, d)
        to_y = (1 - s, t, d)
        to_xy = (1 - s, t_x, d)
        parity = lax.rem(d, 2)
        to_pair = (s, t, d + 1 - 2 * parity)
        left, right = (s, t, d - 1), (s, t, d + 1)
        first_section, last_section = s == 0, s == 1

        def send(src, dst, sems, at, device):
            return pltpu.make_async_remote_copy(
                src_ref=src, dst_ref=dst, send_sem=sems.at[(0, *at)], recv_sem=sems.at[(1, *at)],
                device_id=device, device_id_type=MESH)

        def loop(stop, body):
            def step(i, carry):
                body(i)
                return carry

            lax.fori_loop(0, stop, step, 0)

        barrier = pltpu.get_barrier_semaphore()
        for device in (to_core, to_x, to_y, to_xy):
            pl.semaphore_signal(barrier, inc=1, device_id=device, device_id_type=MESH)

        @pl.when(d > 0)
        def _():
            pl.semaphore_signal(barrier, inc=1, device_id=left, device_id_type=MESH)

        @pl.when(d < count - 1)
        def _():
            pl.semaphore_signal(barrier, inc=1, device_id=right, device_id_type=MESH)

        ends = jnp.where(d > 0, 1, 0) + jnp.where(d < count - 1, 1, 0)
        pl.semaphore_wait(barrier, 4 + ends)

        def at_row(i):
            return pl.ds(pl.multiple_of(i * rows, rows), rows)

        mid_at = at_row

        def grad_at(i):
            return pl.ds(pl.multiple_of(length + i * rows, rows), rows)

        def rows_in(source, device):
            mine, other = gmt.at[:, at_row(t)], gmt.at[:, at_row(t_x)]
            return (
                pltpu.make_async_copy(source.at[xh], mine, sl.at[0]),
                send(source.at[xh], mine, sg, (1,), to_core),
                send(source.at[1 - xh], mine, sg, (0,), device),
                send(other, other, sg, (2,), to_core),
            )

        def rows_wait(copies, target):
            local, core_own, across, core_other = copies
            across.wait_recv()
            core_other.start()
            local.wait()
            core_own.wait()
            core_other.wait()

            def turn(i):
                target[i] = gmt[:, at_row(i)].astype(F32).T.astype(BF16)

            loop(blocks, turn)

        @pl.when(first_section)
        def _():
            for copy in rows_in(xin, to_xy)[:2]:
                copy.start()

        @pl.when(last_section)
        def _():
            rows_in(xin, to_xy)[2].start()

        misc_local = pltpu.make_async_copy(misc, mc.at[0], sl.at[1])
        misc_x = send(misc, mc.at[1], sg, (3,), to_x)
        misc_local.start()
        misc_x.start()
        locals_, pieces = [], []
        for which, (name, target, cuts) in enumerate((("wqh", wq, 2), ("woh", wo, 1), ("wuh", wu, 2), ("wdh", wd, 3))):
            source = r[name]
            locals_.append(pltpu.make_async_copy(source, target.at[0], sl.at[4 + which]))
            half = source.shape[0] // 2
            step = half // cuts
            group = []
            for cut in range(cuts):
                at = pl.ds(pl.multiple_of(parity * half + cut * step, 16), step)
                place = 3 * which + cut
                group.append((
                    send(source.at[at], target.at[1, at], sw, (0, place), to_x),
                    send(target.at[1, at], target.at[1, at], sw, (1, place), to_pair),
                ))
            pieces.append(group)
        for local, group in zip(locals_, pieces, strict=True):
            local.start()
            for across, _ in group:
                across.start()

        @pl.when(last_section)
        def _():
            for copy in rows_in(cot, to_x)[:3]:
                copy.start()

        def pass_on(which, *cuts):
            for cut in cuts:
                across, pair = pieces[which][cut]
                across.wait_recv()
                pair.start()

        def have(which):
            locals_[which].wait()
            for across, pair in pieces[which]:
                across.wait_send()
                pair.wait()

        sown[...] = jnp.zeros_like(sown)
        soth[...] = jnp.zeros_like(soth)
        segment = seg[pl.ds(xh, 1), :]
        segc[...] = jnp.broadcast_to(segment.astype(F32), (128, length)).T

        def ex_at(kind, i):
            return pl.ds(pl.multiple_of(kind * length + i * rows, rows), rows)

        def pair_copy(kind, i):
            return send(ex.at[ex_at(2 * kind, i)], ex.at[ex_at(2 * kind + 1, i)], se, (kind, i), to_core)

        def pair_send(kind, i, value):
            ex[ex_at(2 * kind, i), :] = value.astype(BF16)
            pair_copy(kind, i).start()

        def pair_sum(kind, i):
            pair_copy(kind, i).wait()
            return ex[ex_at(2 * kind, i), :].astype(F32) + ex[ex_at(2 * kind + 1, i), :].astype(F32)

        half_rows = rows // 2
        own_half = pl.ds(pl.multiple_of(core * half_rows, half_rows), half_rows)

        def hop_copy(i, target):
            return send(resb.at[lax.rem(i, 2), own_half], target.at[i, own_half], sh, (0, i), to_y)

        def hop_core(i, target):
            return send(target.at[i, own_half], target.at[i, own_half], sh, (1, i), to_core)

        pass_on(0, 0, 1)

        @pl.when(first_section)
        def _():
            rows_wait(rows_in(xin, to_xy), xbuf)
            pass_on(1, 0)

        @pl.when(last_section)
        def _():
            pass_on(1, 0)
            pass_on(2, 0, 1)
            pass_on(3, 0, 1, 2)
            copies = rows_in(cot, to_x)
            rows_wait(copies, cotb)
            copies[2].wait_send()
            rows_in(xin, to_xy)[2].wait_send()

        misc_local.wait()
        misc_x.wait()
        attn_gain, mlp_gain, out_bias, down_bias = (mc[0, i : i + 1, :] for i in range(4))
        have(0)

        def masked(scores, i, j0, j1, diagonal):
            same = segc[j0:j1, :]
            same = jnp.concatenate([same] * (rows // same.shape[1]), axis=1)
            cols = slice(i * rows, (i + 1) * rows)
            allowed = same == seg[pl.ds(xh, 1), cols].astype(F32)
            if diagonal:
                key = lax.broadcasted_iota(jnp.int32, scores.shape, 0)
                query = lax.broadcasted_iota(jnp.int32, scores.shape, 1)
                allowed = allowed & (key <= query)
            return jnp.where(allowed, scores, NEGATIVE)

        def key_parts(i):
            parts = [(i * rows, (i + 1) * rows, True)]
            if i > 0:
                parts.append((0, i * rows, False))
            return parts

        def project(i):
            full = expanded(xbuf[i])
            normed = (full * norm_factor(full) * attn_gain).astype(BF16)
            nrm[i] = normed
            cols = at_row(i)
            for slot in range(slots):
                three = dot(wq[slot], normed, NT)
                bias = jnp.broadcast_to(mc[slot, 5:6, : 2 * part], (8, 2 * part)).T[:, 0:1]
                query = (three[:part] + bias[:part]).astype(BF16) * SCALE
                key = three[part : 2 * part]
                value = (three[2 * part :] + bias[part:]).astype(BF16).astype(F32)
                for h in range(hs):
                    at = slice(h * HD, (h + 1) * HD)
                    head = slot * hs + h
                    qt[i, head] = query[at].astype(BF16)
                    kt[head, :, cols] = key[at].astype(BF16)
                    vt[head, :, cols] = value[at].astype(BF16)
                    kn[head, cols, :] = key[at].T.astype(BF16)
                    vn[head, cols, :] = value[at].T.astype(BF16)

        def attend(i, h):
            cols = slice(i * rows, (i + 1) * rows)
            parts = key_parts(i)
            query = qt[i, h]
            scores = [masked(dot(kn[h, a:b], query), i, a, b, g) for a, b, g in parts]
            highest = scores[0].max(axis=0, keepdims=True)
            for score in scores[1:]:
                highest = jnp.maximum(highest, score.max(axis=0, keepdims=True))
            total, context = 0.0, 0.0
            for score, (a, b, _) in zip(scores, parts, strict=True):
                power = jnp.exp(score - highest)
                total = total + row_sum(power)
                context = context + dot(vt[h, :, a:b], power.astype(BF16))
            ctx[h, :, cols] = (context / total).astype(BF16)
            lse[i, h] = highest + jnp.log(total)

        def each_block(i, body):
            for block in range(blocks):

                @pl.when(i == block)
                def _():
                    loop(heads, lambda h: body(block, h))

        def attention_rows(i):
            @pl.when(last_section & (i == 0))
            def _():
                hop_copy(0, xbuf).wait_recv()
                hop_core(0, xbuf).start()

            @pl.when(last_section)
            def _():
                hop_core(i, xbuf).wait()

            project(i)
            each_block(i, attend)

            @pl.when(i == 0)
            def _():
                have(1)

            context = ctx[:, :, at_row(i)].reshape(heads * HD, rows)
            pair_send(0, i, dot(context, wo[...].reshape(heads * HD, width), TN))

            for step, (which, cut) in enumerate(((2, 0), (2, 1), (3, 0), (3, 1))):

                @pl.when((i == step) & first_section)
                def _():
                    pass_on(which, cut)

            @pl.when(last_section & (i < blocks - 1))
            def _():
                hop_copy(i + 1, xbuf).wait_recv()
                hop_core(i + 1, xbuf).start()

        def mlp_rows(i):
            @pl.when(i == 0)
            def _():
                have(2)

            branch = pair_sum(0, i) + out_bias
            middle = expanded(xbuf[i]) + centred(branch)
            pool[mid_at(i), :] = middle
            normed = middle * norm_factor(middle) * mlp_gain
            n2t[:, at_row(i)] = normed.T.astype(BF16)
            normed = normed.astype(BF16)
            for slot in range(slots):
                pre = dot(normed, wu[slot]) + mc[slot, 4:5, :]
                square = pre * pre
                bend = jnp.tanh(GELU_C * pre * (1.0 + GELU_A * square))
                grow = 0.5 * (1.0 + bend)
                hid[slot, i] = (pre * grow).astype(BF16)
                slope = GELU_C * (1.0 + 3.0 * GELU_A * square)
                gp[slot, i] = (grow + 0.5 * pre * (1.0 - bend * bend) * slope).astype(BF16)

            @pl.when(i == 0)
            def _():
                @pl.when(first_section)
                def _():
                    pass_on(3, 2)

                have(3)

            branch = dot(hid[0, i], wd[0], NT)
            for slot in range(1, slots):
                branch = branch + dot(hid[slot, i], wd[slot], NT)
            pair_send(1, i, branch)

        def keep_out(i, value):
            @pl.when((i == t) | (i == t_x))
            def _():
                outt[jnp.where(i == t, 0, 1)] = value.T.astype(BF16)

        def result_rows(i):
            result = pool[mid_at(i), :] + centred(pair_sum(1, i) + down_bias)
            keep_out(i, result)

            @pl.when(first_section)
            def _():
                @pl.when(i >= 2)
                def _():
                    hop_copy(i - 2, xbuf).wait_send()

                lane = lax.broadcasted_iota(jnp.int32, result.shape, 1)
                resb[lax.rem(i, 2)] = jnp.where(lane == width - 1, 0.0, result).astype(BF16)
                hop_copy(i, xbuf).start()

        def forward(step):
            i_mlp = jnp.where(first_section, step - blocks, step - 1)
            i_res = i_mlp - 1
            some_res = (i_res >= 0) & (i_res < blocks)

            @pl.when(step < blocks)
            def _():
                attention_rows(step)

            @pl.when(last_section & some_res)
            def _():
                result_rows(i_res)

            @pl.when((i_mlp >= 0) & (i_mlp < blocks))
            def _():
                mlp_rows(i_mlp)

            @pl.when(first_section & some_res)
            def _():
                result_rows(i_res)

        loop(2 * blocks + 1, forward)

        def rows_out(target, which):
            return (
                pltpu.make_async_copy(outt.at[0], target.at[xh], sl.at[2]),
                send(outt.at[1], target.at[xh], so, (which,), to_x),
            )

        act_copies = rows_out(act, 0)
        for copy in act_copies:
            copy.start()

        @pl.when(first_section)
        def _():
            loop(2, lambda i: hop_copy(blocks - 2 + i, xbuf).wait_send())

        def other_at(k):
            row = k * CHUNK
            early = lax.div(row, 2 * rows) * length + 2 * rows + lax.rem(row, 2 * rows)
            return pl.ds(pl.multiple_of(jnp.where(row < 8 * rows, early, row - 8 * rows), CHUNK), CHUNK)

        def own_at(k):
            row = k * CHUNK
            late = jnp.where(row < 7 * rows, row - 5 * rows, row - 3 * rows)
            late = jnp.where(row < 5 * rows, row + 4 * rows, late)
            return pl.ds(pl.multiple_of(jnp.where(row < 2 * rows, row + 2 * rows, late), CHUNK), CHUNK)

        def x_copy(k):
            return send(ex.at[other_at(k)], xrec.at[k], sr, (k,), to_x)

        def put(turn, first, value):
            @pl.when(turn == 0)
            def _():
                for k in range(value.shape[0] // CHUNK):
                    ex[other_at(first + k), :] = value[k * CHUNK : (k + 1) * CHUNK].astype(BF16)

            @pl.when(turn == 1)
            def _():
                for k in range(value.shape[0] // CHUNK):
                    pool[own_at(first + k), :] = value[k * CHUNK : (k + 1) * CHUNK]

        def start(turn, first, number):
            @pl.when(turn == 0)
            def _():
                loop(number, lambda k: x_copy(first + k).start())

        tile = 256
        tiles = width // tile

        def down_part(turn, k):
            at = pl.ds(pl.multiple_of(k * tile, tile), tile)
            first = k * (tile // CHUNK)
            put(turn, first, dot(gmt[at, :], hid[1 - turn].reshape(length, units)))
            start(turn, first, tile // CHUNK)

        def up_part(turn, k):
            at = pl.ds(pl.multiple_of(k * tile, tile), tile)
            first = width // CHUNK + k * (tile // CHUNK)
            put(turn, first, dot(n2t[at, :], gp[1 - turn].reshape(length, units)))
            start(turn, first, tile // CHUNK)

        def mlp_grads(turn):
            loop(tiles, lambda k: down_part(turn, k))
            loop(tiles - 1, lambda k: up_part(turn, k))

        middle = count // 2
        on_left = d < middle
        depth = jnp.where(on_left, d, count - 1 - d)
        has_outer = depth > 0
        is_mid = depth == middle - 1
        side = jnp.where(on_left, 0, 1)
        inner = (s, t, jnp.where(on_left, d + 1, d - 1))
        outer = (s, t, jnp.where(on_left, d - 1, d + 1))
        lag = 3
        lag_in = lag * depth
        lag_mid = lag * middle
        lag_out = lag_mid + lag * (middle - depth)
        lag_all = lag_mid + lag * middle

        def in_copy(k):
            return send(xrec.at[k], cin.at[k], sc, (0, k), inner)

        def cross_copy(k):
            return send(xrec.at[k], fin.at[k], sc, (1, k), inner)

        def back_copy(k):
            return send(fin.at[k], fin.at[k], sc, (2, k), inner)

        def out_copy(k):
            return send(fin.at[k], fin.at[k], sc, (3, k), outer)

        def chunk_out(k):
            place = 0
            for name in ("down", "up", "qkv", "out"):
                number = r[name].shape[0] // CHUNK

                @pl.when((k >= place) & (k < place + number))
                def _():
                    at = pl.ds(pl.multiple_of((k - place) * CHUNK, CHUNK), CHUNK)
                    pltpu.make_async_copy(fin.at[k], r[name].at[at], so.at[0, 2 + k]).start()

                place += number

        small_x = send(soth, srec, ss, (0,), to_x)
        s_in = send(sown, scin, ss, (1,), inner)
        s_cross = send(sown, sfin, ss, (2,), inner)
        s_back = send(sfin, sfin, ss, (3,), inner)
        s_out = send(sfin, sfin, ss, (4,), outer)

        def reduce_small(it):
            small_owner = side == 0
            begin = chunks - 4

            @pl.when(it == begin)
            def _():
                small_x.wait()
                sown[...] = sown[...] + srec[...]

            @pl.when(it == begin + lag_in)
            def _():
                @pl.when(has_outer)
                def _():
                    s_in.wait_recv()
                    sown[...] = sown[...] + scin[...]

                @pl.when(jnp.logical_not(is_mid))
                def _():
                    s_in.start()

                @pl.when(is_mid & jnp.logical_not(small_owner))
                def _():
                    s_cross.start()

            @pl.when((it == begin + lag_mid) & is_mid & small_owner)
            def _():
                s_cross.wait_recv()
                sfin[...] = sfin[...] + sown[...]
                s_back.start()

            @pl.when(it == begin + lag_out)
            def _():
                @pl.when(is_mid & jnp.logical_not(small_owner))
                def _():
                    s_back.wait_recv()

                @pl.when(jnp.logical_not(is_mid))
                def _():
                    s_out.wait_recv()

                @pl.when(has_outer)
                def _():
                    s_out.start()

        def reduce(it):
            @pl.when(it < chunks)
            def _():
                k = it
                x_copy(k).wait()
                xrec[k] = (pool[own_at(k), :] + xrec[k].astype(F32)).astype(BF16)

            k_in = it - lag_in

            @pl.when((k_in >= 0) & (k_in < chunks))
            def _():
                k = k_in
                owner = lax.rem(k, 2) == side

                @pl.when(has_outer)
                def _():
                    in_copy(k).wait_recv()
                    xrec[k] = (xrec[k].astype(F32) + cin[k].astype(F32)).astype(BF16)

                @pl.when(jnp.logical_not(is_mid))
                def _():
                    in_copy(k).start()

                @pl.when(is_mid & jnp.logical_not(owner))
                def _():
                    cross_copy(k).start()

            k_mid = it - lag_mid

            @pl.when((k_mid >= 0) & (k_mid < chunks) & is_mid)
            def _():
                k = k_mid

                @pl.when(lax.rem(k, 2) == side)
                def _():
                    cross_copy(k).wait_recv()
                    fin[k] = (xrec[k].astype(F32) + fin[k].astype(F32)).astype(BF16)
                    back_copy(k).start()

                    @pl.when(has_outer)
                    def _():
                        out_copy(k).start()

                    chunk_out(k)

            k_out = it - lag_out

            @pl.when((k_out >= 0) & (k_out < chunks))
            def _():
                k = k_out
                owner = lax.rem(k, 2) == side

                @pl.when(is_mid & jnp.logical_not(owner))
                def _():
                    back_copy(k).wait_recv()

                @pl.when(jnp.logical_not(is_mid))
                def _():
                    out_copy(k).wait_recv()

                @pl.when(jnp.logical_not(is_mid & owner))
                def _():
                    @pl.when(has_outer)
                    def _():
                        out_copy(k).start()

                    chunk_out(k)

            reduce_small(it)

        def down_back(i):
            @pl.when(first_section)
            def _():
                hop_copy(i, cotb).wait_recv()
                hop_core(i, cotb).start()
                hop_core(i, cotb).wait()

            grad = centred(cotb[i].astype(F32))
            pool[grad_at(i), :] = grad
            gmt[:, at_row(i)] = grad.T.astype(BF16)
            grad = grad.astype(BF16)
            sown[3:4, :] += row_sum(grad.astype(F32))
            branch = 0.0
            for slot, sums in ((0, sown), (1, soth)):
                before = (dot(grad, wd[slot]) * gp[slot, i].astype(F32)).astype(BF16)
                gp[slot, i] = before
                sums[4:5, :] += row_sum(before.astype(F32))
                branch = branch + dot(before, wu[slot], NT)
            pair_send(0, i, branch)

        def out_back(i):
            grad, gain_grad = norm_back(pair_sum(0, i), pool[mid_at(i), :], mlp_gain)
            sown[2:3, :] += gain_grad
            grad = grad + pool[grad_at(i), :]
            pool[grad_at(i), :] = grad
            grad = grad.astype(BF16)
            gat[i] = grad
            sown[1:2, :] += row_sum(grad.astype(F32))
            back = dot(wo[...].reshape(heads * HD, width), grad, NT).astype(BF16)
            for h in range(heads):
                dot_[i, h] = back[h * HD : (h + 1) * HD]

        def attend_back(i, h):
            slot, place = lax.div(h, hs), lax.rem(h, hs)
            query, back = qt[i, h], dot_[i, h]
            parts = key_parts(i)
            cols = slice(i * rows, (i + 1) * rows)
            probs, g_probs = [], []
            centre = 0.0
            for a, b, g in parts:
                prob = jnp.exp(masked(dot(kn[h, a:b], query), i, a, b, g) - lse[i, h])
                g_prob = dot(vn[h, a:b], back)
                centre = centre + row_sum(prob * g_prob)
                probs.append(prob)
                g_probs.append(g_prob)
            g_query = 0.0
            for prob, g_prob, (a, b, _) in zip(probs, g_probs, parts, strict=True):
                g_score = (prob * (g_prob - centre)).astype(BF16)
                g_value = dot(back, prob.astype(BF16), NT)
                g_key = dot(query, g_score, NT)
                g_query = g_query + dot(kt[h, :, a:b], g_score)
                if i == blocks - 1:
                    dv[h, :, a:b] = g_value
                    dk[h, :, a:b] = g_key
                else:
                    dv[h, :, a:b] += g_value
                    dk[h, :, a:b] += g_key
            dqkv[slot, 0, place, :, cols] = (g_query * SCALE).astype(BF16)
            dqkv[slot, 1, place, :, cols] = dk[h, :, cols].astype(BF16)
            dqkv[slot, 2, place, :, cols] = dv[h, :, cols].astype(BF16)

        def qkv_back(i):
            branch = 0.0
            for slot in range(slots):
                three = dqkv[slot, :, :, :, at_row(i)].reshape(3 * part, rows)
                branch = branch + dot(three, wq[slot], TN)
            pair_send(1, i, branch)

        def in_back(i):
            grad, gain_grad = norm_back(pair_sum(1, i), expanded(xbuf[i]), attn_gain)
            sown[0:1, :] += gain_grad
            grad = grad + pool[grad_at(i), :]
            grad = grad - grad[:, width - 1 :]
            keep_out(i, grad)

            @pl.when(last_section)
            def _():
                @pl.when(i < blocks - 2)
                def _():
                    hop_copy(i + 2, cotb).wait_send()

                resb[lax.rem(i, 2)] = grad.astype(BF16)
                hop_copy(i, cotb).start()

        def advance(step, place):
            def body(it, carry):
                reduce(it)
                return carry

            first, stop = 0, 0
            for at, (lo, hi) in EARLY[place].items():
                first = jnp.where(first_section & (step == at), lo, first)
                stop = jnp.where(first_section & (step == at), hi, stop)
            lax.fori_loop(first, stop, body, 0)

        def backward(step):
            later = jnp.where(step >= blocks - 1, 1, 0)
            idle = first_section & (step == blocks - 2)
            n_rest = jnp.where(first_section, jnp.where(idle, -1, step - later), step)
            idle_in = first_section & (step == blocks - 1)
            n_in = jnp.where(first_section, jnp.where(idle_in, -1, step - 1 - later), step - 1)
            last = blocks - 1

            @pl.when(step < blocks)
            def _():
                down_back(last - step)

            @pl.when(step == jnp.where(first_section, blocks - 1, blocks + 1))
            def _():
                loop(2, mlp_grads)

            @pl.when(step == 1)
            def _():
                for copy in act_copies:
                    copy.wait()

            @pl.when((n_in >= 0) & (n_in < blocks))
            def _():
                in_back(last - n_in)

            @pl.when((n_rest >= 0) & (n_rest < blocks))
            def _():
                i = last - n_rest
                out_back(i)
                advance(step, 0)
                each_block(i, attend_back)
                advance(step, 1)
                qkv_back(i)
                advance(step, 2)

        loop(blocks + 2, backward)
        ones = jnp.ones((8, length), BF16)
        sown[5:6, : 3 * part] = dot(ones, dqkv[0].reshape(3 * part, length), NT)[0:1]
        soth[5:6, : 3 * part] = dot(ones, dqkv[1].reshape(3 * part, length), NT)[0:1]
        soth[0:4, :] = sown[0:4, :]
        small_x.start()

        def attention_grads(turn):
            slot = 1 - turn
            up_part(turn, tiles - 1)

            def qkv_part(k):
                first = (2 * width) // CHUNK + k * (part // CHUNK)
                put(turn, first, dot(dqkv[slot, k].reshape(part, length), nrm[...].reshape(length, width)))

            loop(3, qkv_part)
            first = (2 * width + 3 * part) // CHUNK
            context = ctx[pl.ds(slot * hs, hs)].reshape(part, length)
            put(turn, first, dot(context, gat[...].reshape(length, width)))
            start(turn, 2 * (width // CHUNK), chunks - 2 * (width // CHUNK))

        loop(2, attention_grads)
        eg_copies = rows_out(eg, 1)
        for copy in eg_copies:
            copy.start()

        def rest(it, carry):
            reduce(it)
            return carry

        begun = max(hi for place in EARLY for _, hi in place.values())
        lax.fori_loop(jnp.where(first_section, begun, 0), chunks + lag_all, rest, 0)
        small[...] = sfin[...]

        @pl.when(jnp.logical_not(is_mid))
        def _():
            s_in.wait_send()

        @pl.when(is_mid & (side == 1))
        def _():
            s_cross.wait_send()

        @pl.when(is_mid & (side == 0))
        def _():
            s_back.wait_send()

        @pl.when(has_outer)
        def _():
            s_out.wait_send()

        def drain(k):
            owner = lax.rem(k, 2) == side

            @pl.when(jnp.logical_not(is_mid))
            def _():
                in_copy(k).wait_send()

            @pl.when(is_mid & jnp.logical_not(owner))
            def _():
                cross_copy(k).wait_send()

            @pl.when(is_mid & owner)
            def _():
                back_copy(k).wait_send()

            @pl.when(has_outer)
            def _():
                out_copy(k).wait_send()

            pltpu.make_async_copy(fin.at[k], r["down"].at[pl.ds(0, CHUNK)], so.at[0, 2 + k]).wait()

        loop(chunks, drain)

        @pl.when(last_section)
        def _():
            loop(2, lambda i: hop_copy(i, cotb).wait_send())

        for copy in eg_copies:
            copy.wait()

    return kernel


def per_device(
    block_input,
    segments,
    cotangent,
    attn_gain,
    qkv_weight,
    qv_bias,
    out_weight,
    out_bias,
    mlp_gain,
    up_projection_weight,
    up_bias,
    down_projection_weight,
    down_bias,
):
    micros, rows, _, kept = block_input.shape
    width = qkv_weight.shape[1]
    part = qkv_weight.shape[3]
    units = up_projection_weight.shape[2]
    blocks = lax.axis_size("tensor")
    count = lax.axis_size("dp")
    length = blocks * rows
    slots = 2
    hs = part // HD
    heads = slots * hs
    chunks = (2 * width + 4 * part) // CHUNK

    def features_first(array):
        return jnp.pad(array[:, :, 0, :].transpose(0, 2, 1), ((0, 0), (0, width - kept), (0, 0)))

    qv_row = jnp.pad(qv_bias.reshape(1, 2 * part), ((0, 0), (0, width - 2 * part)))
    rows_of = [attn_gain, mlp_gain, out_bias, down_bias, up_bias, qv_row, up_bias, qv_row]
    inputs = {
        "xin": features_first(block_input),
        "cot": features_first(cotangent),
        "wqh": qkv_weight[0].transpose(1, 2, 0).reshape(3 * part, width),
        "woh": out_weight[0],
        "wuh": up_projection_weight[0],
        "wdh": down_projection_weight[0],
        "misc": jnp.concatenate(rows_of).astype(F32),
        "seg": segments[:, 0, :],
    }
    outputs = {
        "act": ((micros, width, rows), BF16),
        "eg": ((micros, width, rows), BF16),
        "down": ((width, units), BF16),
        "up": ((width, units), BF16),
        "qkv": ((3 * part, width), BF16),
        "out": ((part, width), BF16),
        "small": ((8, width), F32),
    }
    scratch = {
        "wq": ((slots, 3 * part, width), BF16),
        "wo": ((slots, part, width), BF16),
        "wu": ((slots, width, units), BF16),
        "wd": ((slots, width, units), BF16),
        "mc": ((slots, 8, width), F32),
        "xbuf": ((blocks, rows, width), BF16),
        "cotb": ((blocks, rows, width), BF16),
        "resb": ((2, rows, width), BF16),
        "outt": ((2, width, rows), BF16),
        "pool": ((max(2 * length, chunks * CHUNK), width), F32),
        "nrm": ((blocks, rows, width), BF16),
        "n2t": ((width, length), BF16),
        "qt": ((blocks, heads, HD, rows), BF16),
        "kt": ((heads, HD, length), BF16),
        "vt": ((heads, HD, length), BF16),
        "kn": ((heads, length, HD), BF16),
        "vn": ((heads, length, HD), BF16),
        "ctx": ((heads, HD, length), BF16),
        "lse": ((blocks, heads, 1, rows), F32),
        "segc": ((length, 128), F32),
        "gp": ((slots, blocks, rows, units), BF16),
        "hid": ((slots, blocks, rows, units), BF16),
        "gmt": ((width, length), BF16),
        "gat": ((blocks, rows, width), BF16),
        "dot": ((blocks, heads, HD, rows), BF16),
        "dqkv": ((slots, 3, hs, HD, length), BF16),
        "dk": ((heads, HD, length), F32),
        "dv": ((heads, HD, length), F32),
        "ex": ((4 * length, width), BF16),
        "xrec": ((chunks, CHUNK, width), BF16),
        "cin": ((chunks, CHUNK, width), BF16),
        "fin": ((chunks, CHUNK, width), BF16),
        "sown": ((8, width), F32),
        "soth": ((8, width), F32),
        "srec": ((8, width), F32),
        "scin": ((8, width), F32),
        "sfin": ((8, width), F32),
    }
    dma = pltpu.SemaphoreType.DMA
    semaphores = {
        "sl": dma((8,)),
        "sg": dma((2, 4)),
        "sw": dma((2, 2, 12)),
        "se": dma((2, 2, blocks)),
        "sh": dma((2, 2, blocks)),
        "so": dma((2, 2 + chunks)),
        "sr": dma((2, chunks)),
        "sc": dma((2, 4, chunks)),
        "ss": dma((2, 5)),
    }
    in_vmem = {"seg", "small"}

    def spec(name):
        return pl.BlockSpec(memory_space=pltpu.VMEM if name in in_vmem else pl.ANY)

    names = [*inputs, *outputs, *scratch, *semaphores]
    act, eg, down, up, qkv, out, small = pl.pallas_call(
        make_kernel(names, count),
        out_shape=[jax.ShapeDtypeStruct(*item) for item in outputs.values()],
        in_specs=[spec(name) for name in inputs],
        out_specs=[spec(name) for name in outputs],
        scratch_shapes=[pltpu.VMEM(*item) for item in scratch.values()] + list(semaphores.values()),
        compiler_params=pltpu.CompilerParams(
            collective_id=0, has_side_effects=True, vmem_limit_bytes=63 * 1024 * 1024
        ),
        name="layers",
    )(*inputs.values())

    def positions_first(array):
        return array[:, :kept, :].transpose(0, 2, 1)[None, :, :, None, :]

    qv = small[5, : 3 * part].reshape(3, part)
    return (
        positions_first(act),
        positions_first(eg).astype(F32),
        small[0:1],
        qkv.reshape(3, part, width).transpose(2, 0, 1).astype(F32)[None],
        qv[0::2][None],
        out.astype(F32)[None],
        small[1:2],
        small[2:3],
        up.astype(F32)[None],
        small[4:5, :units],
        down.astype(F32)[None],
        small[3:4],
    )


def solution(mesh):
    in_specs = (
        P(None, "tensor", "dp", None),
        P(None, "dp", None),
        P(None, "tensor", "dp", None),
        P("section", None),
        P("section", None, None, "tensor"),
        P("section", None, "tensor"),
        P("section", "tensor", None),
        P("section", None),
        P("section", None),
        P("section", None, "tensor"),
        P("section", "tensor"),
        P("section", None, "tensor"),
        P("section", None),
    )
    out_specs = (
        P("section", None, "tensor", "dp", None),
        P("section", None, "tensor", "dp", None),
        P("section", None),
        P("section", None, None, "tensor"),
        P("section", None, "tensor"),
        P("section", "tensor", None),
        P("section", None),
        P("section", None),
        P("section", None, "tensor"),
        P("section", "tensor"),
        P("section", None, "tensor"),
        P("section", None),
    )
    return jax.shard_map(
        per_device, mesh=mesh, in_specs=in_specs, out_specs=out_specs, check_vma=False
    )
```

```python
import jax
import jax.numpy as jnp
from jax import lax
from jax.experimental import pallas as pl
from jax.experimental.pallas import tpu as pltpu
from jax.sharding import PartitionSpec as P

HD = 64
EPS = 1e-05
SCALE = 0.125
NEGATIVE = -1e30
CHUNK = 32
LAG = 4
HEADS_FORWARD = 3
HEADS_BACKWARD = 3
EARLY = ({3: (0, 2), 4: (8, 12), 5: (16, 21)}, {3: (2, 7), 4: (12, 15), 5: (21, 23)}, {3: (7, 8), 4: (15, 16), 5: (23, 26)})
PLAN = {
    "down": ((0, 1, 2, 3, -1, -1, -1, -1), (0, 1, 2, 3, -1, -1, -1, -1)),
    "rest": ((0, -1, -1, 1, 2, 3, -1, -1), (-1, 0, 1, 2, 3, -1, -1, -1)),
    "in": ((-1, 0, -1, -1, 1, 2, 3, -1), (-1, -1, 0, 1, -1, 2, 3, -1)),
    "grads": ((-1, -1, -1, 0, 1, -1, -1, -1), (-1, -1, -1, -1, -1, -1, -1, 2)),
}
MESH = pl.DeviceIdType.MESH
F32 = jnp.float32
BF16 = jnp.bfloat16
NN = (((1,), (0,)), ((), ()))
NT = (((1,), (1,)), ((), ()))
TN = (((0,), (0,)), ((), ()))
GELU_C = 0.7978845608028654
GELU_A = 0.044715


def dot(left, right, dims=NN):
    return lax.dot_general(left, right, dims, preferred_element_type=F32)


def lane_sum(value):
    return jnp.sum(value, axis=-1, keepdims=True)


def row_sum(value):
    return jnp.sum(value, axis=0, keepdims=True)


def expanded(block):
    value = block.astype(F32)
    lane = lax.broadcasted_iota(jnp.int32, value.shape, 1)
    return jnp.where(lane == value.shape[1] - 1, -lane_sum(value), value)


def norm_factor(full):
    return lax.rsqrt(lane_sum(full * full) * (1.0 / full.shape[1]) + EPS)


def centred(value):
    return value - lane_sum(value) * (1.0 / value.shape[1])


def norm_back(grad, full, gain):
    factor = norm_factor(full)
    weighted = grad * gain
    inner = lane_sum(weighted * full) * (1.0 / full.shape[1])
    gain_grad = row_sum(grad * full * factor)
    return centred(factor * weighted - full * (factor * factor * factor * inner)), gain_grad


def make_kernel(names, count):
    def kernel(*refs):
        r = dict(zip(names, refs, strict=True))
        xin, cot, misc, seg = r["xin"], r["cot"], r["misc"], r["seg"]
        act, eg, small = r["act"], r["eg"], r["small"]
        wq, wo, wud, mc = r["wq"], r["wo"], r["wud"], r["mc"]
        xbuf, cotb, resb, outt = r["xbuf"], r["cotb"], r["resb"], r["outt"]
        pool, nrm, n2t = r["pool"], r["nrm"], r["n2t"]
        qt, kt, vt, kn, vn = r["qt"], r["kt"], r["vt"], r["kn"], r["vn"]
        ctx, lse, segc = r["ctx"], r["lse"], r["segc"]
        gp, hid, gmt, gat = r["gp"], r["hid"], r["gmt"], r["gat"]
        dot_, dqkv, dk, dv = r["dot"], r["dqkv"], r["dk"], r["dv"]
        ex, xrec, cin, ready = r["ex"], r["xrec"], r["cin"], r["ready"]
        sown, soth, srec, scin, sfin = r["sown"], r["soth"], r["srec"], r["scin"], r["sfin"]
        sl, sg, sw, se, sh, so, sr, sc, ss = (
            r[name] for name in ("sl", "sg", "sw", "se", "sh", "so", "sr", "sc", "ss"))
        blocks, rows, width = xbuf.shape
        length = blocks * rows
        slots, hs = wq.shape[0], wo.shape[1] // HD
        heads = slots * hs
        part = wo.shape[1]
        units = wud.shape[1]
        chunks = xrec.shape[0]
        wu = [wud.at[pl.ds(slot * width, width)] for slot in range(slots)]
        wd = [wud.at[pl.ds((slots + slot) * width, width)] for slot in range(slots)]

        s = lax.axis_index("section")
        t = lax.axis_index("tensor")
        d = lax.axis_index("dp")
        core, xh = lax.rem(t, 2), lax.div(t, 2)
        t_core = 2 * xh + 1 - core
        t_x = 2 * (1 - xh) + core
        to_core = (s, t_core, d)
        to_x = (s, t_x, d)
        to_y = (1 - s, t, d)
        to_xy = (1 - s, t_x, d)
        parity = lax.rem(d, 2)
        to_pair = (s, t, d + 1 - 2 * parity)
        left, right = (s, t, d - 1), (s, t, d + 1)
        first_section, last_section = s == 0, s == 1

        def send(src, dst, sems, at, device):
            return pltpu.make_async_remote_copy(
                src_ref=src, dst_ref=dst, send_sem=sems.at[(0, *at)], recv_sem=sems.at[(1, *at)],
                device_id=device, device_id_type=MESH)

        def loop(stop, body):
            def step(i, carry):
                body(i)
                return carry

            lax.fori_loop(0, stop, step, 0)

        barrier = pltpu.get_barrier_semaphore()
        for device in (to_core, to_x, to_y, to_xy):
            pl.semaphore_signal(barrier, inc=1, device_id=device, device_id_type=MESH)

        @pl.when(d > 0)
        def _():
            pl.semaphore_signal(barrier, inc=1, device_id=left, device_id_type=MESH)

        @pl.when(d < count - 1)
        def _():
            pl.semaphore_signal(barrier, inc=1, device_id=right, device_id_type=MESH)

        ends = jnp.where(d > 0, 1, 0) + jnp.where(d < count - 1, 1, 0)
        pl.semaphore_wait(barrier, 4 + ends)

        def at_row(i):
            return pl.ds(pl.multiple_of(i * rows, rows), rows)

        mid_at = at_row

        def grad_at(i):
            return pl.ds(pl.multiple_of(length + i * rows, rows), rows)

        def rows_in(source, device):
            mine, other = gmt.at[:, at_row(t)], gmt.at[:, at_row(t_x)]
            return (
                pltpu.make_async_copy(source.at[xh], mine, sl.at[0]),
                send(source.at[xh], mine, sg, (1,), to_core),
                send(source.at[1 - xh], mine, sg, (0,), device),
                send(other, other, sg, (2,), to_core),
            )

        def rows_wait(copies, target):
            local, core_own, across, core_other = copies
            across.wait_recv()
            core_other.start()
            local.wait()
            core_own.wait()
            core_other.wait()

            def turn(i):
                target[i] = gmt[:, at_row(i)].astype(F32).T.astype(BF16)

            loop(blocks, turn)

        @pl.when(first_section)
        def _():
            for copy in rows_in(xin, to_xy)[:2]:
                copy.start()

        @pl.when(last_section)
        def _():
            rows_in(xin, to_xy)[2].start()

        misc_local = pltpu.make_async_copy(misc, mc.at[0], sl.at[1])
        misc_x = send(misc, mc.at[1], sg, (3,), to_x)
        misc_local.start()
        misc_x.start()
        locals_, pieces = [], []
        for which, (name, target, cuts) in enumerate((("wqh", [wq.at[0], wq.at[1]], 2), ("woh", [wo.at[0], wo.at[1]], 1), ("wuh", wu, 2), ("wdh", wd, 3))):
            source = r[name]
            locals_.append(pltpu.make_async_copy(source, target[0], sl.at[4 + which]))
            half = source.shape[0] // 2
            step = half // cuts
            group = []
            for cut in range(cuts):
                at = pl.ds(pl.multiple_of(parity * half + cut * step, 16), step)
                place = 3 * which + cut
                group.append((
                    send(source.at[at], target[1].at[at], sw, (0, place), to_x),
                    send(target[1].at[at], target[1].at[at], sw, (1, place), to_pair),
                ))
            pieces.append(group)
        for local, group in zip(locals_, pieces, strict=True):
            local.start()
            for across, _ in group:
                across.start()

        @pl.when(last_section)
        def _():
            for copy in rows_in(cot, to_x)[:3]:
                copy.start()

        def pass_on(which, *cuts):
            for cut in cuts:
                across, pair = pieces[which][cut]
                across.wait_recv()
                pair.start()

        def have(which):
            locals_[which].wait()
            for across, pair in pieces[which]:
                across.wait_send()
                pair.wait()

        sown[...] = jnp.zeros_like(sown)
        soth[...] = jnp.zeros_like(soth)
        segment = seg[pl.ds(xh, 1), :]
        segc[...] = jnp.broadcast_to(segment.astype(F32), (128, length)).T

        def ex_at(kind, i):
            return pl.ds(pl.multiple_of(kind * length + i * rows, rows), rows)

        def shifted(i):
            return lax.rem(i + 1, blocks)

        def pair_copy(kind, i):
            return send(ex.at[ex_at(2 * kind, i)], ex.at[ex_at(2 * kind + 1, i)], se, (kind, i), to_core)

        def pair_send(kind, i, value):
            ex[ex_at(2 * kind, i), :] = value.astype(BF16)
            pair_copy(kind, i).start()

        def pair_sum(kind, i):
            pair_copy(kind, i).wait()
            return ex[ex_at(2 * kind, i), :].astype(F32) + ex[ex_at(2 * kind + 1, i), :].astype(F32)

        half_rows = rows // 2
        own_half = pl.ds(pl.multiple_of(core * half_rows, half_rows), half_rows)

        def hop_copy(i, target):
            return send(resb.at[lax.rem(i, 2), own_half], target.at[i, own_half], sh, (0, i), to_y)

        def hop_core(i, target):
            return send(target.at[i, own_half], target.at[i, own_half], sh, (1, i), to_core)

        pass_on(0, 0, 1)

        @pl.when(first_section)
        def _():
            rows_wait(rows_in(xin, to_xy), xbuf)
            pass_on(1, 0)

        @pl.when(last_section)
        def _():
            pass_on(1, 0)
            pass_on(2, 0, 1)
            pass_on(3, 0, 1, 2)
            copies = rows_in(cot, to_x)
            rows_wait(copies, cotb)
            copies[2].wait_send()
            rows_in(xin, to_xy)[2].wait_send()

        misc_local.wait()
        misc_x.wait()
        attn_gain, mlp_gain, out_bias, down_bias = (mc[0, i : i + 1, :] for i in range(4))
        have(0)

        def allowed(i, j0, j1, diagonal):
            same = segc[j0:j1, :]
            same = jnp.concatenate([same] * (rows // same.shape[1]), axis=1)
            cols = slice(i * rows, (i + 1) * rows)
            keep = same == seg[pl.ds(xh, 1), cols].astype(F32)
            if diagonal:
                key = lax.broadcasted_iota(jnp.int32, keep.shape, 0)
                query = lax.broadcasted_iota(jnp.int32, keep.shape, 1)
                keep = keep & (key <= query)
            return keep

        def masked(scores, i, j0, j1, diagonal):
            return jnp.where(allowed(i, j0, j1, diagonal), scores, NEGATIVE)

        def key_parts(i):
            parts = [(i * rows, (i + 1) * rows, True)]
            if i > 0:
                parts.append((0, i * rows, False))
            return parts

        def project(i):
            full = expanded(xbuf[i])
            normed = (full * norm_factor(full) * attn_gain).astype(BF16)
            nrm[i] = normed
            cols = at_row(i)
            for slot in range(slots):
                three = dot(wq[slot], normed, NT)
                bias = jnp.broadcast_to(mc[slot, 5:6, : 2 * part], (8, 2 * part)).T[:, 0:1]
                query = (three[:part] + bias[:part]).astype(BF16) * SCALE
                key = three[part : 2 * part]
                value = (three[2 * part :] + bias[part:]).astype(BF16).astype(F32)
                for h in range(hs):
                    at = slice(h * HD, (h + 1) * HD)
                    head = slot * hs + h
                    qt[i, head] = query[at].astype(BF16)
                    kt[head, :, cols] = key[at].astype(BF16)
                    vt[head, :, cols] = value[at].astype(BF16)
                    kn[head, cols, :] = key[at].T.astype(BF16)
                    vn[head, cols, :] = value[at].T.astype(BF16)

        def attend(i, group):
            cols = slice(i * rows, (i + 1) * rows)
            parts = key_parts(i)
            scores = [[masked(dot(kn[h, a:b], qt[i, h]), i, a, b, g) for a, b, g in parts] for h in group]
            tops = []
            for score in scores:
                top = score[0].max(axis=0, keepdims=True)
                for more in score[1:]:
                    top = jnp.maximum(top, more.max(axis=0, keepdims=True))
                tops.append(top)
            powers = [[jnp.exp(one - top) for one in score] for score, top in zip(scores, tops, strict=True)]
            totals = [sum(row_sum(one) for one in power) for power in powers]
            contexts = [
                sum(dot(vt[h, :, a:b], one.astype(BF16)) for one, (a, b, _) in zip(power, parts, strict=True))
                for h, power in zip(group, powers, strict=True)
            ]
            for h, top, total, context in zip(group, tops, totals, contexts, strict=True):
                ctx[h, :, cols] = (context / total).astype(BF16)
                lse[i, h] = top + jnp.log(total)

        def each_block(i, body, number):
            for block in range(blocks):

                @pl.when(i == block)
                def _():
                    loop(heads // number, lambda n: body(block, [n * number + k for k in range(number)]))

        def attention_rows(i):
            @pl.when(last_section & (i == 0))
            def _():
                hop_copy(0, xbuf).wait_recv()
                hop_core(0, xbuf).start()

            @pl.when(last_section)
            def _():
                hop_core(i, xbuf).wait()

            project(i)
            each_block(i, attend, HEADS_FORWARD)

            @pl.when(i == 0)
            def _():
                have(1)

            context = ctx[:, :, at_row(i)].reshape(heads * HD, rows)
            pair_send(0, shifted(i), dot(context, wo[...].reshape(heads * HD, width), TN))

            for step, (which, cut) in enumerate(((2, 0), (2, 1), (3, 0), (3, 1))):

                @pl.when((i == step) & first_section)
                def _():
                    pass_on(which, cut)

            @pl.when(last_section & (i < blocks - 1))
            def _():
                hop_copy(i + 1, xbuf).wait_recv()
                hop_core(i + 1, xbuf).start()

        def up_rows(i):
            @pl.when(i == 0)
            def _():
                have(2)

            branch = pair_sum(0, shifted(i)) + out_bias
            middle = expanded(xbuf[i]) + centred(branch)
            pool[mid_at(i), :] = middle
            normed = middle * norm_factor(middle) * mlp_gain
            n2t[:, at_row(i)] = normed.T.astype(BF16)
            normed = normed.astype(BF16)
            for slot in range(slots):
                pre = dot(normed, wu[slot][...]) + mc[slot, 4:5, :]
                square = pre * pre
                bend = jnp.tanh(GELU_C * pre * (1.0 + GELU_A * square))
                grow = 0.5 * (1.0 + bend)
                hid[slot, i] = (pre * grow).astype(BF16)
                slope = GELU_C * (1.0 + 3.0 * GELU_A * square)
                gp[slot, i] = (grow + 0.5 * pre * (1.0 - bend * bend) * slope).astype(BF16)

        def down_rows(i):
            @pl.when(i == 0)
            def _():
                @pl.when(first_section)
                def _():
                    pass_on(3, 2)

                have(3)

            branch = dot(hid[0, i], wd[0][...], NT)
            for slot in range(1, slots):
                branch = branch + dot(hid[slot, i], wd[slot][...], NT)
            pair_send(1, shifted(i), branch)

        def keep_out(i, value):
            @pl.when((i == t) | (i == t_x))
            def _():
                outt[jnp.where(i == t, 0, 1)] = value.T.astype(BF16)

        def result_rows(i):
            result = pool[mid_at(i), :] + centred(pair_sum(1, shifted(i)) + down_bias)
            keep_out(i, result)

            @pl.when(first_section)
            def _():
                @pl.when(i >= 2)
                def _():
                    hop_copy(i - 2, xbuf).wait_send()

                lane = lax.broadcasted_iota(jnp.int32, result.shape, 1)
                resb[lax.rem(i, 2)] = jnp.where(lane == width - 1, 0.0, result).astype(BF16)
                hop_copy(i, xbuf).start()

        def forward(step):
            i_up = jnp.where(first_section, step - blocks, step - 1)
            i_down = jnp.where(first_section, step - 2 * blocks, step - 1)
            i_res = i_down - 1
            some_res = (i_res >= 0) & (i_res < blocks)

            @pl.when(step < blocks)
            def _():
                attention_rows(step)

            @pl.when(last_section & some_res & (i_res < blocks - 1))
            def _():
                result_rows(i_res)

            @pl.when((i_up >= 0) & (i_up < blocks))
            def _():
                up_rows(i_up)

            @pl.when((i_down >= 0) & (i_down < blocks))
            def _():
                down_rows(i_down)

            @pl.when(first_section & some_res)
            def _():
                result_rows(i_res)

        loop(3 * blocks + 1, forward)

        def rows_out(target, which):
            return (
                pltpu.make_async_copy(outt.at[0], target.at[xh], sl.at[2]),
                send(outt.at[1], target.at[xh], so, (which,), to_x),
            )

        act_copies = rows_out(act, 0)

        @pl.when(first_section)
        def _():
            loop(2, lambda i: hop_copy(blocks - 2 + i, xbuf).wait_send())

        def other_at(k):
            row = k * CHUNK
            third = jnp.where(row < 3 * rows, 0, jnp.where(row < 6 * rows, 1, 2))
            place = row - third * 3 * rows
            kind = jnp.where(place < rows, 0, jnp.where(place < 2 * rows, 1, 2))
            row = kind * (length - rows) + (blocks - 1 - third) * rows + place
            return pl.ds(pl.multiple_of(row, CHUNK), CHUNK)

        def own_at(k):
            row = k * CHUNK
            third = jnp.where(row < 3 * rows, 0, jnp.where(row < 6 * rows, 1, 2))
            place = row - third * 3 * rows
            down = jnp.where(place < rows, place + 3 * rows, place + 6 * rows)
            up = jnp.where(place < 2 * rows, place + rows, place + 4 * rows)
            rest = jnp.where(place < rows, place, place + 3 * rows)
            row = jnp.where(third == 0, down, jnp.where(third == 1, up, rest))
            return pl.ds(pl.multiple_of(row, CHUNK), CHUNK)

        def x_copy(k):
            return send(ex.at[other_at(k)], xrec.at[k], sr, (k,), to_x)

        def put(turn, first, value):
            @pl.when(turn == 0)
            def _():
                for k in range(value.shape[0] // CHUNK):
                    ex[other_at(first + k), :] = value[k * CHUNK : (k + 1) * CHUNK].astype(BF16)

            @pl.when(turn == 1)
            def _():
                for k in range(value.shape[0] // CHUNK):
                    pool[own_at(first + k), :] = value[k * CHUNK : (k + 1) * CHUNK]

        def start(turn, first, number):
            @pl.when(turn == 0)
            def _():
                loop(number, lambda k: x_copy(first + k).start())

        tile = 256
        tiles = width // tile

        def down_part(turn, k):
            at = pl.ds(pl.multiple_of(k * tile, tile), tile)
            first = k * (tile // CHUNK)
            put(turn, first, dot(gmt[at, :], hid[1 - turn].reshape(length, units)))
            start(turn, first, tile // CHUNK)

        def up_part(turn, k):
            at = pl.ds(pl.multiple_of(k * tile, tile), tile)
            first = width // CHUNK + k * (tile // CHUNK)
            put(turn, first, dot(n2t[at, :], gp[1 - turn].reshape(length, units)))
            start(turn, first, tile // CHUNK)

        def down_grads(turn):
            loop(tiles, lambda k: down_part(turn, k))

        def up_grads(turn):
            loop(tiles, lambda k: up_part(turn, k))

        middle = count // 2
        on_left = d < middle
        depth = jnp.where(on_left, d, count - 1 - d)
        has_outer = depth > 0
        is_mid = depth == middle - 1
        inner = (s, t, jnp.where(on_left, d + 1, d - 1))
        outer = (s, t, jnp.where(on_left, d - 1, d + 1))
        lag_in = LAG * depth
        lag_mid = LAG * middle
        lag_out = lag_mid + LAG * (middle - 1 - depth)
        lag_all = lag_mid + LAG * (middle - 1)

        def fin_at(k):
            return pl.ds(pl.multiple_of(k * CHUNK, CHUNK), CHUNK)

        def in_copy(k):
            return send(xrec.at[k], cin.at[k], sc, (0, k), inner)

        def cross_copy(k):
            return send(xrec.at[k], wud.at[fin_at(k)], sc, (1, k), inner)

        def out_copy(k):
            return send(wud.at[fin_at(k)], wud.at[fin_at(k)], sc, (2, k), outer)

        outs, place = [], 0
        for which, name in enumerate(("down", "up", "qkv", "out")):
            number = r[name].shape[0]
            copy = pltpu.make_async_copy(wud.at[pl.ds(place, number)], r[name], so.at[0, 2 + which])
            place += number
            outs.append((place // CHUNK - 1, copy))

        def matrix_out(k):
            for final, copy in outs:

                @pl.when(k == final)
                def _():
                    copy.start()

        small_x = send(soth, srec, ss, (0,), to_x)
        s_in = send(sown, scin, ss, (1,), inner)
        s_cross = send(sown, sfin, ss, (2,), inner)
        s_out = send(sfin, sfin, ss, (3,), outer)

        def reduce_small(it):
            begin = chunks - 8

            @pl.when(it == begin)
            def _():
                small_x.wait()
                sown[...] = sown[...] + srec[...]

            @pl.when(it == begin + lag_in)
            def _():
                @pl.when(has_outer)
                def _():
                    s_in.wait_recv()
                    sown[...] = sown[...] + scin[...]

                @pl.when(jnp.logical_not(is_mid))
                def _():
                    s_in.start()

                @pl.when(is_mid)
                def _():
                    s_cross.start()

            @pl.when(it == begin + lag_out)
            def _():
                @pl.when(is_mid)
                def _():
                    s_cross.wait()
                    sfin[...] = sfin[...] + sown[...]

                @pl.when(jnp.logical_not(is_mid))
                def _():
                    s_out.wait_recv()

                @pl.when(has_outer)
                def _():
                    s_out.start()

        def reduce(it):
            @pl.when((it == 0) & is_mid)
            def _():
                pl.semaphore_signal(ready, inc=1, device_id=inner, device_id_type=MESH)

            @pl.when(it < chunks)
            def _():
                k = it
                x_copy(k).wait()
                xrec[k] = (pool[own_at(k), :] + xrec[k].astype(F32)).astype(BF16)

            k_in = it - lag_in

            @pl.when((k_in >= 0) & (k_in < chunks))
            def _():
                k = k_in

                @pl.when(has_outer)
                def _():
                    in_copy(k).wait_recv()
                    xrec[k] = (xrec[k].astype(F32) + cin[k].astype(F32)).astype(BF16)

                @pl.when(jnp.logical_not(is_mid))
                def _():
                    in_copy(k).start()

                @pl.when(is_mid)
                def _():
                    @pl.when(k == 0)
                    def _():
                        pl.semaphore_wait(ready, 1)

                    cross_copy(k).start()

            k_out = it - lag_out

            @pl.when((k_out >= 0) & (k_out < chunks))
            def _():
                k = k_out

                @pl.when(is_mid)
                def _():
                    cross_copy(k).wait_recv()
                    wud[fin_at(k), :] = (xrec[k].astype(F32) + wud[fin_at(k), :].astype(F32)).astype(BF16)

                @pl.when(jnp.logical_not(is_mid))
                def _():
                    out_copy(k).wait_recv()

                @pl.when(has_outer)
                def _():
                    out_copy(k).start()

                matrix_out(k)

            reduce_small(it)

        def down_back(i):
            @pl.when(first_section)
            def _():
                hop_copy(i, cotb).wait_recv()
                hop_core(i, cotb).start()
                hop_core(i, cotb).wait()

            grad = centred(cotb[i].astype(F32))
            pool[grad_at(i), :] = grad
            gmt[:, at_row(i)] = grad.T.astype(BF16)
            grad = grad.astype(BF16)
            sown[3:4, :] += row_sum(grad.astype(F32))
            branch = 0.0
            for slot, sums in ((0, sown), (1, soth)):
                before = (dot(grad, wd[slot][...]) * gp[slot, i].astype(F32)).astype(BF16)
                gp[slot, i] = before
                sums[4:5, :] += row_sum(before.astype(F32))
                branch = branch + dot(before, wu[slot][...], NT)
            pair_send(0, i, branch)

        def out_back(i):
            grad, gain_grad = norm_back(pair_sum(0, i), pool[mid_at(i), :], mlp_gain)
            sown[2:3, :] += gain_grad
            grad = grad + pool[grad_at(i), :]
            pool[grad_at(i), :] = grad
            grad = grad.astype(BF16)
            gat[i] = grad
            sown[1:2, :] += row_sum(grad.astype(F32))
            back = dot(wo[...].reshape(heads * HD, width), grad, NT).astype(BF16)
            for h in range(heads):
                dot_[i, h] = back[h * HD : (h + 1) * HD]

        def attend_back(i, group):
            parts = key_parts(i)
            cols = slice(i * rows, (i + 1) * rows)
            masks = [jnp.where(allowed(i, a, b, g), 0.0, NEGATIVE) for a, b, g in parts]
            probs, g_probs = [], []
            for h in group:
                less = [mask - lse[i, h] for mask in masks]
                probs.append([jnp.exp(dot(kn[h, a:b], qt[i, h]) + one) for one, (a, b, _) in zip(less, parts, strict=True)])
                g_probs.append([dot(vn[h, a:b], dot_[i, h]) for a, b, _ in parts])
            centres = [
                sum(row_sum(x * y) for x, y in zip(prob, g_prob, strict=True))
                for prob, g_prob in zip(probs, g_probs, strict=True)
            ]
            g_scores = [
                [(x * (y - centre)).astype(BF16) for x, y in zip(prob, g_prob, strict=True)]
                for prob, g_prob, centre in zip(probs, g_probs, centres, strict=True)
            ]
            g_values = [[dot(dot_[i, h], x.astype(BF16), NT) for x in prob] for h, prob in zip(group, probs, strict=True)]
            g_keys = [[dot(qt[i, h], x, NT) for x in g_score] for h, g_score in zip(group, g_scores, strict=True)]
            g_queries = [
                sum(dot(kt[h, :, a:b], x) for x, (a, b, _) in zip(g_score, parts, strict=True))
                for h, g_score in zip(group, g_scores, strict=True)
            ]
            for h, g_value, g_key, g_query in zip(group, g_values, g_keys, g_queries, strict=True):
                slot, place = lax.div(h, hs), lax.rem(h, hs)
                for (a, b, _), value, key in zip(parts, g_value, g_key, strict=True):
                    if i == blocks - 1:
                        dv[h, :, a:b] = value
                        dk[h, :, a:b] = key
                    else:
                        dv[h, :, a:b] += value
                        dk[h, :, a:b] += key
                dqkv[slot, 0, place, :, cols] = (g_query * SCALE).astype(BF16)
                dqkv[slot, 1, place, :, cols] = dk[h, :, cols].astype(BF16)
                dqkv[slot, 2, place, :, cols] = dv[h, :, cols].astype(BF16)

        def qkv_back(i):
            branch = 0.0
            for slot in range(slots):
                three = dqkv[slot, :, :, :, at_row(i)].reshape(3 * part, rows)
                branch = branch + dot(three, wq[slot], TN)
            pair_send(1, i, branch)

        def in_back(i):
            grad, gain_grad = norm_back(pair_sum(1, i), expanded(xbuf[i]), attn_gain)
            sown[0:1, :] += gain_grad
            grad = grad + pool[grad_at(i), :]
            grad = grad - grad[:, width - 1 :]
            keep_out(i, grad)

            @pl.when(last_section)
            def _():
                @pl.when(i < blocks - 2)
                def _():
                    hop_copy(i + 2, cotb).wait_send()

                resb[lax.rem(i, 2)] = grad.astype(BF16)
                hop_copy(i, cotb).start()

        def advance(step, place):
            def body(it, carry):
                reduce(it)
                return carry

            first, stop = 0, 0
            for at, (lo, hi) in EARLY[place].items():
                first = jnp.where(first_section & (step == at), lo, first)
                stop = jnp.where(first_section & (step == at), hi, stop)
            lax.fori_loop(first, stop, body, 0)

        def planned(step, name):
            found = -1
            for at, (first, last) in enumerate(zip(*PLAN[name], strict=True)):
                found = jnp.where(step == at, jnp.where(first_section, first, last), found)
            return found

        def backward(step):
            n_down, n_in, n_rest = (planned(step, name) for name in ("down", "in", "rest"))
            n_grad = planned(step, "grads")
            last = blocks - 1

            @pl.when(n_down >= 0)
            def _():
                down_back(last - n_down)

            @pl.when(step == 0)
            def _():
                @pl.when(last_section)
                def _():
                    result_rows(last)

                for copy in act_copies:
                    copy.start()

            @pl.when((n_grad == 0) | (n_grad == 2))
            def _():
                loop(2, down_grads)

            @pl.when(n_in == 0)
            def _():
                for copy in act_copies:
                    copy.wait()

            @pl.when(n_in >= 0)
            def _():
                in_back(last - n_in)

            @pl.when(n_rest >= 0)
            def _():
                i = last - n_rest
                out_back(i)
                advance(step, 0)
                each_block(i, attend_back, HEADS_BACKWARD)
                advance(step, 1)
                qkv_back(i)
                advance(step, 2)

            @pl.when(n_grad >= 1)
            def _():
                loop(2, up_grads)

        loop(len(PLAN["in"][0]), backward)
        ones = jnp.ones((8, length), BF16)
        sown[5:6, : 3 * part] = dot(ones, dqkv[0].reshape(3 * part, length), NT)[0:1]
        soth[5:6, : 3 * part] = dot(ones, dqkv[1].reshape(3 * part, length), NT)[0:1]
        soth[0:4, :] = sown[0:4, :]
        small_x.start()

        def attention_grads(turn):
            slot = 1 - turn

            def qkv_part(k):
                first = (2 * width) // CHUNK + k * (part // CHUNK)
                put(turn, first, dot(dqkv[slot, k].reshape(part, length), nrm[...].reshape(length, width)))

            loop(3, qkv_part)
            first = (2 * width + 3 * part) // CHUNK
            context = ctx[pl.ds(slot * hs, hs)].reshape(part, length)
            put(turn, first, dot(context, gat[...].reshape(length, width)))
            start(turn, 2 * (width // CHUNK), chunks - 2 * (width // CHUNK))

        loop(2, attention_grads)
        eg_copies = rows_out(eg, 1)
        for copy in eg_copies:
            copy.start()

        def rest(it, carry):
            reduce(it)
            return carry

        begun = max(hi for place in EARLY for _, hi in place.values())
        lax.fori_loop(jnp.where(first_section, begun, 0), chunks + lag_all, rest, 0)
        small[...] = sfin[...]

        @pl.when(jnp.logical_not(is_mid))
        def _():
            s_in.wait_send()

        @pl.when(has_outer)
        def _():
            s_out.wait_send()

        def drain(k):
            @pl.when(jnp.logical_not(is_mid))
            def _():
                in_copy(k).wait_send()

            @pl.when(is_mid)
            def _():
                cross_copy(k).wait_send()

            @pl.when(has_outer)
            def _():
                out_copy(k).wait_send()

        loop(chunks, drain)
        for _, copy in outs:
            copy.wait()

        @pl.when(last_section)
        def _():
            loop(2, lambda i: hop_copy(i, cotb).wait_send())

        for copy in eg_copies:
            copy.wait()

    return kernel


def per_device(
    block_input,
    segments,
    cotangent,
    attn_gain,
    qkv_weight,
    qv_bias,
    out_weight,
    out_bias,
    mlp_gain,
    up_projection_weight,
    up_bias,
    down_projection_weight,
    down_bias,
):
    micros, rows, _, kept = block_input.shape
    width = qkv_weight.shape[1]
    part = qkv_weight.shape[3]
    units = up_projection_weight.shape[2]
    blocks = lax.axis_size("tensor")
    count = lax.axis_size("dp")
    length = blocks * rows
    slots = 2
    hs = part // HD
    heads = slots * hs
    chunks = (2 * width + 4 * part) // CHUNK

    def features_first(array):
        return jnp.pad(array[:, :, 0, :].transpose(0, 2, 1), ((0, 0), (0, width - kept), (0, 0)))

    qv_row = jnp.pad(qv_bias.reshape(1, 2 * part), ((0, 0), (0, width - 2 * part)))
    rows_of = [attn_gain, mlp_gain, out_bias, down_bias, up_bias, qv_row, up_bias, qv_row]
    inputs = {
        "xin": features_first(block_input),
        "cot": features_first(cotangent),
        "wqh": qkv_weight[0].transpose(1, 2, 0).reshape(3 * part, width),
        "woh": out_weight[0],
        "wuh": up_projection_weight[0],
        "wdh": down_projection_weight[0],
        "misc": jnp.concatenate(rows_of).astype(F32),
        "seg": segments[:, 0, :],
    }
    outputs = {
        "act": ((micros, width, rows), BF16),
        "eg": ((micros, width, rows), BF16),
        "down": ((width, units), BF16),
        "up": ((width, units), BF16),
        "qkv": ((3 * part, width), BF16),
        "out": ((part, width), BF16),
        "small": ((8, width), F32),
    }
    scratch = {
        "wq": ((slots, 3 * part, width), BF16),
        "wo": ((slots, part, width), BF16),
        "wud": ((2 * slots * width, units), BF16),
        "mc": ((slots, 8, width), F32),
        "xbuf": ((blocks, rows, width), BF16),
        "cotb": ((blocks, rows, width), BF16),
        "resb": ((2, rows, width), BF16),
        "outt": ((2, width, rows), BF16),
        "pool": ((max(2 * length, chunks * CHUNK), width), F32),
        "nrm": ((blocks, rows, width), BF16),
        "n2t": ((width, length), BF16),
        "qt": ((blocks, heads, HD, rows), BF16),
        "kt": ((heads, HD, length), BF16),
        "vt": ((heads, HD, length), BF16),
        "kn": ((heads, length, HD), BF16),
        "vn": ((heads, length, HD), BF16),
        "ctx": ((heads, HD, length), BF16),
        "lse": ((blocks, heads, 1, rows), F32),
        "segc": ((length, 128), F32),
        "gp": ((slots, blocks, rows, units), BF16),
        "hid": ((slots, blocks, rows, units), BF16),
        "gmt": ((width, length), BF16),
        "gat": ((blocks, rows, width), BF16),
        "dot": ((blocks, heads, HD, rows), BF16),
        "dqkv": ((slots, 3, hs, HD, length), BF16),
        "dk": ((heads, HD, length), F32),
        "dv": ((heads, HD, length), F32),
        "ex": ((4 * length, width), BF16),
        "xrec": ((chunks, CHUNK, width), BF16),
        "cin": ((chunks, CHUNK, width), BF16),
        "sown": ((8, width), F32),
        "soth": ((8, width), F32),
        "srec": ((8, width), F32),
        "scin": ((8, width), F32),
        "sfin": ((8, width), F32),
    }
    dma = pltpu.SemaphoreType.DMA
    semaphores = {
        "sl": dma((8,)),
        "sg": dma((2, 4)),
        "sw": dma((2, 2, 12)),
        "se": dma((2, 2, blocks)),
        "sh": dma((2, 2, blocks)),
        "so": dma((2, 6)),
        "sr": dma((2, chunks)),
        "sc": dma((2, 3, chunks)),
        "ss": dma((2, 4)),
        "ready": pltpu.SemaphoreType.REGULAR,
    }
    in_vmem = {"seg", "small"}

    def spec(name):
        return pl.BlockSpec(memory_space=pltpu.VMEM if name in in_vmem else pl.ANY)

    names = [*inputs, *outputs, *scratch, *semaphores]
    act, eg, down, up, qkv, out, small = pl.pallas_call(
        make_kernel(names, count),
        out_shape=[jax.ShapeDtypeStruct(*item) for item in outputs.values()],
        in_specs=[spec(name) for name in inputs],
        out_specs=[spec(name) for name in outputs],
        scratch_shapes=[pltpu.VMEM(*item) for item in scratch.values()] + list(semaphores.values()),
        compiler_params=pltpu.CompilerParams(
            collective_id=0, has_side_effects=True, vmem_limit_bytes=63 * 1024 * 1024
        ),
        name="layers",
    )(*inputs.values())

    def positions_first(array):
        return array[:, :kept, :].transpose(0, 2, 1)[None, :, :, None, :]

    qv = small[5, : 3 * part].reshape(3, part)
    return (
        positions_first(act),
        positions_first(eg).astype(F32),
        small[0:1],
        qkv.reshape(3, part, width).transpose(2, 0, 1).astype(F32)[None],
        qv[0::2][None],
        out.astype(F32)[None],
        small[1:2],
        small[2:3],
        up.astype(F32)[None],
        small[4:5, :units],
        down.astype(F32)[None],
        small[3:4],
    )


def solution(mesh):
    in_specs = (
        P(None, "tensor", "dp", None),
        P(None, "dp", None),
        P(None, "tensor", "dp", None),
        P("section", None),
        P("section", None, None, "tensor"),
        P("section", None, "tensor"),
        P("section", "tensor", None),
        P("section", None),
        P("section", None),
        P("section", None, "tensor"),
        P("section", "tensor"),
        P("section", None, "tensor"),
        P("section", None),
    )
    out_specs = (
        P("section", None, "tensor", "dp", None),
        P("section", None, "tensor", "dp", None),
        P("section", None),
        P("section", None, None, "tensor"),
        P("section", None, "tensor"),
        P("section", "tensor", None),
        P("section", None),
        P("section", None),
        P("section", None, "tensor"),
        P("section", "tensor"),
        P("section", None, "tensor"),
        P("section", None),
    )
    return jax.shard_map(
        per_device, mesh=mesh, in_specs=in_specs, out_specs=out_specs, check_vma=False
    )
```

```python
import jax
import jax.numpy as jnp
from jax import lax
from jax.experimental import pallas as pl
from jax.experimental.pallas import tpu as pltpu
from jax.sharding import PartitionSpec as P

HD = 64
EPS = 1e-05
SCALE = 0.125
NEGATIVE = -1e30
CHUNK = 32
LAG = 4
HEADS_FORWARD = 6
HEADS_BACKWARD = 3
EARLY = (
    {3: (2, 4), 4: (9, 12), 5: (18, 21)},
    {3: (4, 8), 4: (12, 17), 5: (21, 23)},
    {3: (8, 9), 4: (17, 18), 5: (23, 24)},
    {6: (24, 27)},
    {3: (0, 2)},
)
PLAN = {
    "down": ((0, 1, 2, 3, -1, -1, -1, -1), (0, 1, 2, 3, -1, -1, -1, -1)),
    "rest": ((0, -1, -1, 1, 2, 3, -1, -1), (-1, 0, 1, 2, 3, -1, -1, -1)),
    "in": ((-1, 0, -1, -1, -1, -1, 3, -1), (-1, -1, 0, 1, -1, 2, 3, -1)),
    "late": ((-1, -1, -1, -1, 1, 2, -1, -1), (-1,) * 8),
    "grads": ((-1, -1, -1, 0, 1, -1, -1, -1), (-1, -1, -1, -1, -1, -1, -1, 2)),
}
MESH = pl.DeviceIdType.MESH
F32 = jnp.float32
BF16 = jnp.bfloat16
NN = (((1,), (0,)), ((), ()))
NT = (((1,), (1,)), ((), ()))
TN = (((0,), (0,)), ((), ()))
GELU_C = 0.7978845608028654
GELU_A = 0.044715


def dot(left, right, dims=NN):
    return lax.dot_general(left, right, dims, preferred_element_type=F32)


def lane_sum(value):
    return jnp.sum(value, axis=-1, keepdims=True)


def row_sum(value):
    return jnp.sum(value, axis=0, keepdims=True)


def expanded(block):
    value = block.astype(F32)
    lane = lax.broadcasted_iota(jnp.int32, value.shape, 1)
    return jnp.where(lane == value.shape[1] - 1, -lane_sum(value), value)


def norm_factor(full):
    return lax.rsqrt(lane_sum(full * full) * (1.0 / full.shape[1]) + EPS)


def centred(value):
    return value - lane_sum(value) * (1.0 / value.shape[1])


def norm_back(grad, full, gain):
    factor = norm_factor(full)
    weighted = grad * gain
    inner = lane_sum(weighted * full) * (1.0 / full.shape[1])
    gain_grad = row_sum(grad * full * factor)
    return centred(factor * weighted - full * (factor * factor * factor * inner)), gain_grad


def make_kernel(names, count):
    def kernel(*refs):
        r = dict(zip(names, refs, strict=True))
        xin, cot, seg = r["xin"], r["cot"], r["seg"]
        act, eg, small = r["act"], r["eg"], r["small"]
        wq, wo, wud, mc = r["wq"], r["wo"], r["wud"], r["mc"]
        xbuf, cotb, resb, outt = r["xbuf"], r["cotb"], r["resb"], r["outt"]
        pool, nrm, n2t = r["pool"], r["nrm"], r["n2t"]
        qt, kt, vt, kn, vn = r["qt"], r["kt"], r["vt"], r["kn"], r["vn"]
        ctx, lse, segc = r["ctx"], r["lse"], r["segc"]
        gp, hid, gmt, gat = r["gp"], r["hid"], r["gmt"], r["gat"]
        dot_, dqkv, dk, dv = r["dot"], r["dqkv"], r["dk"], r["dv"]
        ex, xrec, cin, ready = r["ex"], r["xrec"], r["cin"], r["ready"]
        sown, soth, srec, scin, sfin = r["sown"], r["soth"], r["srec"], r["scin"], r["sfin"]
        sl, sg, sw, se, sh, so, sr, sc, ss = (
            r[name] for name in ("sl", "sg", "sw", "se", "sh", "so", "sr", "sc", "ss"))
        blocks, rows, width = xbuf.shape
        length = blocks * rows
        slots, hs = wq.shape[0], wo.shape[1] // HD
        heads = slots * hs
        part = wo.shape[1]
        units = wud.shape[1]
        chunks = xrec.shape[0]
        wu = [wud.at[pl.ds(slot * width, width)] for slot in range(slots)]
        wd = [wud.at[pl.ds((slots + slot) * width, width)] for slot in range(slots)]

        s = lax.axis_index("section")
        t = lax.axis_index("tensor")
        d = lax.axis_index("dp")
        core, xh = lax.rem(t, 2), lax.div(t, 2)
        t_core = 2 * xh + 1 - core
        t_x = 2 * (1 - xh) + core
        to_core = (s, t_core, d)
        to_x = (s, t_x, d)
        to_y = (1 - s, t, d)
        to_xy = (1 - s, t_x, d)
        parity = lax.rem(d, 2)
        to_pair = (s, t, d + 1 - 2 * parity)
        left, right = (s, t, d - 1), (s, t, d + 1)
        first_section, last_section = s == 0, s == 1

        def send(src, dst, sems, at, device):
            return pltpu.make_async_remote_copy(
                src_ref=src, dst_ref=dst, send_sem=sems.at[(0, *at)], recv_sem=sems.at[(1, *at)],
                device_id=device, device_id_type=MESH)

        def loop(stop, body):
            def step(i, carry):
                body(i)
                return carry

            lax.fori_loop(0, stop, step, 0)

        barrier = pltpu.get_barrier_semaphore()
        for device in (to_core, to_x, to_y, to_xy):
            pl.semaphore_signal(barrier, inc=1, device_id=device, device_id_type=MESH)

        @pl.when(d > 0)
        def _():
            pl.semaphore_signal(barrier, inc=1, device_id=left, device_id_type=MESH)

        @pl.when(d < count - 1)
        def _():
            pl.semaphore_signal(barrier, inc=1, device_id=right, device_id_type=MESH)

        ends = jnp.where(d > 0, 1, 0) + jnp.where(d < count - 1, 1, 0)
        pl.semaphore_wait(barrier, 4 + ends)

        def at_row(i):
            return pl.ds(pl.multiple_of(i * rows, rows), rows)

        mid_at = at_row

        def grad_at(i):
            return pl.ds(pl.multiple_of(length + i * rows, rows), rows)

        def rows_in(source, device):
            mine, other = gmt.at[:, at_row(t)], gmt.at[:, at_row(t_x)]
            return (
                pltpu.make_async_copy(source.at[xh], mine, sl.at[0]),
                send(source.at[xh], mine, sg, (1,), to_core),
                send(source.at[1 - xh], mine, sg, (0,), device),
                send(other, other, sg, (2,), to_core),
            )

        def rows_wait(copies, target):
            local, core_own, across, core_other = copies
            across.wait_recv()
            core_other.start()
            local.wait()
            core_own.wait()
            core_other.wait()

            def turn(i):
                target[i] = gmt[:, at_row(i)].astype(F32).T.astype(BF16)

            loop(blocks, turn)

        @pl.when(first_section)
        def _():
            for copy in rows_in(xin, to_xy)[:2]:
                copy.start()

        @pl.when(last_section)
        def _():
            rows_in(xin, to_xy)[2].start()

        mc[0] = jnp.zeros_like(mc[0])
        for row, name in enumerate(("attn_gain", "mlp_gain", "out_bias", "down_bias", "up_bias")):
            mc[0, row : row + 1, :] = r[name][...].astype(F32)
        for row in range(2):
            mc[0, 5 + row : 6 + row, : wo.shape[1]] = r["qv_bias"][0, row : row + 1, :].astype(F32)
        misc_x = send(mc.at[0], mc.at[1], sg, (3,), to_x)
        misc_x.start()
        locals_, pieces = [], []
        for which, (name, target, cuts) in enumerate((("wqh", [wq.at[0], wq.at[1]], 2), ("woh", [wo.at[0], wo.at[1]], 1), ("wuh", wu, 2), ("wdh", wd, 4))):
            source = r[name]
            locals_.append(pltpu.make_async_copy(source, target[0], sl.at[4 + which]))
            half = source.shape[0] // 2
            step = half // cuts
            group = []
            for cut in range(cuts):
                at = pl.ds(pl.multiple_of(parity * half + cut * step, 16), step)
                place = 4 * which + cut
                group.append((
                    send(source.at[at], target[1].at[at], sw, (0, place), to_x),
                    send(target[1].at[at], target[1].at[at], sw, (1, place), to_pair),
                ))
            pieces.append(group)
        for which, (local, group) in enumerate(zip(locals_, pieces, strict=True)):
            if which == 3:

                @pl.when(last_section)
                def _():
                    for copy in rows_in(cot, to_x)[:3]:
                        copy.start()

            local.start()
            for across, _ in group:
                across.start()

        def pass_on(which, *cuts):
            for cut in cuts:
                across, pair = pieces[which][cut]
                across.wait_recv()
                pair.start()

        def have(which):
            locals_[which].wait()
            for across, pair in pieces[which]:
                across.wait_send()
                pair.wait()

        sown[...] = jnp.zeros_like(sown)
        soth[...] = jnp.zeros_like(soth)
        segment = seg[xh]
        segc[...] = jnp.broadcast_to(segment.astype(F32), (128, length)).T

        def ex_at(kind, i):
            return pl.ds(pl.multiple_of(kind * length + i * rows, rows), rows)

        def shifted(i):
            return lax.rem(i + 1, blocks)

        def pair_copy(kind, i):
            return send(ex.at[ex_at(2 * kind, i)], ex.at[ex_at(2 * kind + 1, i)], se, (kind, i), to_core)

        def pair_send(kind, i, value):
            ex[ex_at(2 * kind, i), :] = value.astype(BF16)
            pair_copy(kind, i).start()

        def pair_sum(kind, i):
            pair_copy(kind, i).wait()
            return ex[ex_at(2 * kind, i), :].astype(F32) + ex[ex_at(2 * kind + 1, i), :].astype(F32)

        half_rows = rows // 2
        own_half = pl.ds(pl.multiple_of(core * half_rows, half_rows), half_rows)

        def hop_copy(i, target):
            return send(resb.at[lax.rem(i, 2), own_half], target.at[i, own_half], sh, (0, i), to_y)

        def hop_core(i, target):
            return send(target.at[i, own_half], target.at[i, own_half], sh, (1, i), to_core)

        pass_on(0, 0, 1)

        @pl.when(first_section)
        def _():
            rows_wait(rows_in(xin, to_xy), xbuf)
            pass_on(1, 0)

        @pl.when(last_section)
        def _():
            pass_on(1, 0)
            pass_on(2, 0, 1)
            copies = rows_in(cot, to_x)
            rows_wait(copies, cotb)
            pass_on(3, 0, 1, 2, 3)
            copies[2].wait_send()
            rows_in(xin, to_xy)[2].wait_send()

        misc_x.wait()
        attn_gain, mlp_gain, out_bias, down_bias = (mc[0, i : i + 1, :] for i in range(4))
        have(0)

        def allowed(i, j0, j1, diagonal):
            same = segc[j0:j1, :]
            same = jnp.concatenate([same] * (rows // same.shape[1]), axis=1)
            cols = slice(i * rows, (i + 1) * rows)
            keep = same == seg[xh, :, cols].astype(F32)
            if diagonal:
                key = lax.broadcasted_iota(jnp.int32, keep.shape, 0)
                query = lax.broadcasted_iota(jnp.int32, keep.shape, 1)
                keep = keep & (key <= query)
            return keep

        def masked(scores, i, j0, j1, diagonal):
            return jnp.where(allowed(i, j0, j1, diagonal), scores, NEGATIVE)

        def key_parts(i):
            parts = [(i * rows, (i + 1) * rows, True)]
            if i > 0:
                parts.append((0, i * rows, False))
            return parts

        def project(i):
            full = expanded(xbuf[i])
            normed = (full * norm_factor(full) * attn_gain).astype(BF16)
            nrm[i] = normed
            cols = at_row(i)
            for slot in range(slots):
                three = dot(wq[slot], normed, NT)
                bias = mc[slot, :, :part].T
                query = (three[:part] + bias[:, 5:6]).astype(BF16) * SCALE
                key = three[part : 2 * part]
                value = (three[2 * part :] + bias[:, 6:7]).astype(BF16).astype(F32)
                for h in range(hs):
                    at = slice(h * HD, (h + 1) * HD)
                    head = slot * hs + h
                    qt[i, head] = query[at].astype(BF16)
                    kt[head, :, cols] = key[at].astype(BF16)
                    vt[head, :, cols] = value[at].astype(BF16)
                    kn[head, cols, :] = key[at].T.astype(BF16)
                    vn[head, cols, :] = value[at].T.astype(BF16)

        def attend(i, group):
            cols = slice(i * rows, (i + 1) * rows)
            parts = key_parts(i)
            scores = [[masked(dot(kn[h, a:b], qt[i, h]), i, a, b, g) for a, b, g in parts] for h in group]
            tops = []
            for score in scores:
                top = score[0].max(axis=0, keepdims=True)
                for more in score[1:]:
                    top = jnp.maximum(top, more.max(axis=0, keepdims=True))
                tops.append(top)
            powers = [[jnp.exp(one - top) for one in score] for score, top in zip(scores, tops, strict=True)]
            totals = [sum(row_sum(one) for one in power) for power in powers]
            contexts = [
                sum(dot(vt[h, :, a:b], one.astype(BF16)) for one, (a, b, _) in zip(power, parts, strict=True))
                for h, power in zip(group, powers, strict=True)
            ]
            for h, top, total, context in zip(group, tops, totals, contexts, strict=True):
                ctx[h, :, cols] = (context / total).astype(BF16)
                lse[i, h] = top + jnp.log(total)

        def each_block(i, body, number):
            for block in range(blocks):

                @pl.when(i == block)
                def _():
                    loop(heads // number, lambda n: body(block, [n * number + k for k in range(number)]))

        def attention_rows(i):
            @pl.when(last_section & (i == 0))
            def _():
                hop_copy(0, xbuf).wait_recv()
                hop_core(0, xbuf).start()

            @pl.when(last_section)
            def _():
                hop_core(i, xbuf).wait()

            project(i)
            each_block(i, attend, HEADS_FORWARD)

            @pl.when(i == 0)
            def _():
                have(1)

            context = ctx[:, :, at_row(i)].reshape(heads * HD, rows)
            pair_send(0, shifted(i), dot(context, wo[...].reshape(heads * HD, width), TN))

            for step, (which, cut) in enumerate(((2, 0), (2, 1), (3, 0), (3, 1))):

                @pl.when((i == step) & first_section)
                def _():
                    pass_on(which, cut)

            @pl.when(last_section & (i < blocks - 1))
            def _():
                hop_copy(i + 1, xbuf).wait_recv()
                hop_core(i + 1, xbuf).start()

        def up_rows(i):
            @pl.when(i == 0)
            def _():
                have(2)

            branch = pair_sum(0, shifted(i)) + out_bias
            middle = expanded(xbuf[i]) + centred(branch)
            pool[mid_at(i), :] = middle
            normed = middle * norm_factor(middle) * mlp_gain
            n2t[:, at_row(i)] = normed.T.astype(BF16)
            normed = normed.astype(BF16)
            for slot in range(slots):
                pre = dot(normed, wu[slot][...]) + mc[slot, 4:5, :]
                square = pre * pre
                bend = jnp.tanh(pre * (GELU_C + (GELU_C * GELU_A) * square))
                grow = 0.5 + 0.5 * bend
                value = pre * grow
                hid[slot, i] = value.astype(BF16)
                slope = GELU_C + (3.0 * GELU_C * GELU_A) * square
                gp[slot, i] = (grow + value * (1.0 - bend) * slope).astype(BF16)

            for step, cut in ((0, 2), (1, 3)):

                @pl.when((i == step) & first_section)
                def _():
                    pass_on(3, cut)

        def down_rows(i):
            @pl.when(i == 0)
            def _():
                have(3)

            branch = dot(hid[0, i], wd[0][...], NT)
            for slot in range(1, slots):
                branch = branch + dot(hid[slot, i], wd[slot][...], NT)
            pair_send(1, shifted(i), branch)

        def keep_out(i, value):
            @pl.when((i == t) | (i == t_x))
            def _():
                outt[jnp.where(i == t, 0, 1)] = value.T.astype(BF16)

        def result_rows(i):
            result = pool[mid_at(i), :] + centred(pair_sum(1, shifted(i)) + down_bias)
            keep_out(i, result)

            @pl.when(first_section)
            def _():
                @pl.when(i >= 2)
                def _():
                    hop_copy(i - 2, xbuf).wait_send()

                lane = lax.broadcasted_iota(jnp.int32, result.shape, 1)
                resb[lax.rem(i, 2)] = jnp.where(lane == width - 1, 0.0, result).astype(BF16)
                hop_copy(i, xbuf).start()

        def forward(step):
            i_up = jnp.where(first_section, step - blocks, step - 1)
            i_down = jnp.where(first_section, step - 2 * blocks, step - 1)
            i_res = i_down - 1
            some_res = (i_res >= 0) & (i_res < blocks)

            @pl.when(step < blocks)
            def _():
                attention_rows(step)

            @pl.when(last_section & some_res & (i_res < blocks - 1))
            def _():
                result_rows(i_res)

            @pl.when((i_up >= 0) & (i_up < blocks))
            def _():
                up_rows(i_up)

            @pl.when((i_down >= 0) & (i_down < blocks))
            def _():
                down_rows(i_down)

            @pl.when(first_section & some_res)
            def _():
                result_rows(i_res)

        loop(3 * blocks + 1, forward)

        def rows_out(target, which):
            return (
                pltpu.make_async_copy(outt.at[0], target.at[xh], sl.at[2]),
                send(outt.at[1], target.at[xh], so, (which,), to_x),
            )

        act_copies = rows_out(act, 0)

        @pl.when(first_section)
        def _():
            loop(2, lambda i: hop_copy(blocks - 2 + i, xbuf).wait_send())

        def other_at(k):
            row = k * CHUNK
            third = jnp.where(row < 3 * rows, 0, jnp.where(row < 6 * rows, 1, 2))
            place = row - third * 3 * rows
            kind = jnp.where(place < rows, 0, jnp.where(place < 2 * rows, 1, 2))
            row = kind * (length - rows) + (blocks - 1 - third) * rows + place
            return pl.ds(pl.multiple_of(row, CHUNK), CHUNK)

        def own_at(k):
            row = k * CHUNK
            third = jnp.where(row < 3 * rows, 0, jnp.where(row < 6 * rows, 1, 2))
            place = row - third * 3 * rows
            down = jnp.where(place < rows, place + 3 * rows, place + 6 * rows)
            up = jnp.where(place < 2 * rows, place + rows, place + 4 * rows)
            rest = jnp.where(place < rows, place, place + 3 * rows)
            row = jnp.where(third == 0, down, jnp.where(third == 1, up, rest))
            return pl.ds(pl.multiple_of(row, CHUNK), CHUNK)

        def x_copy(k):
            return send(ex.at[other_at(k)], xrec.at[k], sr, (k,), to_x)

        def put(turn, first, value):
            @pl.when(turn == 0)
            def _():
                for k in range(value.shape[0] // CHUNK):
                    ex[other_at(first + k), :] = value[k * CHUNK : (k + 1) * CHUNK].astype(BF16)

            @pl.when(turn == 1)
            def _():
                for k in range(value.shape[0] // CHUNK):
                    pool[own_at(first + k), :] = value[k * CHUNK : (k + 1) * CHUNK]

        def start(turn, first, number):
            @pl.when(turn == 0)
            def _():
                loop(number, lambda k: x_copy(first + k).start())

        tile = 256
        tiles = width // tile

        def down_part(turn, k):
            at = pl.ds(pl.multiple_of(k * tile, tile), tile)
            first = k * (tile // CHUNK)
            put(turn, first, dot(gmt[at, :], hid[1 - turn].reshape(length, units)))
            start(turn, first, tile // CHUNK)

        def up_part(turn, k):
            at = pl.ds(pl.multiple_of(k * tile, tile), tile)
            first = width // CHUNK + k * (tile // CHUNK)
            put(turn, first, dot(n2t[at, :], gp[1 - turn].reshape(length, units)))
            start(turn, first, tile // CHUNK)

        def down_grads(turn):
            loop(tiles, lambda k: down_part(turn, k))

        def up_grads(turn):
            loop(tiles, lambda k: up_part(turn, k))

        middle = count // 2
        on_left = d < middle
        depth = jnp.where(on_left, d, count - 1 - d)
        has_outer = depth > 0
        is_mid = depth == middle - 1
        inner = (s, t, jnp.where(on_left, d + 1, d - 1))
        outer = (s, t, jnp.where(on_left, d - 1, d + 1))
        lag_in = LAG * depth
        lag_mid = LAG * middle
        lag_out = lag_mid + LAG * (middle - 1 - depth)
        lag_all = lag_mid + LAG * (middle - 1)

        def fin_at(k):
            return pl.ds(pl.multiple_of(k * CHUNK, CHUNK), CHUNK)

        def in_copy(k):
            return send(xrec.at[k], cin.at[k], sc, (0, k), inner)

        def cross_copy(k):
            return send(xrec.at[k], wud.at[fin_at(k)], sc, (1, k), inner)

        def out_copy(k):
            return send(wud.at[fin_at(k)], wud.at[fin_at(k)], sc, (2, k), outer)

        outs, place = [], 0
        for which, name in enumerate(("down", "up", "qkv", "out")):
            number = r[name].shape[0]
            copy = pltpu.make_async_copy(wud.at[pl.ds(place, number)], r[name], so.at[0, 2 + which])
            place += number
            outs.append((place // CHUNK - 1, copy))

        def matrix_out(k):
            for final, copy in outs:

                @pl.when(k == final)
                def _():
                    copy.start()

        small_x = send(soth, srec, ss, (0,), to_x)
        s_in = send(sown, scin, ss, (1,), inner)
        s_cross = send(sown, sfin, ss, (2,), inner)
        s_out = send(sfin, sfin, ss, (3,), outer)

        def reduce_small(it):
            begin = chunks - 8

            @pl.when(it == begin)
            def _():
                small_x.wait()
                sown[...] = sown[...] + srec[...]

            @pl.when(it == begin + lag_in)
            def _():
                @pl.when(has_outer)
                def _():
                    s_in.wait_recv()
                    sown[...] = sown[...] + scin[...]

                @pl.when(jnp.logical_not(is_mid))
                def _():
                    s_in.start()

                @pl.when(is_mid)
                def _():
                    s_cross.start()

            @pl.when(it == begin + lag_out)
            def _():
                @pl.when(is_mid)
                def _():
                    s_cross.wait()
                    sfin[...] = sfin[...] + sown[...]

                @pl.when(jnp.logical_not(is_mid))
                def _():
                    s_out.wait_recv()

                @pl.when(has_outer)
                def _():
                    s_out.start()

        def reduce(it):
            @pl.when((it == 0) & is_mid)
            def _():
                pl.semaphore_signal(ready, inc=1, device_id=inner, device_id_type=MESH)

            @pl.when(it < chunks)
            def _():
                k = it
                x_copy(k).wait()
                xrec[k] = (pool[own_at(k), :] + xrec[k].astype(F32)).astype(BF16)

            k_in = it - lag_in

            @pl.when((k_in >= 0) & (k_in < chunks))
            def _():
                k = k_in

                @pl.when(has_outer)
                def _():
                    in_copy(k).wait_recv()
                    xrec[k] = (xrec[k].astype(F32) + cin[k].astype(F32)).astype(BF16)

                @pl.when(jnp.logical_not(is_mid))
                def _():
                    in_copy(k).start()

                @pl.when(is_mid)
                def _():
                    @pl.when(k == 0)
                    def _():
                        pl.semaphore_wait(ready, 1)

                    cross_copy(k).start()

            k_out = it - lag_out

            @pl.when((k_out >= 0) & (k_out < chunks))
            def _():
                k = k_out

                @pl.when(is_mid)
                def _():
                    cross_copy(k).wait_recv()
                    wud[fin_at(k), :] = (xrec[k].astype(F32) + wud[fin_at(k), :].astype(F32)).astype(BF16)

                @pl.when(jnp.logical_not(is_mid))
                def _():
                    out_copy(k).wait_recv()

                @pl.when(has_outer)
                def _():
                    out_copy(k).start()

                matrix_out(k)

            reduce_small(it)

        def down_back(i):
            @pl.when(first_section)
            def _():
                hop_copy(i, cotb).wait_recv()
                hop_core(i, cotb).start()
                hop_core(i, cotb).wait()

            grad = centred(cotb[i].astype(F32))
            pool[grad_at(i), :] = grad
            gmt[:, at_row(i)] = grad.T.astype(BF16)
            grad = grad.astype(BF16)
            sown[3:4, :] += row_sum(grad.astype(F32))
            branch = 0.0
            for slot, sums in ((0, sown), (1, soth)):
                before = (dot(grad, wd[slot][...]) * gp[slot, i].astype(F32)).astype(BF16)
                gp[slot, i] = before
                sums[4:5, :] += row_sum(before.astype(F32))
                branch = branch + dot(before, wu[slot][...], NT)
            pair_send(0, i, branch)

        def out_back(i):
            grad, gain_grad = norm_back(pair_sum(0, i), pool[mid_at(i), :], mlp_gain)
            sown[2:3, :] += gain_grad
            grad = grad + pool[grad_at(i), :]
            pool[grad_at(i), :] = grad
            grad = grad.astype(BF16)
            gat[i] = grad
            sown[1:2, :] += row_sum(grad.astype(F32))
            back = dot(wo[...].reshape(heads * HD, width), grad, NT).astype(BF16)
            for h in range(heads):
                dot_[i, h] = back[h * HD : (h + 1) * HD]

        def attend_back(i, group):
            parts = key_parts(i)
            cols = slice(i * rows, (i + 1) * rows)
            masks = [jnp.where(allowed(i, a, b, g), 0.0, NEGATIVE) for a, b, g in parts]
            probs, g_probs = [], []
            for h in group:
                less = [mask - lse[i, h] for mask in masks]
                probs.append([jnp.exp(dot(kn[h, a:b], qt[i, h]) + one) for one, (a, b, _) in zip(less, parts, strict=True)])
                g_probs.append([dot(vn[h, a:b], dot_[i, h]) for a, b, _ in parts])
            centres = [
                sum(row_sum(x * y) for x, y in zip(prob, g_prob, strict=True))
                for prob, g_prob in zip(probs, g_probs, strict=True)
            ]
            g_scores = [
                [(x * (y - centre)).astype(BF16) for x, y in zip(prob, g_prob, strict=True)]
                for prob, g_prob, centre in zip(probs, g_probs, centres, strict=True)
            ]
            g_values = [[dot(dot_[i, h], x.astype(BF16), NT) for x in prob] for h, prob in zip(group, probs, strict=True)]
            g_keys = [[dot(qt[i, h], x, NT) for x in g_score] for h, g_score in zip(group, g_scores, strict=True)]
            g_queries = [
                sum(dot(kt[h, :, a:b], x) for x, (a, b, _) in zip(g_score, parts, strict=True))
                for h, g_score in zip(group, g_scores, strict=True)
            ]
            for h, g_value, g_key, g_query in zip(group, g_values, g_keys, g_queries, strict=True):
                slot, place = lax.div(h, hs), lax.rem(h, hs)
                for (a, b, _), value, key in zip(parts, g_value, g_key, strict=True):
                    if i == blocks - 1:
                        dv[h, :, a:b] = value
                        dk[h, :, a:b] = key
                    else:
                        dv[h, :, a:b] += value
                        dk[h, :, a:b] += key
                dqkv[slot, 0, place, :, cols] = (g_query * SCALE).astype(BF16)
                dqkv[slot, 1, place, :, cols] = dk[h, :, cols].astype(BF16)
                dqkv[slot, 2, place, :, cols] = dv[h, :, cols].astype(BF16)

        def qkv_back(i):
            branch = 0.0
            for slot in range(slots):
                three = dqkv[slot, :, :, :, at_row(i)].reshape(3 * part, rows)
                branch = branch + dot(three, wq[slot], TN)
            pair_send(1, i, branch)

        def in_back(i):
            grad, gain_grad = norm_back(pair_sum(1, i), expanded(xbuf[i]), attn_gain)
            sown[0:1, :] += gain_grad
            grad = grad + pool[grad_at(i), :]
            grad = grad - grad[:, width - 1 :]
            keep_out(i, grad)

            @pl.when(last_section)
            def _():
                @pl.when(i < blocks - 2)
                def _():
                    hop_copy(i + 2, cotb).wait_send()

                resb[lax.rem(i, 2)] = grad.astype(BF16)
                hop_copy(i, cotb).start()

        def advance(step, place):
            def body(it, carry):
                reduce(it)
                return carry

            first, stop = 0, 0
            for at, (lo, hi) in EARLY[place].items():
                first = jnp.where(first_section & (step == at), lo, first)
                stop = jnp.where(first_section & (step == at), hi, stop)
            lax.fori_loop(first, stop, body, 0)

        def planned(step, name):
            found = -1
            for at, (first, last) in enumerate(zip(*PLAN[name], strict=True)):
                found = jnp.where(step == at, jnp.where(first_section, first, last), found)
            return found

        def backward(step):
            n_down, n_in, n_rest, n_late = (planned(step, name) for name in ("down", "in", "rest", "late"))
            n_grad = planned(step, "grads")
            last = blocks - 1
            advance(step, 3)

            @pl.when(n_down >= 0)
            def _():
                down_back(last - n_down)

            @pl.when(step == 0)
            def _():
                @pl.when(last_section)
                def _():
                    result_rows(last)

                for copy in act_copies:
                    copy.start()

            @pl.when((n_grad == 0) | (n_grad == 2))
            def _():
                loop(2, down_grads)
                advance(step, 4)

            @pl.when(n_in == 0)
            def _():
                for copy in act_copies:
                    copy.wait()

            @pl.when(n_in >= 0)
            def _():
                in_back(last - n_in)

            @pl.when(n_rest >= 0)
            def _():
                i = last - n_rest
                out_back(i)
                advance(step, 0)

                @pl.when(n_late >= 0)
                def _():
                    in_back(last - n_late)

                @pl.when(n_grad == 1)
                def _():
                    loop(2, up_grads)

                each_block(i, attend_back, HEADS_BACKWARD)
                advance(step, 1)
                qkv_back(i)
                advance(step, 2)

            @pl.when(n_grad == 2)
            def _():
                loop(2, up_grads)

        loop(len(PLAN["in"][0]), backward)
        ones = jnp.ones((8, length), BF16)
        sown[5:6, : 3 * part] = dot(ones, dqkv[0].reshape(3 * part, length), NT)[0:1]
        soth[5:6, : 3 * part] = dot(ones, dqkv[1].reshape(3 * part, length), NT)[0:1]
        soth[0:4, :] = sown[0:4, :]
        small_x.start()

        def attention_grads(turn):
            slot = 1 - turn

            def qkv_part(k):
                first = (2 * width) // CHUNK + k * (part // CHUNK)
                put(turn, first, dot(dqkv[slot, k].reshape(part, length), nrm[...].reshape(length, width)))

            loop(3, qkv_part)
            first = (2 * width + 3 * part) // CHUNK
            context = ctx[pl.ds(slot * hs, hs)].reshape(part, length)
            put(turn, first, dot(context, gat[...].reshape(length, width)))
            start(turn, 2 * (width // CHUNK), chunks - 2 * (width // CHUNK))

        loop(2, attention_grads)
        eg_copies = rows_out(eg, 1)
        for copy in eg_copies:
            copy.start()

        def rest(it, carry):
            reduce(it)
            return carry

        begun = max(hi for place in EARLY for _, hi in place.values())
        lax.fori_loop(jnp.where(first_section, begun, 0), chunks + lag_all, rest, 0)
        small[...] = sfin[...]

        @pl.when(jnp.logical_not(is_mid))
        def _():
            s_in.wait_send()

        @pl.when(has_outer)
        def _():
            s_out.wait_send()

        def drain(k):
            @pl.when(jnp.logical_not(is_mid))
            def _():
                in_copy(k).wait_send()

            @pl.when(is_mid)
            def _():
                cross_copy(k).wait_send()

            @pl.when(has_outer)
            def _():
                out_copy(k).wait_send()

        loop(chunks, drain)
        for _, copy in outs:
            copy.wait()

        @pl.when(last_section)
        def _():
            loop(2, lambda i: hop_copy(i, cotb).wait_send())

        for copy in eg_copies:
            copy.wait()

    return kernel


def per_device(
    block_input,
    segments,
    cotangent,
    attn_gain,
    qkv_weight,
    qv_bias,
    out_weight,
    out_bias,
    mlp_gain,
    up_projection_weight,
    up_bias,
    down_projection_weight,
    down_bias,
):
    micros, rows, _, kept = block_input.shape
    width = qkv_weight.shape[1]
    part = qkv_weight.shape[3]
    units = up_projection_weight.shape[2]
    blocks = lax.axis_size("tensor")
    count = lax.axis_size("dp")
    length = blocks * rows
    slots = 2
    hs = part // HD
    heads = slots * hs
    chunks = (2 * width + 4 * part) // CHUNK

    def features_first(array):
        return jnp.pad(array[:, :, 0, :].transpose(0, 2, 1), ((0, 0), (0, width - kept), (0, 0)))

    inputs = {
        "xin": features_first(block_input),
        "cot": features_first(cotangent),
        "wqh": qkv_weight[0].transpose(1, 2, 0).reshape(3 * part, width),
        "woh": out_weight[0],
        "wuh": up_projection_weight[0],
        "wdh": down_projection_weight[0],
        "attn_gain": attn_gain,
        "mlp_gain": mlp_gain,
        "out_bias": out_bias,
        "down_bias": down_bias,
        "up_bias": up_bias,
        "qv_bias": qv_bias,
        "seg": segments,
    }
    outputs = {
        "act": ((micros, width, rows), BF16),
        "eg": ((micros, width, rows), BF16),
        "down": ((width, units), BF16),
        "up": ((width, units), BF16),
        "qkv": ((3 * part, width), BF16),
        "out": ((part, width), BF16),
        "small": ((8, width), F32),
    }
    scratch = {
        "wq": ((slots, 3 * part, width), BF16),
        "wo": ((slots, part, width), BF16),
        "wud": ((2 * slots * width, units), BF16),
        "mc": ((slots, 8, width), F32),
        "xbuf": ((blocks, rows, width), BF16),
        "cotb": ((blocks, rows, width), BF16),
        "resb": ((2, rows, width), BF16),
        "outt": ((2, width, rows), BF16),
        "pool": ((max(2 * length, chunks * CHUNK), width), F32),
        "nrm": ((blocks, rows, width), BF16),
        "n2t": ((width, length), BF16),
        "qt": ((blocks, heads, HD, rows), BF16),
        "kt": ((heads, HD, length), BF16),
        "vt": ((heads, HD, length), BF16),
        "kn": ((heads, length, HD), BF16),
        "vn": ((heads, length, HD), BF16),
        "ctx": ((heads, HD, length), BF16),
        "lse": ((blocks, heads, 1, rows), F32),
        "segc": ((length, 128), F32),
        "gp": ((slots, blocks, rows, units), BF16),
        "hid": ((slots, blocks, rows, units), BF16),
        "gmt": ((width, length), BF16),
        "gat": ((blocks, rows, width), BF16),
        "dot": ((blocks, heads, HD, rows), BF16),
        "dqkv": ((slots, 3, hs, HD, length), BF16),
        "dk": ((heads, HD, length), F32),
        "dv": ((heads, HD, length), F32),
        "ex": ((4 * length, width), BF16),
        "xrec": ((chunks, CHUNK, width), BF16),
        "cin": ((chunks, CHUNK, width), BF16),
        "sown": ((8, width), F32),
        "soth": ((8, width), F32),
        "srec": ((8, width), F32),
        "scin": ((8, width), F32),
        "sfin": ((8, width), F32),
    }
    dma = pltpu.SemaphoreType.DMA
    semaphores = {
        "sl": dma((8,)),
        "sg": dma((2, 4)),
        "sw": dma((2, 2, 16)),
        "se": dma((2, 2, blocks)),
        "sh": dma((2, 2, blocks)),
        "so": dma((2, 6)),
        "sr": dma((2, chunks)),
        "sc": dma((2, 3, chunks)),
        "ss": dma((2, 4)),
        "ready": pltpu.SemaphoreType.REGULAR,
    }
    in_vmem = {"attn_gain", "mlp_gain", "out_bias", "down_bias", "up_bias", "qv_bias", "seg", "small"}

    def spec(name):
        return pl.BlockSpec(memory_space=pltpu.VMEM if name in in_vmem else pl.ANY)

    names = [*inputs, *outputs, *scratch, *semaphores]
    act, eg, down, up, qkv, out, small = pl.pallas_call(
        make_kernel(names, count),
        out_shape=[jax.ShapeDtypeStruct(*item) for item in outputs.values()],
        in_specs=[spec(name) for name in inputs],
        out_specs=[spec(name) for name in outputs],
        scratch_shapes=[pltpu.VMEM(*item) for item in scratch.values()] + list(semaphores.values()),
        compiler_params=pltpu.CompilerParams(
            collective_id=0, has_side_effects=True, vmem_limit_bytes=63 * 1024 * 1024
        ),
        name="layers",
    )(*inputs.values())

    def positions_first(array):
        return array[:, :kept, :].transpose(0, 2, 1)[None, :, :, None, :]

    qv = small[5, : 3 * part].reshape(3, part)
    return (
        positions_first(act),
        positions_first(eg).astype(F32),
        small[0:1],
        qkv.reshape(3, part, width).transpose(2, 0, 1).astype(F32)[None],
        qv[0::2][None],
        out.astype(F32)[None],
        small[1:2],
        small[2:3],
        up.astype(F32)[None],
        small[4:5, :units],
        down.astype(F32)[None],
        small[3:4],
    )


def solution(mesh):
    in_specs = (
        P(None, "tensor", "dp", None),
        P(None, "dp", None),
        P(None, "tensor", "dp", None),
        P("section", None),
        P("section", None, None, "tensor"),
        P("section", None, "tensor"),
        P("section", "tensor", None),
        P("section", None),
        P("section", None),
        P("section", None, "tensor"),
        P("section", "tensor"),
        P("section", None, "tensor"),
        P("section", None),
    )
    out_specs = (
        P("section", None, "tensor", "dp", None),
        P("section", None, "tensor", "dp", None),
        P("section", None),
        P("section", None, None, "tensor"),
        P("section", None, "tensor"),
        P("section", "tensor", None),
        P("section", None),
        P("section", None),
        P("section", None, "tensor"),
        P("section", "tensor"),
        P("section", None, "tensor"),
        P("section", None),
    )
    return jax.shard_map(
        per_device, mesh=mesh, in_specs=in_specs, out_specs=out_specs, check_vma=False
    )
```

```python
import jax
import jax.numpy as jnp
from jax import lax
from jax.experimental import pallas as pl
from jax.experimental.pallas import tpu as pltpu
from jax.sharding import PartitionSpec as P

HD = 64
EPS = 1e-05
SCALE = 0.125
NEGATIVE = -1e30
CHUNK = 64
LAG = 3
HEADS_FORWARD = 6
HEADS_BACKWARD = 3
EARLY = (
    {3: (1, 3), 4: (7, 9), 5: (14, 16)},
    {3: (3, 6), 4: (9, 13), 5: (16, 17)},
    {3: (6, 7), 4: (13, 14), 5: (17, 18)},
    {6: (18, 20)},
    {3: (0, 1)},
)
PLAN = {
    "down": ((0, 1, 2, 3, -1, -1, -1, -1), (0, 1, 2, 3, -1, -1, -1, -1)),
    "rest": ((0, -1, -1, 1, 2, 3, -1, -1), (-1, 0, 1, 2, 3, -1, -1, -1)),
    "in": ((-1, 0, -1, -1, -1, -1, 3, -1), (-1, -1, 0, 1, -1, 2, 3, -1)),
    "late": ((-1, -1, -1, -1, 1, 2, -1, -1), (-1,) * 8),
    "grads": ((-1, -1, -1, 0, 1, -1, -1, -1), (-1, -1, -1, -1, -1, -1, -1, 2)),
}
MESH = pl.DeviceIdType.MESH
F32 = jnp.float32
BF16 = jnp.bfloat16
NN = (((1,), (0,)), ((), ()))
NT = (((1,), (1,)), ((), ()))
TN = (((0,), (0,)), ((), ()))
GELU_C = 0.7978845608028654
GELU_A = 0.044715


def dot(left, right, dims=NN):
    return lax.dot_general(left, right, dims, preferred_element_type=F32)


def lane_sum(value):
    return jnp.sum(value, axis=-1, keepdims=True)


def row_sum(value):
    return jnp.sum(value, axis=0, keepdims=True)


def expanded(block):
    value = block.astype(F32)
    lane = lax.broadcasted_iota(jnp.int32, value.shape, 1)
    return jnp.where(lane == value.shape[1] - 1, -lane_sum(value), value)


def norm_factor(full):
    return lax.rsqrt(lane_sum(full * full) * (1.0 / full.shape[1]) + EPS)


def centred(value):
    return value - lane_sum(value) * (1.0 / value.shape[1])


def norm_back(grad, full, gain):
    factor = norm_factor(full)
    weighted = grad * gain
    inner = lane_sum(weighted * full) * (1.0 / full.shape[1])
    gain_grad = row_sum(grad * full * factor)
    return centred(factor * weighted - full * (factor * factor * factor * inner)), gain_grad


def make_kernel(names, count):
    def kernel(*refs):
        r = dict(zip(names, refs, strict=True))
        xin, cot, seg = r["xin"], r["cot"], r["seg"]
        act, eg, small = r["act"], r["eg"], r["small"]
        wq, wo, wud, mc = r["wq"], r["wo"], r["wud"], r["mc"]
        xbuf, cotb, resb, outt = r["xbuf"], r["cotb"], r["resb"], r["outt"]
        pool, nrm, n2t = r["pool"], r["nrm"], r["n2t"]
        qt, kt, vt, kn, vn = r["qt"], r["kt"], r["vt"], r["kn"], r["vn"]
        ctx, lse, segc = r["ctx"], r["lse"], r["segc"]
        gp, hid, gmt, gat = r["gp"], r["hid"], r["gmt"], r["gat"]
        dot_, dqkv, dk, dv = r["dot"], r["dqkv"], r["dk"], r["dv"]
        ex, xrec, cin, ready = r["ex"], r["xrec"], r["cin"], r["ready"]
        sown, soth, srec, scin, sfin = r["sown"], r["soth"], r["srec"], r["scin"], r["sfin"]
        sl, sg, sw, se, sh, so, sr, sc, ss = (
            r[name] for name in ("sl", "sg", "sw", "se", "sh", "so", "sr", "sc", "ss"))
        blocks, rows, width = xbuf.shape
        length = blocks * rows
        slots, hs = wq.shape[0], wo.shape[1] // HD
        heads = slots * hs
        part = wo.shape[1]
        units = wud.shape[1]
        chunks = xrec.shape[0]
        wu = [wud.at[pl.ds(slot * width, width)] for slot in range(slots)]
        wd = [wud.at[pl.ds((slots + slot) * width, width)] for slot in range(slots)]

        s = lax.axis_index("section")
        t = lax.axis_index("tensor")
        d = lax.axis_index("dp")
        core, xh = lax.rem(t, 2), lax.div(t, 2)
        t_core = 2 * xh + 1 - core
        t_x = 2 * (1 - xh) + core
        to_core = (s, t_core, d)
        to_x = (s, t_x, d)
        to_y = (1 - s, t, d)
        to_xy = (1 - s, t_x, d)
        parity = lax.rem(d, 2)
        to_pair = (s, t, d + 1 - 2 * parity)
        left, right = (s, t, d - 1), (s, t, d + 1)
        first_section, last_section = s == 0, s == 1

        def send(src, dst, sems, at, device):
            return pltpu.make_async_remote_copy(
                src_ref=src, dst_ref=dst, send_sem=sems.at[(0, *at)], recv_sem=sems.at[(1, *at)],
                device_id=device, device_id_type=MESH)

        def loop(stop, body):
            def step(i, carry):
                body(i)
                return carry

            lax.fori_loop(0, stop, step, 0)

        barrier = pltpu.get_barrier_semaphore()
        for device in (to_core, to_x, to_y, to_xy):
            pl.semaphore_signal(barrier, inc=1, device_id=device, device_id_type=MESH)

        @pl.when(d > 0)
        def _():
            pl.semaphore_signal(barrier, inc=1, device_id=left, device_id_type=MESH)

        @pl.when(d < count - 1)
        def _():
            pl.semaphore_signal(barrier, inc=1, device_id=right, device_id_type=MESH)

        ends = jnp.where(d > 0, 1, 0) + jnp.where(d < count - 1, 1, 0)
        pl.semaphore_wait(barrier, 4 + ends)

        def at_row(i):
            return pl.ds(pl.multiple_of(i * rows, rows), rows)

        mid_at = at_row

        def grad_at(i):
            return pl.ds(pl.multiple_of(length + i * rows, rows), rows)

        def rows_in(source, device):
            mine, other = gmt.at[:, at_row(t)], gmt.at[:, at_row(t_x)]
            return (
                pltpu.make_async_copy(source.at[xh], mine, sl.at[0]),
                send(source.at[xh], mine, sg, (1,), to_core),
                send(source.at[1 - xh], mine, sg, (0,), device),
                send(other, other, sg, (2,), to_core),
            )

        def rows_wait(copies, target):
            local, core_own, across, core_other = copies
            across.wait_recv()
            core_other.start()
            local.wait()
            core_own.wait()
            core_other.wait()

            def turn(i):
                target[i] = gmt[:, at_row(i)].astype(F32).T.astype(BF16)

            loop(blocks, turn)

        @pl.when(first_section)
        def _():
            for copy in rows_in(xin, to_xy)[:2]:
                copy.start()

        @pl.when(last_section)
        def _():
            rows_in(xin, to_xy)[2].start()

        mc[0] = jnp.zeros_like(mc[0])
        for row, name in enumerate(("attn_gain", "mlp_gain", "out_bias", "down_bias", "up_bias")):
            mc[0, row : row + 1, :] = r[name][...].astype(F32)
        for row in range(2):
            mc[0, 5 + row : 6 + row, : wo.shape[1]] = r["qv_bias"][0, row : row + 1, :].astype(F32)
        misc_x = send(mc.at[0], mc.at[1], sg, (3,), to_x)
        misc_x.start()
        locals_, pieces = [], []
        for which, (name, target, cuts) in enumerate((("wqh", [wq.at[0], wq.at[1]], 2), ("woh", [wo.at[0], wo.at[1]], 1), ("wuh", wu, 2), ("wdh", wd, 4))):
            source = r[name]
            locals_.append(pltpu.make_async_copy(source, target[0], sl.at[4 + which]))
            half = source.shape[0] // 2
            step = half // cuts
            group = []
            for cut in range(cuts):
                at = pl.ds(pl.multiple_of(parity * half + cut * step, 16), step)
                place = 4 * which + cut
                group.append((
                    send(source.at[at], target[1].at[at], sw, (0, place), to_x),
                    send(target[1].at[at], target[1].at[at], sw, (1, place), to_pair),
                ))
            pieces.append(group)
        for which, (local, group) in enumerate(zip(locals_, pieces, strict=True)):
            if which == 3:

                @pl.when(last_section)
                def _():
                    for copy in rows_in(cot, to_x)[:3]:
                        copy.start()

            local.start()
            for across, _ in group:
                across.start()

        def pass_on(which, *cuts):
            for cut in cuts:
                across, pair = pieces[which][cut]
                across.wait_recv()
                pair.start()

        def have(which):
            locals_[which].wait()
            for across, pair in pieces[which]:
                across.wait_send()
                pair.wait()

        sown[...] = jnp.zeros_like(sown)
        soth[...] = jnp.zeros_like(soth)
        segment = seg[xh]
        segc[...] = jnp.broadcast_to(segment.astype(F32), (128, length)).T

        def ex_at(kind, i):
            return pl.ds(pl.multiple_of(kind * length + i * rows, rows), rows)

        def shifted(i):
            return lax.rem(i + 1, blocks)

        def pair_copy(kind, i):
            return send(ex.at[ex_at(2 * kind, i)], ex.at[ex_at(2 * kind + 1, i)], se, (kind, i), to_core)

        def pair_send(kind, i, value):
            ex[ex_at(2 * kind, i), :] = value.astype(BF16)
            pair_copy(kind, i).start()

        def pair_sum(kind, i):
            pair_copy(kind, i).wait()
            return ex[ex_at(2 * kind, i), :].astype(F32) + ex[ex_at(2 * kind + 1, i), :].astype(F32)

        half_rows = rows // 2
        own_half = pl.ds(pl.multiple_of(core * half_rows, half_rows), half_rows)

        def hop_copy(i, target):
            return send(resb.at[lax.rem(i, 2), own_half], target.at[i, own_half], sh, (0, i), to_y)

        def hop_core(i, target):
            return send(target.at[i, own_half], target.at[i, own_half], sh, (1, i), to_core)

        pass_on(0, 0, 1)

        @pl.when(first_section)
        def _():
            rows_wait(rows_in(xin, to_xy), xbuf)
            pass_on(1, 0)

        @pl.when(last_section)
        def _():
            pass_on(1, 0)
            pass_on(2, 0, 1)
            copies = rows_in(cot, to_x)
            rows_wait(copies, cotb)
            pass_on(3, 0, 1, 2, 3)
            copies[2].wait_send()
            rows_in(xin, to_xy)[2].wait_send()

        misc_x.wait()
        attn_gain, mlp_gain, out_bias, down_bias = (mc[0, i : i + 1, :] for i in range(4))
        have(0)

        def allowed(i, j0, j1, diagonal):
            same = segc[j0:j1, :]
            same = jnp.concatenate([same] * (rows // same.shape[1]), axis=1)
            cols = slice(i * rows, (i + 1) * rows)
            keep = same == seg[xh, :, cols].astype(F32)
            if diagonal:
                key = lax.broadcasted_iota(jnp.int32, keep.shape, 0)
                query = lax.broadcasted_iota(jnp.int32, keep.shape, 1)
                keep = keep & (key <= query)
            return keep

        def masked(scores, i, j0, j1, diagonal):
            return jnp.where(allowed(i, j0, j1, diagonal), scores, NEGATIVE)

        def key_parts(i):
            parts = [(i * rows, (i + 1) * rows, True)]
            if i > 0:
                parts.append((0, i * rows, False))
            return parts

        def project(i):
            full = expanded(xbuf[i])
            normed = (full * norm_factor(full) * attn_gain).astype(BF16)
            nrm[i] = normed
            cols = at_row(i)
            for slot in range(slots):
                three = dot(wq[slot], normed, NT)
                bias = mc[slot, :, :part].T
                query = (three[:part] + bias[:, 5:6]).astype(BF16) * SCALE
                key = three[part : 2 * part]
                value = (three[2 * part :] + bias[:, 6:7]).astype(BF16).astype(F32)
                for h in range(hs):
                    at = slice(h * HD, (h + 1) * HD)
                    head = slot * hs + h
                    qt[i, head] = query[at].astype(BF16)
                    kt[head, :, cols] = key[at].astype(BF16)
                    vt[head, :, cols] = value[at].astype(BF16)
                    kn[head, cols, :] = key[at].T.astype(BF16)
                    vn[head, cols, :] = value[at].T.astype(BF16)

        def attend(i, group):
            cols = slice(i * rows, (i + 1) * rows)
            parts = key_parts(i)
            scores = [[masked(dot(kn[h, a:b], qt[i, h]), i, a, b, g) for a, b, g in parts] for h in group]
            tops = []
            for score in scores:
                top = score[0].max(axis=0, keepdims=True)
                for more in score[1:]:
                    top = jnp.maximum(top, more.max(axis=0, keepdims=True))
                tops.append(top)
            powers = [[jnp.exp(one - top) for one in score] for score, top in zip(scores, tops, strict=True)]
            totals = [sum(row_sum(one) for one in power) for power in powers]
            contexts = [
                sum(dot(vt[h, :, a:b], one.astype(BF16)) for one, (a, b, _) in zip(power, parts, strict=True))
                for h, power in zip(group, powers, strict=True)
            ]
            for h, top, total, context in zip(group, tops, totals, contexts, strict=True):
                ctx[h, :, cols] = (context / total).astype(BF16)
                lse[i, h] = top + jnp.log(total)

        def each_block(i, body, number):
            for block in range(blocks):

                @pl.when(i == block)
                def _():
                    loop(heads // number, lambda n: body(block, [n * number + k for k in range(number)]))

        def attention_rows(i):
            @pl.when(last_section & (i == 0))
            def _():
                hop_copy(0, xbuf).wait_recv()
                hop_core(0, xbuf).start()

            @pl.when(last_section)
            def _():
                hop_core(i, xbuf).wait()

            project(i)
            each_block(i, attend, HEADS_FORWARD)

            @pl.when(i == 0)
            def _():
                have(1)

            context = ctx[:, :, at_row(i)].reshape(heads * HD, rows)
            pair_send(0, shifted(i), dot(context, wo[...].reshape(heads * HD, width), TN))

            for step, (which, cut) in enumerate(((2, 0), (2, 1), (3, 0), (3, 1))):

                @pl.when((i == step) & first_section)
                def _():
                    pass_on(which, cut)

            @pl.when(last_section & (i < blocks - 1))
            def _():
                hop_copy(i + 1, xbuf).wait_recv()
                hop_core(i + 1, xbuf).start()

        def up_rows(i):
            @pl.when(i == 0)
            def _():
                have(2)

            branch = pair_sum(0, shifted(i)) + out_bias
            middle = expanded(xbuf[i]) + centred(branch)
            pool[mid_at(i), :] = middle
            normed = middle * norm_factor(middle) * mlp_gain
            normed = normed.astype(BF16)
            for slot in range(slots):
                pre = dot(normed, wu[slot][...]) + mc[slot, 4:5, :]
                square = pre * pre
                bend = jnp.tanh(pre * (GELU_C + (GELU_C * GELU_A) * square))
                grow = 0.5 + 0.5 * bend
                value = pre * grow
                hid[slot, i] = value.astype(BF16)
                slope = GELU_C + (3.0 * GELU_C * GELU_A) * square
                gp[slot, i] = (grow + value * (1.0 - bend) * slope).astype(BF16)

            for step, cut in ((0, 2), (1, 3)):

                @pl.when((i == step) & first_section)
                def _():
                    pass_on(3, cut)

        def down_rows(i):
            @pl.when(i == 0)
            def _():
                have(3)

            branch = dot(hid[0, i], wd[0][...], NT)
            for slot in range(1, slots):
                branch = branch + dot(hid[slot, i], wd[slot][...], NT)
            pair_send(1, shifted(i), branch)

        def keep_out(i, value):
            @pl.when((i == t) | (i == t_x))
            def _():
                outt[jnp.where(i == t, 0, 1)] = value.T.astype(BF16)

        def result_rows(i):
            result = pool[mid_at(i), :] + centred(pair_sum(1, shifted(i)) + down_bias)
            keep_out(i, result)

            @pl.when(first_section)
            def _():
                @pl.when(i >= 2)
                def _():
                    hop_copy(i - 2, xbuf).wait_send()

                lane = lax.broadcasted_iota(jnp.int32, result.shape, 1)
                resb[lax.rem(i, 2)] = jnp.where(lane == width - 1, 0.0, result).astype(BF16)
                hop_copy(i, xbuf).start()

        def forward(step):
            i_up = jnp.where(first_section, step - blocks, step - 1)
            i_down = jnp.where(first_section, step - 2 * blocks, step - 1)
            i_res = i_down - 1
            some_res = (i_res >= 0) & (i_res < blocks)

            @pl.when(step < blocks)
            def _():
                attention_rows(step)

            @pl.when(last_section & some_res & (i_res < blocks - 1))
            def _():
                result_rows(i_res)

            @pl.when((i_up >= 0) & (i_up < blocks))
            def _():
                up_rows(i_up)

            @pl.when((i_down >= 0) & (i_down < blocks))
            def _():
                down_rows(i_down)

            @pl.when(first_section & some_res)
            def _():
                result_rows(i_res)

        loop(3 * blocks + 1, forward)

        def rows_out(target, which):
            return (
                pltpu.make_async_copy(outt.at[0], target.at[xh], sl.at[2]),
                send(outt.at[1], target.at[xh], so, (which,), to_x),
            )

        act_copies = rows_out(act, 0)

        @pl.when(first_section)
        def _():
            loop(2, lambda i: hop_copy(blocks - 2 + i, xbuf).wait_send())

        def other_at(k):
            row = k * CHUNK
            third = jnp.where(row < 3 * rows, 0, jnp.where(row < 6 * rows, 1, 2))
            place = row - third * 3 * rows
            kind = jnp.where(place < rows, 0, jnp.where(place < 2 * rows, 1, 2))
            row = kind * (length - rows) + (blocks - 1 - third) * rows + place
            return pl.ds(pl.multiple_of(row, CHUNK), CHUNK)

        def own_at(k):
            row = k * CHUNK
            third = jnp.where(row < 3 * rows, 0, jnp.where(row < 6 * rows, 1, 2))
            place = row - third * 3 * rows
            down = jnp.where(place < rows, place + 3 * rows, place + 6 * rows)
            up = jnp.where(place < 2 * rows, place + rows, place + 4 * rows)
            rest = jnp.where(place < rows, place, place + 3 * rows)
            row = jnp.where(third == 0, down, jnp.where(third == 1, up, rest))
            return pl.ds(pl.multiple_of(row, CHUNK), CHUNK)

        def x_copy(k):
            return send(ex.at[other_at(k)], xrec.at[k], sr, (k,), to_x)

        def put(turn, first, value):
            @pl.when(turn == 0)
            def _():
                for k in range(value.shape[0] // CHUNK):
                    ex[other_at(first + k), :] = value[k * CHUNK : (k + 1) * CHUNK].astype(BF16)

            @pl.when(turn == 1)
            def _():
                for k in range(value.shape[0] // CHUNK):
                    pool[own_at(first + k), :] = value[k * CHUNK : (k + 1) * CHUNK]

        def start(turn, first, number):
            @pl.when(turn == 0)
            def _():
                loop(number, lambda k: x_copy(first + k).start())

        tile = 256
        tiles = width // tile

        def down_part(turn, k):
            at = pl.ds(pl.multiple_of(k * tile, tile), tile)
            first = k * (tile // CHUNK)
            put(turn, first, dot(gmt[at, :], hid[1 - turn].reshape(length, units)))
            start(turn, first, tile // CHUNK)

        def up_part(turn, k):
            at = pl.ds(pl.multiple_of(k * tile, tile), tile)
            first = width // CHUNK + k * (tile // CHUNK)
            put(turn, first, dot(n2t[at, :], gp[1 - turn].reshape(length, units)))
            start(turn, first, tile // CHUNK)

        def turn_normed(i):
            middle = pool[mid_at(i), :]
            n2t[:, at_row(i)] = (middle * norm_factor(middle) * mlp_gain).T.astype(BF16)

        def down_grads(turn):
            loop(tiles, lambda k: down_part(turn, k))

        def up_grads(turn):
            loop(tiles, lambda k: up_part(turn, k))

        middle = count // 2
        on_left = d < middle
        depth = jnp.where(on_left, d, count - 1 - d)
        has_outer = depth > 0
        is_mid = depth == middle - 1
        inner = (s, t, jnp.where(on_left, d + 1, d - 1))
        outer = (s, t, jnp.where(on_left, d - 1, d + 1))
        lag_in = LAG * depth
        lag_mid = LAG * middle
        lag_out = lag_mid + LAG * (middle - 1 - depth)
        lag_all = lag_mid + LAG * (middle - 1)

        def fin_at(k):
            return pl.ds(pl.multiple_of(k * CHUNK, CHUNK), CHUNK)

        def in_copy(k):
            return send(xrec.at[k], cin.at[k], sc, (0, k), inner)

        def cross_copy(k):
            return send(xrec.at[k], wud.at[fin_at(k)], sc, (1, k), inner)

        def out_copy(k):
            return send(wud.at[fin_at(k)], wud.at[fin_at(k)], sc, (2, k), outer)

        outs, place = [], 0
        for which, name in enumerate(("down", "up", "qkv", "out")):
            number = r[name].shape[0]
            copy = pltpu.make_async_copy(wud.at[pl.ds(place, number)], r[name], so.at[0, 2 + which])
            place += number
            outs.append((place // CHUNK - 1, copy))

        def matrix_out(k):
            for final, copy in outs:

                @pl.when(k == final)
                def _():
                    copy.start()

        small_x = send(soth, srec, ss, (0,), to_x)
        s_in = send(sown, scin, ss, (1,), inner)
        s_cross = send(sown, sfin, ss, (2,), inner)
        s_out = send(sfin, sfin, ss, (3,), outer)

        def reduce_small(it):
            begin = chunks - 4

            @pl.when(it == begin)
            def _():
                small_x.wait()
                sown[...] = sown[...] + srec[...]

            @pl.when(it == begin + lag_in)
            def _():
                @pl.when(has_outer)
                def _():
                    s_in.wait_recv()
                    sown[...] = sown[...] + scin[...]

                @pl.when(jnp.logical_not(is_mid))
                def _():
                    s_in.start()

                @pl.when(is_mid)
                def _():
                    s_cross.start()

            @pl.when(it == begin + lag_out)
            def _():
                @pl.when(is_mid)
                def _():
                    s_cross.wait()
                    sfin[...] = sfin[...] + sown[...]

                @pl.when(jnp.logical_not(is_mid))
                def _():
                    s_out.wait_recv()

                @pl.when(has_outer)
                def _():
                    s_out.start()

        def reduce(it):
            @pl.when((it == 0) & is_mid)
            def _():
                pl.semaphore_signal(ready, inc=1, device_id=inner, device_id_type=MESH)

            @pl.when(it < chunks)
            def _():
                k = it
                x_copy(k).wait()
                xrec[k] = (pool[own_at(k), :] + xrec[k].astype(F32)).astype(BF16)

            k_in = it - lag_in

            @pl.when((k_in >= 0) & (k_in < chunks))
            def _():
                k = k_in

                @pl.when(has_outer)
                def _():
                    in_copy(k).wait_recv()
                    xrec[k] = (xrec[k].astype(F32) + cin[k].astype(F32)).astype(BF16)

                @pl.when(jnp.logical_not(is_mid))
                def _():
                    in_copy(k).start()

                @pl.when(is_mid)
                def _():
                    @pl.when(k == 0)
                    def _():
                        pl.semaphore_wait(ready, 1)

                    cross_copy(k).start()

            k_out = it - lag_out

            @pl.when((k_out >= 0) & (k_out < chunks))
            def _():
                k = k_out

                @pl.when(is_mid)
                def _():
                    cross_copy(k).wait_recv()
                    wud[fin_at(k), :] = (xrec[k].astype(F32) + wud[fin_at(k), :].astype(F32)).astype(BF16)

                @pl.when(jnp.logical_not(is_mid))
                def _():
                    out_copy(k).wait_recv()

                @pl.when(has_outer)
                def _():
                    out_copy(k).start()

                matrix_out(k)

            reduce_small(it)

        def grad_rows(i):
            @pl.when(first_section)
            def _():
                hop_copy(i, cotb).wait_recv()
                hop_core(i, cotb).start()
                hop_core(i, cotb).wait()
                turn_grad(i)

        def turn_grad(i):
            gmt[:, at_row(i)] = centred(cotb[i].astype(F32)).T.astype(BF16)

        def down_back(i):
            grad = centred(cotb[i].astype(F32))
            pool[grad_at(i), :] = grad
            grad = grad.astype(BF16)
            sown[3:4, :] += row_sum(grad.astype(F32))
            branch = 0.0
            for slot, sums in ((0, sown), (1, soth)):
                before = (dot(grad, wd[slot][...]) * gp[slot, i].astype(F32)).astype(BF16)
                gp[slot, i] = before
                sums[4:5, :] += row_sum(before.astype(F32))
                branch = branch + dot(before, wu[slot][...], NT)
            pair_send(0, i, branch)

        def out_back(i):
            grad, gain_grad = norm_back(pair_sum(0, i), pool[mid_at(i), :], mlp_gain)
            sown[2:3, :] += gain_grad
            grad = grad + pool[grad_at(i), :]
            pool[grad_at(i), :] = grad
            grad = grad.astype(BF16)
            gat[i] = grad
            sown[1:2, :] += row_sum(grad.astype(F32))
            back = dot(wo[...].reshape(heads * HD, width), grad, NT).astype(BF16)
            for h in range(heads):
                dot_[i, h] = back[h * HD : (h + 1) * HD]

        def attend_back(i, group):
            parts = key_parts(i)
            cols = slice(i * rows, (i + 1) * rows)
            masks = [jnp.where(allowed(i, a, b, g), 0.0, NEGATIVE) for a, b, g in parts]
            probs, g_probs = [], []
            for h in group:
                less = [mask - lse[i, h] for mask in masks]
                probs.append([jnp.exp(dot(kn[h, a:b], qt[i, h]) + one) for one, (a, b, _) in zip(less, parts, strict=True)])
                g_probs.append([dot(vn[h, a:b], dot_[i, h]) for a, b, _ in parts])
            centres = [
                sum(row_sum(x * y) for x, y in zip(prob, g_prob, strict=True))
                for prob, g_prob in zip(probs, g_probs, strict=True)
            ]
            g_scores = [
                [(x * (y - centre)).astype(BF16) for x, y in zip(prob, g_prob, strict=True)]
                for prob, g_prob, centre in zip(probs, g_probs, centres, strict=True)
            ]
            g_values = [[dot(dot_[i, h], x.astype(BF16), NT) for x in prob] for h, prob in zip(group, probs, strict=True)]
            g_keys = [[dot(qt[i, h], x, NT) for x in g_score] for h, g_score in zip(group, g_scores, strict=True)]
            g_queries = [
                sum(dot(kt[h, :, a:b], x) for x, (a, b, _) in zip(g_score, parts, strict=True))
                for h, g_score in zip(group, g_scores, strict=True)
            ]
            for h, g_value, g_key, g_query in zip(group, g_values, g_keys, g_queries, strict=True):
                slot, place = lax.div(h, hs), lax.rem(h, hs)
                for (a, b, _), value, key in zip(parts, g_value, g_key, strict=True):
                    if i == blocks - 1:
                        dv[h, :, a:b] = value
                        dk[h, :, a:b] = key
                    else:
                        dv[h, :, a:b] += value
                        dk[h, :, a:b] += key
                dqkv[slot, 0, place, :, cols] = (g_query * SCALE).astype(BF16)
                dqkv[slot, 1, place, :, cols] = dk[h, :, cols].astype(BF16)
                dqkv[slot, 2, place, :, cols] = dv[h, :, cols].astype(BF16)

        def qkv_back(i):
            branch = 0.0
            for slot in range(slots):
                three = dqkv[slot, :, :, :, at_row(i)].reshape(3 * part, rows)
                branch = branch + dot(three, wq[slot], TN)
            pair_send(1, i, branch)

        def in_back(i):
            grad, gain_grad = norm_back(pair_sum(1, i), expanded(xbuf[i]), attn_gain)
            sown[0:1, :] += gain_grad
            grad = grad + pool[grad_at(i), :]
            grad = grad - grad[:, width - 1 :]
            keep_out(i, grad)

            @pl.when(last_section)
            def _():
                @pl.when(i < blocks - 2)
                def _():
                    hop_copy(i + 2, cotb).wait_send()

                resb[lax.rem(i, 2)] = grad.astype(BF16)
                hop_copy(i, cotb).start()

        def advance(step, place):
            def body(it, carry):
                reduce(it)
                return carry

            first, stop = 0, 0
            for at, (lo, hi) in EARLY[place].items():
                first = jnp.where(first_section & (step == at), lo, first)
                stop = jnp.where(first_section & (step == at), hi, stop)
            lax.fori_loop(first, stop, body, 0)

        def planned(step, name):
            found = -1
            for at, (first, last) in enumerate(zip(*PLAN[name], strict=True)):
                found = jnp.where(step == at, jnp.where(first_section, first, last), found)
            return found

        def turns(first, stop, body):
            def one(turn, carry):
                body(turn)
                return carry

            lax.fori_loop(first, stop, one, 0)

        def backward(step):
            n_down, n_in, n_rest, n_late = (planned(step, name) for name in ("down", "in", "rest", "late"))
            n_grad = planned(step, "grads")
            last = blocks - 1
            advance(step, 3)

            @pl.when(step == jnp.where(first_section, blocks - 2, 2 * blocks - 1))
            def _():
                loop(blocks, turn_normed)

            @pl.when(last_section & (step == 2 * blocks - 1))
            def _():
                loop(blocks, turn_grad)

            @pl.when(n_down >= 0)
            def _():
                grad_rows(last - n_down)

            early = jnp.where(n_grad == 0, 1, 0)
            turns(0, early, down_grads)

            @pl.when(n_down >= 0)
            def _():
                down_back(last - n_down)

            @pl.when(step == 0)
            def _():
                @pl.when(last_section)
                def _():
                    result_rows(last)

                for copy in act_copies:
                    copy.start()

            @pl.when((n_grad == 0) | (n_grad == 2))
            def _():
                turns(early, 2, down_grads)
                advance(step, 4)

            @pl.when(n_in == 0)
            def _():
                for copy in act_copies:
                    copy.wait()

            @pl.when(n_in >= 0)
            def _():
                in_back(last - n_in)

            @pl.when(n_rest >= 0)
            def _():
                i = last - n_rest
                out_back(i)
                advance(step, 0)

                @pl.when(n_late >= 0)
                def _():
                    in_back(last - n_late)

                @pl.when(n_grad == 1)
                def _():
                    loop(2, up_grads)

                each_block(i, attend_back, HEADS_BACKWARD)
                advance(step, 1)
                qkv_back(i)
                advance(step, 2)

            @pl.when(n_grad == 2)
            def _():
                loop(2, up_grads)

        loop(len(PLAN["in"][0]), backward)
        ones = jnp.ones((8, length), BF16)
        sown[5:6, : 3 * part] = dot(ones, dqkv[0].reshape(3 * part, length), NT)[0:1]
        soth[5:6, : 3 * part] = dot(ones, dqkv[1].reshape(3 * part, length), NT)[0:1]
        soth[0:4, :] = sown[0:4, :]
        small_x.start()

        def attention_grads(turn):
            slot = 1 - turn

            def qkv_part(k):
                first = (2 * width) // CHUNK + k * (part // CHUNK)
                put(turn, first, dot(dqkv[slot, k].reshape(part, length), nrm[...].reshape(length, width)))

            loop(3, qkv_part)
            first = (2 * width + 3 * part) // CHUNK
            context = ctx[pl.ds(slot * hs, hs)].reshape(part, length)
            put(turn, first, dot(context, gat[...].reshape(length, width)))
            start(turn, 2 * (width // CHUNK), chunks - 2 * (width // CHUNK))

        loop(2, attention_grads)
        eg_copies = rows_out(eg, 1)
        for copy in eg_copies:
            copy.start()

        def rest(it, carry):
            reduce(it)
            return carry

        begun = max(hi for place in EARLY for _, hi in place.values())
        lax.fori_loop(jnp.where(first_section, begun, 0), chunks + lag_all, rest, 0)
        small[...] = sfin[...]

        @pl.when(jnp.logical_not(is_mid))
        def _():
            s_in.wait_send()

        @pl.when(has_outer)
        def _():
            s_out.wait_send()

        def drain(k):
            @pl.when(jnp.logical_not(is_mid))
            def _():
                in_copy(k).wait_send()

            @pl.when(is_mid)
            def _():
                cross_copy(k).wait_send()

            @pl.when(has_outer)
            def _():
                out_copy(k).wait_send()

        loop(chunks, drain)
        for _, copy in outs:
            copy.wait()

        @pl.when(last_section)
        def _():
            loop(2, lambda i: hop_copy(i, cotb).wait_send())

        for copy in eg_copies:
            copy.wait()

    return kernel


def per_device(
    block_input,
    segments,
    cotangent,
    attn_gain,
    qkv_weight,
    qv_bias,
    out_weight,
    out_bias,
    mlp_gain,
    up_projection_weight,
    up_bias,
    down_projection_weight,
    down_bias,
):
    micros, rows, _, kept = block_input.shape
    width = qkv_weight.shape[1]
    part = qkv_weight.shape[3]
    units = up_projection_weight.shape[2]
    blocks = lax.axis_size("tensor")
    count = lax.axis_size("dp")
    length = blocks * rows
    slots = 2
    hs = part // HD
    heads = slots * hs
    chunks = (2 * width + 4 * part) // CHUNK

    def features_first(array):
        first = array[:, :, 0, :].transpose(2, 0, 1)
        return jnp.pad(first, ((0, width - kept), (0, 0), (0, 0))).transpose(1, 0, 2)

    inputs = {
        "xin": features_first(block_input),
        "cot": features_first(cotangent),
        "wqh": qkv_weight[0].transpose(1, 2, 0).reshape(3 * part, width),
        "woh": out_weight[0],
        "wuh": up_projection_weight[0],
        "wdh": down_projection_weight[0],
        "attn_gain": attn_gain,
        "mlp_gain": mlp_gain,
        "out_bias": out_bias,
        "down_bias": down_bias,
        "up_bias": up_bias,
        "qv_bias": qv_bias,
        "seg": segments,
    }
    outputs = {
        "act": ((micros, width, rows), BF16),
        "eg": ((micros, width, rows), BF16),
        "down": ((width, units), BF16),
        "up": ((width, units), BF16),
        "qkv": ((3 * part, width), BF16),
        "out": ((part, width), BF16),
        "small": ((8, width), F32),
    }
    scratch = {
        "wq": ((slots, 3 * part, width), BF16),
        "wo": ((slots, part, width), BF16),
        "wud": ((2 * slots * width, units), BF16),
        "mc": ((slots, 8, width), F32),
        "xbuf": ((blocks, rows, width), BF16),
        "cotb": ((blocks, rows, width), BF16),
        "resb": ((2, rows, width), BF16),
        "outt": ((2, width, rows), BF16),
        "pool": ((max(2 * length, chunks * CHUNK), width), F32),
        "nrm": ((blocks, rows, width), BF16),
        "n2t": ((width, length), BF16),
        "qt": ((blocks, heads, HD, rows), BF16),
        "kt": ((heads, HD, length), BF16),
        "vt": ((heads, HD, length), BF16),
        "kn": ((heads, length, HD), BF16),
        "vn": ((heads, length, HD), BF16),
        "ctx": ((heads, HD, length), BF16),
        "lse": ((blocks, heads, 1, rows), F32),
        "segc": ((length, 128), F32),
        "gp": ((slots, blocks, rows, units), BF16),
        "hid": ((slots, blocks, rows, units), BF16),
        "gmt": ((width, length), BF16),
        "gat": ((blocks, rows, width), BF16),
        "dot": ((blocks, heads, HD, rows), BF16),
        "dqkv": ((slots, 3, hs, HD, length), BF16),
        "dk": ((heads, HD, length), F32),
        "dv": ((heads, HD, length), F32),
        "ex": ((4 * length, width), BF16),
        "xrec": ((chunks, CHUNK, width), BF16),
        "cin": ((chunks, CHUNK, width), BF16),
        "sown": ((8, width), F32),
        "soth": ((8, width), F32),
        "srec": ((8, width), F32),
        "scin": ((8, width), F32),
        "sfin": ((8, width), F32),
    }
    dma = pltpu.SemaphoreType.DMA
    semaphores = {
        "sl": dma((8,)),
        "sg": dma((2, 4)),
        "sw": dma((2, 2, 16)),
        "se": dma((2, 2, blocks)),
        "sh": dma((2, 2, blocks)),
        "so": dma((2, 6)),
        "sr": dma((2, chunks)),
        "sc": dma((2, 3, chunks)),
        "ss": dma((2, 4)),
        "ready": pltpu.SemaphoreType.REGULAR,
    }
    in_vmem = {"attn_gain", "mlp_gain", "out_bias", "down_bias", "up_bias", "qv_bias", "seg", "small"}

    def spec(name):
        return pl.BlockSpec(memory_space=pltpu.VMEM if name in in_vmem else pl.ANY)

    names = [*inputs, *outputs, *scratch, *semaphores]
    act, eg, down, up, qkv, out, small = pl.pallas_call(
        make_kernel(names, count),
        out_shape=[jax.ShapeDtypeStruct(*item) for item in outputs.values()],
        in_specs=[spec(name) for name in inputs],
        out_specs=[spec(name) for name in outputs],
        scratch_shapes=[pltpu.VMEM(*item) for item in scratch.values()] + list(semaphores.values()),
        compiler_params=pltpu.CompilerParams(
            collective_id=0, has_side_effects=True, vmem_limit_bytes=63 * 1024 * 1024
        ),
        name="layers",
    )(*inputs.values())

    def positions_first(array):
        return array[:, :kept, :].transpose(0, 2, 1)[None, :, :, None, :]

    qv = small[5, : 3 * part].reshape(3, part)
    return (
        positions_first(act),
        positions_first(eg).astype(F32),
        small[0:1],
        qkv.reshape(3, part, width).transpose(2, 0, 1).astype(F32)[None],
        qv[0::2][None],
        out.astype(F32)[None],
        small[1:2],
        small[2:3],
        up.astype(F32)[None],
        small[4:5, :units],
        down.astype(F32)[None],
        small[3:4],
    )


def solution(mesh):
    in_specs = (
        P(None, "tensor", "dp", None),
        P(None, "dp", None),
        P(None, "tensor", "dp", None),
        P("section", None),
        P("section", None, None, "tensor"),
        P("section", None, "tensor"),
        P("section", "tensor", None),
        P("section", None),
        P("section", None),
        P("section", None, "tensor"),
        P("section", "tensor"),
        P("section", None, "tensor"),
        P("section", None),
    )
    out_specs = (
        P("section", None, "tensor", "dp", None),
        P("section", None, "tensor", "dp", None),
        P("section", None),
        P("section", None, None, "tensor"),
        P("section", None, "tensor"),
        P("section", "tensor", None),
        P("section", None),
        P("section", None),
        P("section", None, "tensor"),
        P("section", "tensor"),
        P("section", None, "tensor"),
        P("section", None),
    )
    return jax.shard_map(
        per_device, mesh=mesh, in_specs=in_specs, out_specs=out_specs, check_vma=False
    )
```

```python
import jax
import jax.numpy as jnp
from jax import lax
from jax.experimental import pallas as pl
from jax.experimental.pallas import tpu as pltpu
from jax.sharding import PartitionSpec as P

HD = 64
EPS = 1e-05
SCALE = 0.125
NEGATIVE = -1e30
CHUNK = 64
LAG = 3
HEADS_FORWARD = 6
HEADS_BACKWARD = 3
EARLY = (
    {3: (1, 4), 4: (8, 10), 5: (16, 18)},
    {3: (4, 7), 4: (10, 15), 5: (18, 19)},
    {3: (7, 8), 4: (15, 16), 5: (19, 20)},
    {6: (20, 23)},
    {3: (0, 1)},
)
PLAN = {
    "down": ((0, 1, 2, 3, -1, -1, -1, -1), (0, 1, 2, 3, -1, -1, -1, -1)),
    "rest": ((0, -1, -1, 1, 2, 3, -1, -1), (-1, 0, 1, 2, 3, -1, -1, -1)),
    "in": ((-1, 0, -1, -1, -1, -1, 3, -1), (-1, -1, 0, 1, -1, 2, 3, -1)),
    "late": ((-1, -1, -1, -1, 1, 2, -1, -1), (-1,) * 8),
    "grads": ((-1, -1, -1, 0, 1, -1, -1, -1), (-1, -1, -1, -1, -1, -1, -1, 2)),
}
MESH = pl.DeviceIdType.MESH
F32 = jnp.float32
BF16 = jnp.bfloat16
NN = (((1,), (0,)), ((), ()))
NT = (((1,), (1,)), ((), ()))
TN = (((0,), (0,)), ((), ()))
GELU_C = 0.7978845608028654
GELU_A = 0.044715


def dot(left, right, dims=NN):
    return lax.dot_general(left, right, dims, preferred_element_type=F32)


def lane_sum(value):
    return jnp.sum(value, axis=-1, keepdims=True)


def row_sum(value):
    return jnp.sum(value, axis=0, keepdims=True)


def expanded(block):
    value = block.astype(F32)
    lane = lax.broadcasted_iota(jnp.int32, value.shape, 1)
    return jnp.where(lane == value.shape[1] - 1, -lane_sum(value), value)


def norm_factor(full):
    return lax.rsqrt(lane_sum(full * full) * (1.0 / full.shape[1]) + EPS)


def centred(value):
    return value - lane_sum(value) * (1.0 / value.shape[1])


def norm_back(grad, full, gain):
    factor = norm_factor(full)
    weighted = grad * gain
    inner = lane_sum(weighted * full) * (1.0 / full.shape[1])
    gain_grad = row_sum(grad * full * factor)
    return centred(factor * weighted - full * (factor * factor * factor * inner)), gain_grad


def make_kernel(names, count):
    def kernel(*refs):
        r = dict(zip(names, refs, strict=True))
        xin, cot, seg = r["xin"], r["cot"], r["seg"]
        act, eg, small = r["act"], r["eg"], r["small"]
        wq, wo, wud, mc = r["wq"], r["wo"], r["wud"], r["mc"]
        xbuf, cotb, resb, outt = r["xbuf"], r["cotb"], r["resb"], r["outt"]
        pool, nrm, n2t = r["pool"], r["nrm"], r["n2t"]
        qt, kt, vt, kn, vn = r["qt"], r["kt"], r["vt"], r["kn"], r["vn"]
        ctx, lse, segc = r["ctx"], r["lse"], r["segc"]
        gp, hid, gmt, gat = r["gp"], r["hid"], r["gmt"], r["gat"]
        dot_, dqkv, dk, dv = r["dot"], r["dqkv"], r["dk"], r["dv"]
        ex, xrec, cin, ready = r["ex"], r["xrec"], r["cin"], r["ready"]
        sown, soth, srec, scin, sfin = r["sown"], r["soth"], r["srec"], r["scin"], r["sfin"]
        sl, sg, sw, se, sh, so, sr, sc, ss = (
            r[name] for name in ("sl", "sg", "sw", "se", "sh", "so", "sr", "sc", "ss"))
        blocks, rows, width = xbuf.shape
        length = blocks * rows
        slots, hs = wq.shape[0], wo.shape[1] // HD
        heads = slots * hs
        part = wo.shape[1]
        units = wud.shape[1]
        chunks = xrec.shape[0]
        wu = [wud.at[pl.ds(slot * width, width)] for slot in range(slots)]
        wd = [wud.at[pl.ds((slots + slot) * width, width)] for slot in range(slots)]

        s = lax.axis_index("section")
        t = lax.axis_index("tensor")
        d = lax.axis_index("dp")
        core, xh = lax.rem(t, 2), lax.div(t, 2)
        t_core = 2 * xh + 1 - core
        t_x = 2 * (1 - xh) + core
        to_core = (s, t_core, d)
        to_x = (s, t_x, d)
        to_y = (1 - s, t, d)
        to_xy = (1 - s, t_x, d)
        parity = lax.rem(d, 2)
        to_pair = (s, t, d + 1 - 2 * parity)
        left, right = (s, t, d - 1), (s, t, d + 1)
        first_section, last_section = s == 0, s == 1

        def send(src, dst, sems, at, device):
            return pltpu.make_async_remote_copy(
                src_ref=src, dst_ref=dst, send_sem=sems.at[(0, *at)], recv_sem=sems.at[(1, *at)],
                device_id=device, device_id_type=MESH)

        def loop(stop, body):
            def step(i, carry):
                body(i)
                return carry

            lax.fori_loop(0, stop, step, 0)

        barrier = pltpu.get_barrier_semaphore()
        for device in (to_core, to_x, to_y, to_xy):
            pl.semaphore_signal(barrier, inc=1, device_id=device, device_id_type=MESH)

        @pl.when(d > 0)
        def _():
            pl.semaphore_signal(barrier, inc=1, device_id=left, device_id_type=MESH)

        @pl.when(d < count - 1)
        def _():
            pl.semaphore_signal(barrier, inc=1, device_id=right, device_id_type=MESH)

        ends = jnp.where(d > 0, 1, 0) + jnp.where(d < count - 1, 1, 0)
        pl.semaphore_wait(barrier, 4 + ends)

        def at_row(i):
            return pl.ds(pl.multiple_of(i * rows, rows), rows)

        mid_at = at_row

        def grad_at(i):
            return pl.ds(pl.multiple_of(length + i * rows, rows), rows)

        def rows_in(source, device):
            mine, other = gmt.at[:, at_row(t)], gmt.at[:, at_row(t_x)]
            return (
                pltpu.make_async_copy(source.at[xh], mine, sl.at[0]),
                send(source.at[xh], mine, sg, (1,), to_core),
                send(source.at[1 - xh], mine, sg, (0,), device),
                send(other, other, sg, (2,), to_core),
            )

        def rows_wait(copies, target):
            local, core_own, across, core_other = copies
            across.wait_recv()
            core_other.start()
            local.wait()
            core_own.wait()
            core_other.wait()

            def turn(i):
                target[i] = gmt[:, at_row(i)].astype(F32).T.astype(BF16)

            loop(blocks, turn)

        @pl.when(first_section)
        def _():
            for copy in rows_in(xin, to_xy)[:2]:
                copy.start()

        @pl.when(last_section)
        def _():
            rows_in(xin, to_xy)[2].start()

        mc[0] = jnp.zeros_like(mc[0])
        for row, name in enumerate(("attn_gain", "mlp_gain", "out_bias", "down_bias", "up_bias")):
            mc[0, row : row + 1, :] = r[name][...].astype(F32)
        for row in range(2):
            mc[0, 5 + row : 6 + row, : wo.shape[1]] = r["qv_bias"][0, row : row + 1, :].astype(F32)
        misc_x = send(mc.at[0], mc.at[1], sg, (3,), to_x)
        misc_x.start()
        locals_, pieces = [], []
        for which, (name, target, cuts) in enumerate((("wqh", [wq.at[0], wq.at[1]], 2), ("woh", [wo.at[0], wo.at[1]], 1), ("wuh", wu, 2), ("wdh", wd, 4))):
            source = r[name]
            locals_.append(pltpu.make_async_copy(source, target[0], sl.at[4 + which]))
            half = source.shape[0] // 2
            step = half // cuts
            group = []
            for cut in range(cuts):
                at = pl.ds(pl.multiple_of(parity * half + cut * step, 16), step)
                place = 4 * which + cut
                group.append((
                    send(source.at[at], target[1].at[at], sw, (0, place), to_x),
                    send(target[1].at[at], target[1].at[at], sw, (1, place), to_pair),
                ))
            pieces.append(group)
        for which, (local, group) in enumerate(zip(locals_, pieces, strict=True)):
            if which == 3:

                @pl.when(last_section)
                def _():
                    for copy in rows_in(cot, to_x)[:3]:
                        copy.start()

            local.start()
            for across, _ in group:
                across.start()

        def pass_on(which, *cuts):
            for cut in cuts:
                across, pair = pieces[which][cut]
                across.wait_recv()
                pair.start()

        def have(which):
            locals_[which].wait()
            for across, pair in pieces[which]:
                across.wait_send()
                pair.wait()

        sown[...] = jnp.zeros_like(sown)
        soth[...] = jnp.zeros_like(soth)
        segment = seg[xh]
        segc[...] = jnp.broadcast_to(segment.astype(F32), (128, length)).T

        def ex_at(kind, i):
            return pl.ds(pl.multiple_of(kind * length + i * rows, rows), rows)

        def shifted(i):
            return lax.rem(i + 1, blocks)

        def pair_copy(kind, i):
            return send(ex.at[ex_at(2 * kind, i)], ex.at[ex_at(2 * kind + 1, i)], se, (kind, i), to_core)

        def pair_send(kind, i, value):
            ex[ex_at(2 * kind, i), :] = value.astype(BF16)
            pair_copy(kind, i).start()

        def pair_sum(kind, i):
            pair_copy(kind, i).wait()
            return ex[ex_at(2 * kind, i), :].astype(F32) + ex[ex_at(2 * kind + 1, i), :].astype(F32)

        half_rows = rows // 2
        own_half = pl.ds(pl.multiple_of(core * half_rows, half_rows), half_rows)

        def hop_copy(i, target):
            return send(resb.at[lax.rem(i, 2), own_half], target.at[i, own_half], sh, (0, i), to_y)

        def hop_core(i, target):
            return send(target.at[i, own_half], target.at[i, own_half], sh, (1, i), to_core)

        pass_on(0, 0, 1)

        @pl.when(first_section)
        def _():
            rows_wait(rows_in(xin, to_xy), xbuf)
            pass_on(1, 0)

        @pl.when(last_section)
        def _():
            pass_on(1, 0)
            pass_on(2, 0, 1)
            copies = rows_in(cot, to_x)
            rows_wait(copies, cotb)
            pass_on(3, 0, 1, 2, 3)
            copies[2].wait_send()
            rows_in(xin, to_xy)[2].wait_send()

        misc_x.wait()
        attn_gain, mlp_gain, out_bias, down_bias = (mc[0, i : i + 1, :] for i in range(4))
        have(0)

        def allowed(i, j0, j1, diagonal):
            same = segc[j0:j1, :]
            same = jnp.concatenate([same] * (rows // same.shape[1]), axis=1)
            cols = slice(i * rows, (i + 1) * rows)
            keep = same == seg[xh, :, cols].astype(F32)
            if diagonal:
                key = lax.broadcasted_iota(jnp.int32, keep.shape, 0)
                query = lax.broadcasted_iota(jnp.int32, keep.shape, 1)
                keep = keep & (key <= query)
            return keep

        def masked(scores, i, j0, j1, diagonal):
            return jnp.where(allowed(i, j0, j1, diagonal), scores, NEGATIVE)

        def key_parts(i):
            parts = [(i * rows, (i + 1) * rows, True)]
            if i > 0:
                parts.append((0, i * rows, False))
            return parts

        def project(i):
            full = expanded(xbuf[i])
            normed = (full * norm_factor(full) * attn_gain).astype(BF16)
            nrm[i] = normed
            cols = at_row(i)
            for slot in range(slots):
                three = dot(wq[slot], normed, NT)
                bias = mc[slot, :, :part].T
                query = (three[:part] + bias[:, 5:6]).astype(BF16) * SCALE
                key = three[part : 2 * part]
                value = (three[2 * part :] + bias[:, 6:7]).astype(BF16).astype(F32)
                for h in range(hs):
                    at = slice(h * HD, (h + 1) * HD)
                    head = slot * hs + h
                    qt[i, head] = query[at].astype(BF16)
                    kt[head, :, cols] = key[at].astype(BF16)
                    vt[head, :, cols] = value[at].astype(BF16)
                    kn[head, cols, :] = key[at].T.astype(BF16)
                    vn[head, cols, :] = value[at].T.astype(BF16)

        def attend(i, group):
            cols = slice(i * rows, (i + 1) * rows)
            parts = key_parts(i)
            scores = [[masked(dot(kn[h, a:b], qt[i, h]), i, a, b, g) for a, b, g in parts] for h in group]
            tops = []
            for score in scores:
                top = score[0].max(axis=0, keepdims=True)
                for more in score[1:]:
                    top = jnp.maximum(top, more.max(axis=0, keepdims=True))
                tops.append(top)
            powers = [[jnp.exp(one - top) for one in score] for score, top in zip(scores, tops, strict=True)]
            totals = [sum(row_sum(one) for one in power) for power in powers]
            contexts = [
                sum(dot(vt[h, :, a:b], one.astype(BF16)) for one, (a, b, _) in zip(power, parts, strict=True))
                for h, power in zip(group, powers, strict=True)
            ]
            for h, top, total, context in zip(group, tops, totals, contexts, strict=True):
                ctx[h, :, cols] = (context / total).astype(BF16)
                lse[i, h] = top + jnp.log(total)

        def each_block(i, body, number):
            for block in range(blocks):

                @pl.when(i == block)
                def _():
                    loop(heads // number, lambda n: body(block, [n * number + k for k in range(number)]))

        def attention_rows(i):
            @pl.when(last_section & (i == 0))
            def _():
                hop_copy(0, xbuf).wait_recv()
                hop_core(0, xbuf).start()

            @pl.when(last_section)
            def _():
                hop_core(i, xbuf).wait()

            project(i)
            each_block(i, attend, HEADS_FORWARD)

            @pl.when(i == 0)
            def _():
                have(1)

            context = ctx[:, :, at_row(i)].reshape(heads * HD, rows)
            pair_send(0, shifted(i), dot(context, wo[...].reshape(heads * HD, width), TN))

            for step, (which, cut) in enumerate(((2, 0), (2, 1), (3, 0), (3, 1))):

                @pl.when((i == step) & first_section)
                def _():
                    pass_on(which, cut)

            @pl.when(last_section & (i < blocks - 1))
            def _():
                hop_copy(i + 1, xbuf).wait_recv()
                hop_core(i + 1, xbuf).start()

        def up_rows(i):
            @pl.when(i == 0)
            def _():
                have(2)

            branch = pair_sum(0, shifted(i)) + out_bias
            middle = expanded(xbuf[i]) + centred(branch)
            pool[mid_at(i), :] = middle
            normed = middle * norm_factor(middle) * mlp_gain
            normed = normed.astype(BF16)
            for slot in range(slots):
                pre = dot(normed, wu[slot][...]) + mc[slot, 4:5, :]
                square = pre * pre
                bend = jnp.tanh(pre * (GELU_C + (GELU_C * GELU_A) * square))
                grow = 0.5 + 0.5 * bend
                value = pre * grow
                hid[slot, i] = value.astype(BF16)
                slope = GELU_C + (3.0 * GELU_C * GELU_A) * square
                gp[slot, i] = (grow + value * (1.0 - bend) * slope).astype(BF16)

            for step, cut in ((0, 2), (1, 3)):

                @pl.when((i == step) & first_section)
                def _():
                    pass_on(3, cut)

        def down_rows(i):
            @pl.when(i == 0)
            def _():
                have(3)

            branch = dot(hid[0, i], wd[0][...], NT)
            for slot in range(1, slots):
                branch = branch + dot(hid[slot, i], wd[slot][...], NT)
            pair_send(1, shifted(i), branch)

        def keep_out(i, value):
            @pl.when((i == t) | (i == t_x))
            def _():
                outt[jnp.where(i == t, 0, 1)] = value.T.astype(BF16)

        def result_rows(i):
            result = pool[mid_at(i), :] + centred(pair_sum(1, shifted(i)) + down_bias)
            keep_out(i, result)

            @pl.when(first_section)
            def _():
                @pl.when(i >= 2)
                def _():
                    hop_copy(i - 2, xbuf).wait_send()

                lane = lax.broadcasted_iota(jnp.int32, result.shape, 1)
                resb[lax.rem(i, 2)] = jnp.where(lane == width - 1, 0.0, result).astype(BF16)
                hop_copy(i, xbuf).start()

        def forward(step):
            i_up = jnp.where(first_section, step - blocks, step - 1)
            i_down = jnp.where(first_section, step - 2 * blocks, step - 1)
            i_res = i_down - 1
            some_res = (i_res >= 0) & (i_res < blocks)

            @pl.when(step < blocks)
            def _():
                attention_rows(step)

            @pl.when(last_section & some_res & (i_res < blocks - 1))
            def _():
                result_rows(i_res)

            @pl.when((i_up >= 0) & (i_up < blocks))
            def _():
                up_rows(i_up)

            @pl.when((i_down >= 0) & (i_down < blocks))
            def _():
                down_rows(i_down)

            @pl.when(first_section & some_res)
            def _():
                result_rows(i_res)

        loop(3 * blocks + 1, forward)

        def rows_out(target, which):
            return (
                pltpu.make_async_copy(outt.at[0], target.at[xh], sl.at[2]),
                send(outt.at[1], target.at[xh], so, (which,), to_x),
            )

        act_copies = rows_out(act, 0)

        @pl.when(first_section)
        def _():
            loop(2, lambda i: hop_copy(blocks - 2 + i, xbuf).wait_send())

        def other_at(k):
            row = k * CHUNK
            third = jnp.where(row < 3 * rows, 0, jnp.where(row < 6 * rows, 1, 2))
            place = row - third * 3 * rows
            kind = jnp.where(place < rows, 0, jnp.where(place < 2 * rows, 1, 2))
            row = kind * (length - rows) + (blocks - 1 - third) * rows + place
            return pl.ds(pl.multiple_of(row, CHUNK), CHUNK)

        def own_at(k):
            row = k * CHUNK
            third = jnp.where(row < 3 * rows, 0, jnp.where(row < 6 * rows, 1, 2))
            place = row - third * 3 * rows
            down = jnp.where(place < rows, place + 3 * rows, place + 6 * rows)
            up = jnp.where(place < 2 * rows, place + rows, place + 4 * rows)
            rest = jnp.where(place < rows, place, place + 3 * rows)
            row = jnp.where(third == 0, down, jnp.where(third == 1, up, rest))
            return pl.ds(pl.multiple_of(row, CHUNK), CHUNK)

        def x_copy(k):
            return send(ex.at[other_at(k)], xrec.at[k], sr, (k,), to_x)

        def put(turn, first, value):
            @pl.when(turn == 0)
            def _():
                for k in range(value.shape[0] // CHUNK):
                    ex[other_at(first + k), :] = value[k * CHUNK : (k + 1) * CHUNK].astype(BF16)

            @pl.when(turn == 1)
            def _():
                for k in range(value.shape[0] // CHUNK):
                    pool[own_at(first + k), :] = value[k * CHUNK : (k + 1) * CHUNK]

        def start(turn, first, number):
            @pl.when(turn == 0)
            def _():
                loop(number, lambda k: x_copy(first + k).start())

        tile = 256
        tiles = width // tile

        def down_part(turn, k):
            at = pl.ds(pl.multiple_of(k * tile, tile), tile)
            first = k * (tile // CHUNK)
            put(turn, first, dot(gmt[at, :], hid[1 - turn].reshape(length, units)))
            start(turn, first, tile // CHUNK)

        def up_part(turn, k):
            at = pl.ds(pl.multiple_of(k * tile, tile), tile)
            first = width // CHUNK + k * (tile // CHUNK)
            put(turn, first, dot(n2t[at, :], gp[1 - turn].reshape(length, units)))
            start(turn, first, tile // CHUNK)

        def turn_normed(i):
            middle = pool[mid_at(i), :]
            n2t[:, at_row(i)] = (middle * norm_factor(middle) * mlp_gain).T.astype(BF16)

        def down_grads(turn):
            loop(tiles, lambda k: down_part(turn, k))

        def up_grads(turn):
            loop(tiles, lambda k: up_part(turn, k))

        middle = count // 2
        on_left = d < middle
        depth = jnp.where(on_left, d, count - 1 - d)
        has_outer = depth > 0
        is_mid = depth == middle - 1
        inner = (s, t, jnp.where(on_left, d + 1, d - 1))
        outer = (s, t, jnp.where(on_left, d - 1, d + 1))
        lag_in = LAG * depth
        lag_mid = LAG * middle
        lag_out = lag_mid + LAG * (middle - 1 - depth)
        lag_all = lag_mid + LAG * (middle - 1)

        def fin_at(k):
            return pl.ds(pl.multiple_of(k * CHUNK, CHUNK), CHUNK)

        def in_copy(k):
            return send(xrec.at[k], cin.at[k], sc, (0, k), inner)

        def cross_copy(k):
            return send(xrec.at[k], wud.at[fin_at(k)], sc, (1, k), inner)

        def out_copy(k):
            return send(wud.at[fin_at(k)], wud.at[fin_at(k)], sc, (2, k), outer)

        outs, place = [], 0
        for which, name in enumerate(("down", "up", "qkv", "out")):
            number = r[name].shape[0]
            copy = pltpu.make_async_copy(wud.at[pl.ds(place, number)], r[name], so.at[0, 2 + which])
            place += number
            outs.append((place // CHUNK - 1, copy))

        def matrix_out(k):
            for final, copy in outs:

                @pl.when(k == final)
                def _():
                    copy.start()

        small_x = send(soth, srec, ss, (0,), to_x)
        s_in = send(sown, scin, ss, (1,), inner)
        s_cross = send(sown, sfin, ss, (2,), inner)
        s_out = send(sfin, sfin, ss, (3,), outer)

        def reduce_small(it):
            begin = chunks - 4

            @pl.when(it == begin)
            def _():
                small_x.wait()
                sown[...] = sown[...] + srec[...]

            @pl.when(it == begin + lag_in)
            def _():
                @pl.when(has_outer)
                def _():
                    s_in.wait_recv()
                    sown[...] = sown[...] + scin[...]

                @pl.when(jnp.logical_not(is_mid))
                def _():
                    s_in.start()

                @pl.when(is_mid)
                def _():
                    s_cross.start()

            @pl.when(it == begin + lag_out)
            def _():
                @pl.when(is_mid)
                def _():
                    s_cross.wait()
                    sfin[...] = sfin[...] + sown[...]

                @pl.when(jnp.logical_not(is_mid))
                def _():
                    s_out.wait_recv()

                @pl.when(has_outer)
                def _():
                    s_out.start()

        def reduce(it):
            @pl.when((it == 0) & is_mid)
            def _():
                pl.semaphore_signal(ready, inc=1, device_id=inner, device_id_type=MESH)

            @pl.when(it < chunks)
            def _():
                k = it
                x_copy(k).wait()
                xrec[k] = (pool[own_at(k), :] + xrec[k].astype(F32)).astype(BF16)

            k_in = it - lag_in

            @pl.when((k_in >= 0) & (k_in < chunks))
            def _():
                k = k_in

                @pl.when(has_outer)
                def _():
                    in_copy(k).wait_recv()
                    xrec[k] = (xrec[k].astype(F32) + cin[k].astype(F32)).astype(BF16)

                @pl.when(jnp.logical_not(is_mid))
                def _():
                    in_copy(k).start()

                @pl.when(is_mid)
                def _():
                    @pl.when(k == 0)
                    def _():
                        pl.semaphore_wait(ready, 1)

                    cross_copy(k).start()

            k_out = it - lag_out

            @pl.when((k_out >= 0) & (k_out < chunks))
            def _():
                k = k_out

                @pl.when(is_mid)
                def _():
                    cross_copy(k).wait_recv()
                    wud[fin_at(k), :] = (xrec[k].astype(F32) + wud[fin_at(k), :].astype(F32)).astype(BF16)

                @pl.when(jnp.logical_not(is_mid))
                def _():
                    out_copy(k).wait_recv()

                @pl.when(has_outer)
                def _():
                    out_copy(k).start()

                matrix_out(k)

            reduce_small(it)

        def grad_rows(i):
            @pl.when(first_section)
            def _():
                hop_copy(i, cotb).wait_recv()
                hop_core(i, cotb).start()
                hop_core(i, cotb).wait()
                turn_grad(i)

        def turn_grad(i):
            gmt[:, at_row(i)] = centred(cotb[i].astype(F32)).T.astype(BF16)

        def down_back(i):
            grad = centred(cotb[i].astype(F32))
            pool[grad_at(i), :] = grad
            grad = grad.astype(BF16)
            sown[3:4, :] += row_sum(grad.astype(F32))
            befores = []
            for slot, sums in ((0, sown), (1, soth)):
                before = (dot(grad, wd[slot][...]) * gp[slot, i].astype(F32)).astype(BF16)
                gp[slot, i] = before
                sums[4:5, :] += row_sum(before.astype(F32))
                befores.append(before)
            both = jnp.concatenate([wu[slot][...] for slot in range(slots)], axis=1)
            pair_send(0, i, dot(jnp.concatenate(befores, axis=1), both, NT))

        def out_back(i):
            grad, gain_grad = norm_back(pair_sum(0, i), pool[mid_at(i), :], mlp_gain)
            sown[2:3, :] += gain_grad
            grad = grad + pool[grad_at(i), :]
            pool[grad_at(i), :] = grad
            grad = grad.astype(BF16)
            gat[i] = grad
            sown[1:2, :] += row_sum(grad.astype(F32))
            back = dot(wo[...].reshape(heads * HD, width), grad, NT).astype(BF16)
            for h in range(heads):
                dot_[i, h] = back[h * HD : (h + 1) * HD]

        def attend_back(i, group):
            parts = key_parts(i)
            cols = slice(i * rows, (i + 1) * rows)
            masks = [jnp.where(allowed(i, a, b, g), 0.0, NEGATIVE) for a, b, g in parts]
            probs, g_probs = [], []
            for h in group:
                less = [mask - lse[i, h] for mask in masks]
                probs.append([jnp.exp(dot(kn[h, a:b], qt[i, h]) + one) for one, (a, b, _) in zip(less, parts, strict=True)])
                g_probs.append([dot(vn[h, a:b], dot_[i, h]) for a, b, _ in parts])
            centres = [
                sum(row_sum(x * y) for x, y in zip(prob, g_prob, strict=True))
                for prob, g_prob in zip(probs, g_probs, strict=True)
            ]
            g_scores = [
                [(x * (y - centre)).astype(BF16) for x, y in zip(prob, g_prob, strict=True)]
                for prob, g_prob, centre in zip(probs, g_probs, centres, strict=True)
            ]
            g_values = [[dot(dot_[i, h], x.astype(BF16), NT) for x in prob] for h, prob in zip(group, probs, strict=True)]
            g_keys = [[dot(qt[i, h], x, NT) for x in g_score] for h, g_score in zip(group, g_scores, strict=True)]
            g_queries = [
                sum(dot(kt[h, :, a:b], x) for x, (a, b, _) in zip(g_score, parts, strict=True))
                for h, g_score in zip(group, g_scores, strict=True)
            ]
            for h, g_value, g_key, g_query in zip(group, g_values, g_keys, g_queries, strict=True):
                slot, place = lax.div(h, hs), lax.rem(h, hs)
                for (a, b, _), value, key in zip(parts, g_value, g_key, strict=True):
                    if i == blocks - 1:
                        dv[h, :, a:b] = value
                        dk[h, :, a:b] = key
                    else:
                        dv[h, :, a:b] += value
                        dk[h, :, a:b] += key
                dqkv[slot, 0, place, :, cols] = (g_query * SCALE).astype(BF16)
                dqkv[slot, 1, place, :, cols] = dk[h, :, cols].astype(BF16)
                dqkv[slot, 2, place, :, cols] = dv[h, :, cols].astype(BF16)

        def qkv_back(i):
            three = dqkv[:, :, :, :, at_row(i)].reshape(slots * 3 * part, rows)
            pair_send(1, i, dot(three, wq[...].reshape(slots * 3 * part, width), TN))

        def in_back(i):
            grad, gain_grad = norm_back(pair_sum(1, i), expanded(xbuf[i]), attn_gain)
            sown[0:1, :] += gain_grad
            grad = grad + pool[grad_at(i), :]
            grad = grad - grad[:, width - 1 :]
            keep_out(i, grad)

            @pl.when(last_section)
            def _():
                @pl.when(i < blocks - 2)
                def _():
                    hop_copy(i + 2, cotb).wait_send()

                resb[lax.rem(i, 2)] = grad.astype(BF16)
                hop_copy(i, cotb).start()

        def advance(step, place):
            def body(it, carry):
                reduce(it)
                return carry

            first, stop = 0, 0
            for at, (lo, hi) in EARLY[place].items():
                first = jnp.where(first_section & (step == at), lo, first)
                stop = jnp.where(first_section & (step == at), hi, stop)
            lax.fori_loop(first, stop, body, 0)

        def planned(step, name):
            found = -1
            for at, (first, last) in enumerate(zip(*PLAN[name], strict=True)):
                found = jnp.where(step == at, jnp.where(first_section, first, last), found)
            return found

        def turns(first, stop, body):
            def one(turn, carry):
                body(turn)
                return carry

            lax.fori_loop(first, stop, one, 0)

        def backward(step):
            n_down, n_in, n_rest, n_late = (planned(step, name) for name in ("down", "in", "rest", "late"))
            n_grad = planned(step, "grads")
            last = blocks - 1
            advance(step, 3)

            @pl.when(step == jnp.where(first_section, blocks - 2, 2 * blocks - 1))
            def _():
                loop(blocks, turn_normed)

            @pl.when(last_section & (step == 2 * blocks - 1))
            def _():
                loop(blocks, turn_grad)

            @pl.when(n_down >= 0)
            def _():
                grad_rows(last - n_down)

            early = jnp.where(n_grad == 0, 1, 0)
            turns(0, early, down_grads)

            @pl.when(n_down >= 0)
            def _():
                down_back(last - n_down)

            @pl.when(step == 0)
            def _():
                @pl.when(last_section)
                def _():
                    result_rows(last)

                for copy in act_copies:
                    copy.start()

            @pl.when((n_grad == 0) | (n_grad == 2))
            def _():
                turns(early, 2, down_grads)
                advance(step, 4)

            @pl.when(n_in == 0)
            def _():
                for copy in act_copies:
                    copy.wait()

            @pl.when(n_in >= 0)
            def _():
                in_back(last - n_in)

            @pl.when(n_rest >= 0)
            def _():
                i = last - n_rest
                out_back(i)
                advance(step, 0)

                @pl.when(n_late >= 0)
                def _():
                    in_back(last - n_late)

                @pl.when(n_grad == 1)
                def _():
                    loop(2, up_grads)

                each_block(i, attend_back, HEADS_BACKWARD)
                advance(step, 1)
                qkv_back(i)
                advance(step, 2)

            @pl.when(n_grad == 2)
            def _():
                loop(2, up_grads)

        loop(len(PLAN["in"][0]), backward)
        ones = jnp.ones((8, length), BF16)
        sown[5:6, : 3 * part] = dot(ones, dqkv[0].reshape(3 * part, length), NT)[0:1]
        soth[5:6, : 3 * part] = dot(ones, dqkv[1].reshape(3 * part, length), NT)[0:1]
        soth[0:4, :] = sown[0:4, :]
        small_x.start()

        def attention_grads(turn):
            slot = 1 - turn

            def qkv_part(k):
                first = (2 * width) // CHUNK + k * (part // CHUNK)
                put(turn, first, dot(dqkv[slot, k].reshape(part, length), nrm[...].reshape(length, width)))

            loop(3, qkv_part)
            first = (2 * width + 3 * part) // CHUNK
            context = ctx[pl.ds(slot * hs, hs)].reshape(part, length)
            put(turn, first, dot(context, gat[...].reshape(length, width)))
            start(turn, 2 * (width // CHUNK), chunks - 2 * (width // CHUNK))

        loop(2, attention_grads)
        eg_copies = rows_out(eg, 1)
        for copy in eg_copies:
            copy.start()

        def rest(it, carry):
            reduce(it)
            return carry

        begun = max(hi for place in EARLY for _, hi in place.values())
        lax.fori_loop(jnp.where(first_section, begun, 0), chunks + lag_all, rest, 0)
        small[...] = sfin[...]

        @pl.when(jnp.logical_not(is_mid))
        def _():
            s_in.wait_send()

        @pl.when(has_outer)
        def _():
            s_out.wait_send()

        def drain(k):
            @pl.when(jnp.logical_not(is_mid))
            def _():
                in_copy(k).wait_send()

            @pl.when(is_mid)
            def _():
                cross_copy(k).wait_send()

            @pl.when(has_outer)
            def _():
                out_copy(k).wait_send()

        loop(chunks, drain)
        for _, copy in outs:
            copy.wait()

        @pl.when(last_section)
        def _():
            loop(2, lambda i: hop_copy(i, cotb).wait_send())

        for copy in eg_copies:
            copy.wait()

    return kernel


def per_device(
    block_input,
    segments,
    cotangent,
    attn_gain,
    qkv_weight,
    qv_bias,
    out_weight,
    out_bias,
    mlp_gain,
    up_projection_weight,
    up_bias,
    down_projection_weight,
    down_bias,
):
    micros, rows, _, kept = block_input.shape
    width = qkv_weight.shape[1]
    part = qkv_weight.shape[3]
    units = up_projection_weight.shape[2]
    blocks = lax.axis_size("tensor")
    count = lax.axis_size("dp")
    length = blocks * rows
    slots = 2
    hs = part // HD
    heads = slots * hs
    chunks = (2 * width + 4 * part) // CHUNK

    def features_first(array):
        first = array[:, :, 0, :].transpose(2, 0, 1)
        return jnp.pad(first, ((0, width - kept), (0, 0), (0, 0))).transpose(1, 0, 2)

    inputs = {
        "xin": features_first(block_input),
        "cot": features_first(cotangent),
        "wqh": qkv_weight[0].transpose(1, 2, 0).reshape(3 * part, width),
        "woh": out_weight[0],
        "wuh": up_projection_weight[0],
        "wdh": down_projection_weight[0],
        "attn_gain": attn_gain,
        "mlp_gain": mlp_gain,
        "out_bias": out_bias,
        "down_bias": down_bias,
        "up_bias": up_bias,
        "qv_bias": qv_bias,
        "seg": segments,
    }
    outputs = {
        "act": ((micros, width, rows), BF16),
        "eg": ((micros, width, rows), BF16),
        "down": ((width, units), BF16),
        "up": ((width, units), BF16),
        "qkv": ((3 * part, width), BF16),
        "out": ((part, width), BF16),
        "small": ((8, width), F32),
    }
    scratch = {
        "wq": ((slots, 3 * part, width), BF16),
        "wo": ((slots, part, width), BF16),
        "wud": ((2 * slots * width, units), BF16),
        "mc": ((slots, 8, width), F32),
        "xbuf": ((blocks, rows, width), BF16),
        "cotb": ((blocks, rows, width), BF16),
        "resb": ((2, rows, width), BF16),
        "outt": ((2, width, rows), BF16),
        "pool": ((max(2 * length, chunks * CHUNK), width), F32),
        "nrm": ((blocks, rows, width), BF16),
        "n2t": ((width, length), BF16),
        "qt": ((blocks, heads, HD, rows), BF16),
        "kt": ((heads, HD, length), BF16),
        "vt": ((heads, HD, length), BF16),
        "kn": ((heads, length, HD), BF16),
        "vn": ((heads, length, HD), BF16),
        "ctx": ((heads, HD, length), BF16),
        "lse": ((blocks, heads, 1, rows), F32),
        "segc": ((length, 128), F32),
        "gp": ((slots, blocks, rows, units), BF16),
        "hid": ((slots, blocks, rows, units), BF16),
        "gmt": ((width, length), BF16),
        "gat": ((blocks, rows, width), BF16),
        "dot": ((blocks, heads, HD, rows), BF16),
        "dqkv": ((slots, 3, hs, HD, length), BF16),
        "dk": ((heads, HD, length), F32),
        "dv": ((heads, HD, length), F32),
        "ex": ((4 * length, width), BF16),
        "xrec": ((chunks, CHUNK, width), BF16),
        "cin": ((chunks, CHUNK, width), BF16),
        "sown": ((8, width), F32),
        "soth": ((8, width), F32),
        "srec": ((8, width), F32),
        "scin": ((8, width), F32),
        "sfin": ((8, width), F32),
    }
    dma = pltpu.SemaphoreType.DMA
    semaphores = {
        "sl": dma((8,)),
        "sg": dma((2, 4)),
        "sw": dma((2, 2, 16)),
        "se": dma((2, 2, blocks)),
        "sh": dma((2, 2, blocks)),
        "so": dma((2, 6)),
        "sr": dma((2, chunks)),
        "sc": dma((2, 3, chunks)),
        "ss": dma((2, 4)),
        "ready": pltpu.SemaphoreType.REGULAR,
    }
    in_vmem = {"attn_gain", "mlp_gain", "out_bias", "down_bias", "up_bias", "qv_bias", "seg", "small"}

    def spec(name):
        return pl.BlockSpec(memory_space=pltpu.VMEM if name in in_vmem else pl.ANY)

    names = [*inputs, *outputs, *scratch, *semaphores]
    act, eg, down, up, qkv, out, small = pl.pallas_call(
        make_kernel(names, count),
        out_shape=[jax.ShapeDtypeStruct(*item) for item in outputs.values()],
        in_specs=[spec(name) for name in inputs],
        out_specs=[spec(name) for name in outputs],
        scratch_shapes=[pltpu.VMEM(*item) for item in scratch.values()] + list(semaphores.values()),
        compiler_params=pltpu.CompilerParams(
            collective_id=0, has_side_effects=True, vmem_limit_bytes=63 * 1024 * 1024
        ),
        name="layers",
    )(*inputs.values())

    def positions_first(array):
        return array[:, :kept, :].transpose(0, 2, 1)[None, :, :, None, :]

    qv = small[5, : 3 * part].reshape(3, part)
    return (
        positions_first(act),
        positions_first(eg).astype(F32),
        small[0:1],
        qkv.reshape(3, part, width).transpose(2, 0, 1).astype(F32)[None],
        qv[0::2][None],
        out.astype(F32)[None],
        small[1:2],
        small[2:3],
        up.astype(F32)[None],
        small[4:5, :units],
        down.astype(F32)[None],
        small[3:4],
    )


def solution(mesh):
    in_specs = (
        P(None, "tensor", "dp", None),
        P(None, "dp", None),
        P(None, "tensor", "dp", None),
        P("section", None),
        P("section", None, None, "tensor"),
        P("section", None, "tensor"),
        P("section", "tensor", None),
        P("section", None),
        P("section", None),
        P("section", None, "tensor"),
        P("section", "tensor"),
        P("section", None, "tensor"),
        P("section", None),
    )
    out_specs = (
        P("section", None, "tensor", "dp", None),
        P("section", None, "tensor", "dp", None),
        P("section", None),
        P("section", None, None, "tensor"),
        P("section", None, "tensor"),
        P("section", "tensor", None),
        P("section", None),
        P("section", None),
        P("section", None, "tensor"),
        P("section", "tensor"),
        P("section", None, "tensor"),
        P("section", None),
    )
    return jax.shard_map(
        per_device, mesh=mesh, in_specs=in_specs, out_specs=out_specs, check_vma=False
    )
```

```python
import jax
import jax.numpy as jnp
from jax import lax
from jax.experimental import pallas as pl
from jax.experimental.pallas import tpu as pltpu
from jax.sharding import PartitionSpec as P

HD = 64
EPS = 1e-05
SCALE = 0.125
NEGATIVE = -1e30
CHUNK = 64
LAG = 3
HEADS_FORWARD = 6
HEADS_BACKWARD = 3
EARLY = (
    {3: (1, 4), 4: (8, 10), 5: (16, 18)},
    {3: (4, 7), 4: (10, 15), 5: (18, 19)},
    {3: (7, 8), 4: (15, 16), 5: (19, 20)},
    {6: (20, 23)},
    {3: (0, 1)},
)
PLAN = {
    "down": ((0, 1, 2, 3, -1, -1, -1, -1), (0, 1, 2, 3, -1, -1, -1, -1)),
    "rest": ((0, -1, -1, 1, 2, 3, -1, -1), (-1, 0, 1, 2, 3, -1, -1, -1)),
    "in": ((-1, 0, -1, -1, -1, -1, 3, -1), (-1, -1, 0, 1, -1, 2, 3, -1)),
    "late": ((-1, -1, -1, -1, 1, 2, -1, -1), (-1,) * 8),
    "grads": ((-1, -1, -1, 0, 1, -1, -1, -1), (-1, -1, -1, -1, -1, -1, -1, 2)),
}
MESH = pl.DeviceIdType.MESH
F32 = jnp.float32
BF16 = jnp.bfloat16
NN = (((1,), (0,)), ((), ()))
NT = (((1,), (1,)), ((), ()))
TN = (((0,), (0,)), ((), ()))
GELU_C = 0.7978845608028654
GELU_A = 0.044715


def dot(left, right, dims=NN):
    return lax.dot_general(left, right, dims, preferred_element_type=F32)


def lane_sum(value):
    return jnp.sum(value, axis=-1, keepdims=True)


def row_sum(value):
    return jnp.sum(value, axis=0, keepdims=True)


def expanded(block):
    value = block.astype(F32)
    lane = lax.broadcasted_iota(jnp.int32, value.shape, 1)
    return jnp.where(lane == value.shape[1] - 1, -lane_sum(value), value)


def norm_factor(full):
    return lax.rsqrt(lane_sum(full * full) * (1.0 / full.shape[1]) + EPS)


def centred(value):
    return value - lane_sum(value) * (1.0 / value.shape[1])


def norm_back(grad, full, gain):
    factor = norm_factor(full)
    weighted = grad * gain
    inner = lane_sum(weighted * full) * (1.0 / full.shape[1])
    gain_grad = row_sum(grad * full * factor)
    return centred(factor * weighted - full * (factor * factor * factor * inner)), gain_grad


def make_kernel(names, count):
    def kernel(*refs):
        r = dict(zip(names, refs, strict=True))
        xin, cot, seg = r["xin"], r["cot"], r["seg"]
        act, eg, small = r["act"], r["eg"], r["small"]
        wq, wo, wud, mc = r["wq"], r["wo"], r["wud"], r["mc"]
        xbuf, cotb, resb, outt = r["xbuf"], r["cotb"], r["resb"], r["outt"]
        pool, nrm, n2t = r["pool"], r["nrm"], r["n2t"]
        qt, kt, vt, kn, vn = r["qt"], r["kt"], r["vt"], r["kn"], r["vn"]
        ctx, lse, segc = r["ctx"], r["lse"], r["segc"]
        gp, hid, gmt, gat = r["gp"], r["hid"], r["gmt"], r["gat"]
        dot_, dqkv, dk, dv = r["dot"], r["dqkv"], r["dk"], r["dv"]
        ex, xrec, cin, ready = r["ex"], r["xrec"], r["cin"], r["ready"]
        sown, soth, srec, scin, sfin = r["sown"], r["soth"], r["srec"], r["scin"], r["sfin"]
        sl, sg, sw, se, sh, so, sr, sc, ss = (
            r[name] for name in ("sl", "sg", "sw", "se", "sh", "so", "sr", "sc", "ss"))
        blocks, rows, width = xbuf.shape
        length = blocks * rows
        slots, hs = wq.shape[0], wo.shape[1] // HD
        heads = slots * hs
        part = wo.shape[1]
        units = wud.shape[1]
        chunks = xrec.shape[0]
        wu = [wud.at[pl.ds(slot * width, width)] for slot in range(slots)]
        wd = [wud.at[pl.ds((slots + slot) * width, width)] for slot in range(slots)]

        s = lax.axis_index("section")
        t = lax.axis_index("tensor")
        d = lax.axis_index("dp")
        core, xh = lax.rem(t, 2), lax.div(t, 2)
        t_core = 2 * xh + 1 - core
        t_x = 2 * (1 - xh) + core
        to_core = (s, t_core, d)
        to_x = (s, t_x, d)
        to_y = (1 - s, t, d)
        to_xy = (1 - s, t_x, d)
        parity = lax.rem(d, 2)
        to_pair = (s, t, d + 1 - 2 * parity)
        left, right = (s, t, d - 1), (s, t, d + 1)
        first_section, last_section = s == 0, s == 1

        def send(src, dst, sems, at, device):
            return pltpu.make_async_remote_copy(
                src_ref=src, dst_ref=dst, send_sem=sems.at[(0, *at)], recv_sem=sems.at[(1, *at)],
                device_id=device, device_id_type=MESH)

        def loop(stop, body):
            def step(i, carry):
                body(i)
                return carry

            lax.fori_loop(0, stop, step, 0)

        barrier = pltpu.get_barrier_semaphore()
        for device in (to_core, to_x, to_y, to_xy):
            pl.semaphore_signal(barrier, inc=1, device_id=device, device_id_type=MESH)

        @pl.when(d > 0)
        def _():
            pl.semaphore_signal(barrier, inc=1, device_id=left, device_id_type=MESH)

        @pl.when(d < count - 1)
        def _():
            pl.semaphore_signal(barrier, inc=1, device_id=right, device_id_type=MESH)

        ends = jnp.where(d > 0, 1, 0) + jnp.where(d < count - 1, 1, 0)
        pl.semaphore_wait(barrier, 4 + ends)

        def at_row(i):
            return pl.ds(pl.multiple_of(i * rows, rows), rows)

        mid_at = at_row

        def grad_at(i):
            return pl.ds(pl.multiple_of(length + i * rows, rows), rows)

        def rows_in(source, device):
            mine, other = gmt.at[:, at_row(t)], gmt.at[:, at_row(t_x)]
            return (
                pltpu.make_async_copy(source.at[xh], mine, sl.at[0]),
                send(source.at[xh], mine, sg, (1,), to_core),
                send(source.at[1 - xh], mine, sg, (0,), device),
                send(other, other, sg, (2,), to_core),
            )

        def rows_wait(copies, target):
            local, core_own, across, core_other = copies
            across.wait_recv()
            core_other.start()
            local.wait()
            core_own.wait()
            core_other.wait()

            def turn(i):
                target[i] = gmt[:, at_row(i)].astype(F32).T.astype(BF16)

            loop(blocks, turn)

        @pl.when(first_section)
        def _():
            for copy in rows_in(xin, to_xy)[:2]:
                copy.start()

        @pl.when(last_section)
        def _():
            rows_in(xin, to_xy)[2].start()

        mc[0] = jnp.zeros_like(mc[0])
        for row, name in enumerate(("attn_gain", "mlp_gain", "out_bias", "down_bias", "up_bias")):
            mc[0, row : row + 1, :] = r[name][...].astype(F32)
        for row in range(2):
            mc[0, 5 + row : 6 + row, : wo.shape[1]] = r["qv_bias"][0, row : row + 1, :].astype(F32)
        misc_x = send(mc.at[0], mc.at[1], sg, (3,), to_x)
        misc_x.start()
        locals_, pieces = [], []
        for which, (name, target, cuts) in enumerate((("wqh", [wq.at[0], wq.at[1]], 2), ("woh", [wo.at[0], wo.at[1]], 1), ("wuh", wu, 2), ("wdh", wd, 4))):
            source = r[name]
            locals_.append(pltpu.make_async_copy(source, target[0], sl.at[4 + which]))
            half = source.shape[0] // 2
            step = half // cuts
            group = []
            for cut in range(cuts):
                at = pl.ds(pl.multiple_of(parity * half + cut * step, 16), step)
                place = 4 * which + cut
                group.append((
                    send(source.at[at], target[1].at[at], sw, (0, place), to_x),
                    send(target[1].at[at], target[1].at[at], sw, (1, place), to_pair),
                ))
            pieces.append(group)
        for which, (local, group) in enumerate(zip(locals_, pieces, strict=True)):
            if which == 3:

                @pl.when(last_section)
                def _():
                    for copy in rows_in(cot, to_x)[:3]:
                        copy.start()

            local.start()
            for across, _ in group:
                across.start()

        def pass_on(which, *cuts):
            for cut in cuts:
                across, pair = pieces[which][cut]
                across.wait_recv()
                pair.start()

        def have(which):
            locals_[which].wait()
            for across, pair in pieces[which]:
                across.wait_send()
                pair.wait()

        sown[...] = jnp.zeros_like(sown)
        soth[...] = jnp.zeros_like(soth)
        segment = seg[xh]
        segc[...] = jnp.broadcast_to(segment.astype(F32), (128, length)).T

        def ex_at(kind, i):
            return pl.ds(pl.multiple_of(kind * length + i * rows, rows), rows)

        def shifted(i):
            return lax.rem(i + 1, blocks)

        def pair_copy(kind, i):
            return send(ex.at[ex_at(2 * kind, i)], ex.at[ex_at(2 * kind + 1, i)], se, (kind, i), to_core)

        def pair_send(kind, i, value):
            ex[ex_at(2 * kind, i), :] = value.astype(BF16)
            pair_copy(kind, i).start()

        def pair_sum(kind, i):
            pair_copy(kind, i).wait()
            return ex[ex_at(2 * kind, i), :].astype(F32) + ex[ex_at(2 * kind + 1, i), :].astype(F32)

        half_rows = rows // 2
        own_half = pl.ds(pl.multiple_of(core * half_rows, half_rows), half_rows)

        def hop_copy(i, target):
            return send(resb.at[lax.rem(i, 2), own_half], target.at[i, own_half], sh, (0, i), to_y)

        def hop_core(i, target):
            return send(target.at[i, own_half], target.at[i, own_half], sh, (1, i), to_core)

        pass_on(0, 0, 1)

        @pl.when(first_section)
        def _():
            rows_wait(rows_in(xin, to_xy), xbuf)
            pass_on(1, 0)

        @pl.when(last_section)
        def _():
            pass_on(1, 0)
            pass_on(2, 0, 1)
            copies = rows_in(cot, to_x)
            rows_wait(copies, cotb)
            pass_on(3, 0, 1, 2, 3)
            copies[2].wait_send()
            rows_in(xin, to_xy)[2].wait_send()

        misc_x.wait()
        attn_gain, mlp_gain, out_bias, down_bias = (mc[0, i : i + 1, :] for i in range(4))
        have(0)

        def allowed(i, j0, j1, diagonal):
            same = segc[j0:j1, :]
            same = jnp.concatenate([same] * (rows // same.shape[1]), axis=1)
            cols = slice(i * rows, (i + 1) * rows)
            keep = same == seg[xh, :, cols].astype(F32)
            if diagonal:
                key = lax.broadcasted_iota(jnp.int32, keep.shape, 0)
                query = lax.broadcasted_iota(jnp.int32, keep.shape, 1)
                keep = keep & (key <= query)
            return keep

        def masked(scores, i, j0, j1, diagonal):
            return jnp.where(allowed(i, j0, j1, diagonal), scores, NEGATIVE)

        def key_parts(i):
            parts = [(i * rows, (i + 1) * rows, True)]
            if i > 0:
                parts.append((0, i * rows, False))
            return parts

        def project(i):
            full = expanded(xbuf[i])
            normed = (full * norm_factor(full) * attn_gain).astype(BF16)
            nrm[i] = normed
            cols = at_row(i)
            for slot in range(slots):
                three = dot(wq[slot], normed, NT)
                bias = mc[slot, :, :part].T
                query = (three[:part] + bias[:, 5:6]).astype(BF16) * SCALE
                key = three[part : 2 * part]
                value = (three[2 * part :] + bias[:, 6:7]).astype(BF16).astype(F32)
                for h in range(hs):
                    at = slice(h * HD, (h + 1) * HD)
                    head = slot * hs + h
                    qt[i, head] = query[at].astype(BF16)
                    kt[head, :, cols] = key[at].astype(BF16)
                    vt[head, :, cols] = value[at].astype(BF16)
                    kn[head, cols, :] = key[at].T.astype(BF16)
                    vn[head, cols, :] = value[at].T.astype(BF16)

        def attend(i, group):
            cols = slice(i * rows, (i + 1) * rows)
            parts = key_parts(i)
            scores = [[masked(dot(kn[h, a:b], qt[i, h]), i, a, b, g) for a, b, g in parts] for h in group]
            tops = []
            for score in scores:
                top = score[0].max(axis=0, keepdims=True)
                for more in score[1:]:
                    top = jnp.maximum(top, more.max(axis=0, keepdims=True))
                tops.append(top)
            powers = [[jnp.exp(one - top) for one in score] for score, top in zip(scores, tops, strict=True)]
            totals = [sum(row_sum(one) for one in power) for power in powers]
            contexts = [
                sum(dot(vt[h, :, a:b], one.astype(BF16)) for one, (a, b, _) in zip(power, parts, strict=True))
                for h, power in zip(group, powers, strict=True)
            ]
            for h, top, total, context in zip(group, tops, totals, contexts, strict=True):
                ctx[h, :, cols] = (context / total).astype(BF16)
                lse[i, h] = top + jnp.log(total)

        def each_block(i, body, number):
            for block in range(blocks):

                @pl.when(i == block)
                def _():
                    for first in range(0, heads, number):
                        body(block, range(first, first + number))

        def attention_rows(i):
            @pl.when(last_section & (i == 0))
            def _():
                hop_copy(0, xbuf).wait_recv()
                hop_core(0, xbuf).start()

            @pl.when(last_section)
            def _():
                hop_core(i, xbuf).wait()

            project(i)
            each_block(i, attend, HEADS_FORWARD)

            @pl.when(i == 0)
            def _():
                have(1)

            context = ctx[:, :, at_row(i)].reshape(heads * HD, rows)
            pair_send(0, shifted(i), dot(context, wo[...].reshape(heads * HD, width), TN))

            for step, (which, cut) in enumerate(((2, 0), (2, 1), (3, 0), (3, 1))):

                @pl.when((i == step) & first_section)
                def _():
                    pass_on(which, cut)

            @pl.when(last_section & (i < blocks - 1))
            def _():
                hop_copy(i + 1, xbuf).wait_recv()
                hop_core(i + 1, xbuf).start()

        def up_rows(i):
            @pl.when(i == 0)
            def _():
                have(2)

            branch = pair_sum(0, shifted(i)) + out_bias
            middle = expanded(xbuf[i]) + centred(branch)
            pool[mid_at(i), :] = middle
            normed = middle * norm_factor(middle) * mlp_gain
            normed = normed.astype(BF16)
            for slot in range(slots):
                pre = dot(normed, wu[slot][...]) + mc[slot, 4:5, :]
                square = pre * pre
                bend = jnp.tanh(pre * (GELU_C + (GELU_C * GELU_A) * square))
                grow = 0.5 + 0.5 * bend
                value = pre * grow
                hid[slot, i] = value.astype(BF16)
                slope = GELU_C + (3.0 * GELU_C * GELU_A) * square
                gp[slot, i] = (grow + value * (1.0 - bend) * slope).astype(BF16)

            for step, cut in ((0, 2), (1, 3)):

                @pl.when((i == step) & first_section)
                def _():
                    pass_on(3, cut)

        def down_rows(i):
            @pl.when(i == 0)
            def _():
                have(3)

            units_all = jnp.concatenate([hid[slot, i] for slot in range(slots)], axis=1)
            both = jnp.concatenate([wd[slot][...] for slot in range(slots)], axis=1)
            pair_send(1, shifted(i), dot(units_all, both, NT))

        def keep_out(i, value):
            @pl.when((i == t) | (i == t_x))
            def _():
                outt[jnp.where(i == t, 0, 1)] = value.T.astype(BF16)

        def result_rows(i):
            result = pool[mid_at(i), :] + centred(pair_sum(1, shifted(i)) + down_bias)
            keep_out(i, result)

            @pl.when(first_section)
            def _():
                @pl.when(i >= 2)
                def _():
                    hop_copy(i - 2, xbuf).wait_send()

                lane = lax.broadcasted_iota(jnp.int32, result.shape, 1)
                resb[lax.rem(i, 2)] = jnp.where(lane == width - 1, 0.0, result).astype(BF16)
                hop_copy(i, xbuf).start()

        def forward(step):
            i_up = jnp.where(first_section, step - blocks, step - 1)
            i_down = jnp.where(first_section, step - 2 * blocks, step - 1)
            i_res = i_down - 1
            some_res = (i_res >= 0) & (i_res < blocks)

            @pl.when(step < blocks)
            def _():
                attention_rows(step)

            @pl.when(last_section & some_res & (i_res < blocks - 1))
            def _():
                result_rows(i_res)

            @pl.when((i_up >= 0) & (i_up < blocks))
            def _():
                up_rows(i_up)

            @pl.when((i_down >= 0) & (i_down < blocks))
            def _():
                down_rows(i_down)

            @pl.when(first_section & some_res)
            def _():
                result_rows(i_res)

        loop(3 * blocks + 1, forward)

        def rows_out(target, which):
            return (
                pltpu.make_async_copy(outt.at[0], target.at[xh], sl.at[2]),
                send(outt.at[1], target.at[xh], so, (which,), to_x),
            )

        act_copies = rows_out(act, 0)

        @pl.when(first_section)
        def _():
            loop(2, lambda i: hop_copy(blocks - 2 + i, xbuf).wait_send())

        def other_at(k):
            row = k * CHUNK
            third = jnp.where(row < 3 * rows, 0, jnp.where(row < 6 * rows, 1, 2))
            place = row - third * 3 * rows
            kind = jnp.where(place < rows, 0, jnp.where(place < 2 * rows, 1, 2))
            row = kind * (length - rows) + (blocks - 1 - third) * rows + place
            return pl.ds(pl.multiple_of(row, CHUNK), CHUNK)

        def own_at(k):
            row = k * CHUNK
            third = jnp.where(row < 3 * rows, 0, jnp.where(row < 6 * rows, 1, 2))
            place = row - third * 3 * rows
            down = jnp.where(place < rows, place + 3 * rows, place + 6 * rows)
            up = jnp.where(place < 2 * rows, place + rows, place + 4 * rows)
            rest = jnp.where(place < rows, place, place + 3 * rows)
            row = jnp.where(third == 0, down, jnp.where(third == 1, up, rest))
            return pl.ds(pl.multiple_of(row, CHUNK), CHUNK)

        def x_copy(k):
            return send(ex.at[other_at(k)], xrec.at[k], sr, (k,), to_x)

        def put(turn, first, value):
            @pl.when(turn == 0)
            def _():
                for k in range(value.shape[0] // CHUNK):
                    ex[other_at(first + k), :] = value[k * CHUNK : (k + 1) * CHUNK].astype(BF16)

            @pl.when(turn == 1)
            def _():
                for k in range(value.shape[0] // CHUNK):
                    pool[own_at(first + k), :] = value[k * CHUNK : (k + 1) * CHUNK]

        def start(turn, first, number):
            @pl.when(turn == 0)
            def _():
                loop(number, lambda k: x_copy(first + k).start())

        tile = 256
        tiles = width // tile

        def down_part(turn, k):
            at = pl.ds(pl.multiple_of(k * tile, tile), tile)
            first = k * (tile // CHUNK)
            put(turn, first, dot(gmt[at, :], hid[1 - turn].reshape(length, units)))
            start(turn, first, tile // CHUNK)

        def up_part(turn, k):
            at = pl.ds(pl.multiple_of(k * tile, tile), tile)
            first = width // CHUNK + k * (tile // CHUNK)
            put(turn, first, dot(n2t[at, :], gp[1 - turn].reshape(length, units)))
            start(turn, first, tile // CHUNK)

        def turn_normed(i):
            middle = pool[mid_at(i), :]
            n2t[:, at_row(i)] = (middle * norm_factor(middle) * mlp_gain).T.astype(BF16)

        def down_grads(turn):
            loop(tiles, lambda k: down_part(turn, k))

        def up_grads(turn):
            loop(tiles, lambda k: up_part(turn, k))

        middle = count // 2
        on_left = d < middle
        depth = jnp.where(on_left, d, count - 1 - d)
        has_outer = depth > 0
        is_mid = depth == middle - 1
        inner = (s, t, jnp.where(on_left, d + 1, d - 1))
        outer = (s, t, jnp.where(on_left, d - 1, d + 1))
        lag_in = LAG * depth
        lag_mid = LAG * middle
        lag_out = lag_mid + LAG * (middle - 1 - depth)
        lag_all = lag_mid + LAG * (middle - 1)

        def fin_at(k):
            return pl.ds(pl.multiple_of(k * CHUNK, CHUNK), CHUNK)

        def in_copy(k):
            return send(xrec.at[k], cin.at[k], sc, (0, k), inner)

        def cross_copy(k):
            return send(xrec.at[k], wud.at[fin_at(k)], sc, (1, k), inner)

        def out_copy(k):
            return send(wud.at[fin_at(k)], wud.at[fin_at(k)], sc, (2, k), outer)

        outs, place = [], 0
        for which, name in enumerate(("down", "up", "qkv", "out")):
            number = r[name].shape[0]
            copy = pltpu.make_async_copy(wud.at[pl.ds(place, number)], r[name], so.at[0, 2 + which])
            place += number
            outs.append((place // CHUNK - 1, copy))

        def matrix_out(k):
            for final, copy in outs:

                @pl.when(k == final)
                def _():
                    copy.start()

        small_x = send(soth, srec, ss, (0,), to_x)
        s_in = send(sown, scin, ss, (1,), inner)
        s_cross = send(sown, sfin, ss, (2,), inner)
        s_out = send(sfin, sfin, ss, (3,), outer)

        def reduce_small(it):
            begin = chunks - 4

            @pl.when(it == begin)
            def _():
                small_x.wait()
                sown[...] = sown[...] + srec[...]

            @pl.when(it == begin + lag_in)
            def _():
                @pl.when(has_outer)
                def _():
                    s_in.wait_recv()
                    sown[...] = sown[...] + scin[...]

                @pl.when(jnp.logical_not(is_mid))
                def _():
                    s_in.start()

                @pl.when(is_mid)
                def _():
                    s_cross.start()

            @pl.when(it == begin + lag_out)
            def _():
                @pl.when(is_mid)
                def _():
                    s_cross.wait()
                    sfin[...] = sfin[...] + sown[...]

                @pl.when(jnp.logical_not(is_mid))
                def _():
                    s_out.wait_recv()

                @pl.when(has_outer)
                def _():
                    s_out.start()

        def reduce(it):
            @pl.when((it == 0) & is_mid)
            def _():
                pl.semaphore_signal(ready, inc=1, device_id=inner, device_id_type=MESH)

            @pl.when(it < chunks)
            def _():
                k = it
                x_copy(k).wait()
                xrec[k] = (pool[own_at(k), :] + xrec[k].astype(F32)).astype(BF16)

            k_in = it - lag_in

            @pl.when((k_in >= 0) & (k_in < chunks))
            def _():
                k = k_in

                @pl.when(has_outer)
                def _():
                    in_copy(k).wait_recv()
                    xrec[k] = (xrec[k].astype(F32) + cin[k].astype(F32)).astype(BF16)

                @pl.when(jnp.logical_not(is_mid))
                def _():
                    in_copy(k).start()

                @pl.when(is_mid)
                def _():
                    @pl.when(k == 0)
                    def _():
                        pl.semaphore_wait(ready, 1)

                    cross_copy(k).start()

            k_out = it - lag_out

            @pl.when((k_out >= 0) & (k_out < chunks))
            def _():
                k = k_out

                @pl.when(is_mid)
                def _():
                    cross_copy(k).wait_recv()
                    wud[fin_at(k), :] = (xrec[k].astype(F32) + wud[fin_at(k), :].astype(F32)).astype(BF16)

                @pl.when(jnp.logical_not(is_mid))
                def _():
                    out_copy(k).wait_recv()

                @pl.when(has_outer)
                def _():
                    out_copy(k).start()

                matrix_out(k)

            reduce_small(it)

        def grad_rows(i):
            @pl.when(first_section)
            def _():
                hop_copy(i, cotb).wait_recv()
                hop_core(i, cotb).start()
                hop_core(i, cotb).wait()
                turn_grad(i)

        def turn_grad(i):
            gmt[:, at_row(i)] = centred(cotb[i].astype(F32)).T.astype(BF16)

        def down_back(i):
            grad = centred(cotb[i].astype(F32))
            pool[grad_at(i), :] = grad
            grad = grad.astype(BF16)
            sown[3:4, :] += row_sum(grad.astype(F32))
            befores = []
            for slot, sums in ((0, sown), (1, soth)):
                before = (dot(grad, wd[slot][...]) * gp[slot, i].astype(F32)).astype(BF16)
                gp[slot, i] = before
                sums[4:5, :] += row_sum(before.astype(F32))
                befores.append(before)
            both = jnp.concatenate([wu[slot][...] for slot in range(slots)], axis=1)
            pair_send(0, i, dot(jnp.concatenate(befores, axis=1), both, NT))

        def out_back(i):
            grad, gain_grad = norm_back(pair_sum(0, i), pool[mid_at(i), :], mlp_gain)
            sown[2:3, :] += gain_grad
            grad = grad + pool[grad_at(i), :]
            pool[grad_at(i), :] = grad
            grad = grad.astype(BF16)
            gat[i] = grad
            sown[1:2, :] += row_sum(grad.astype(F32))
            back = dot(wo[...].reshape(heads * HD, width), grad, NT).astype(BF16)
            for h in range(heads):
                dot_[i, h] = back[h * HD : (h + 1) * HD]

        def attend_back(i, group):
            parts = key_parts(i)
            cols = slice(i * rows, (i + 1) * rows)
            masks = [jnp.where(allowed(i, a, b, g), 0.0, NEGATIVE) for a, b, g in parts]
            probs, g_probs = [], []
            for h in group:
                less = [mask - lse[i, h] for mask in masks]
                probs.append([jnp.exp(dot(kn[h, a:b], qt[i, h]) + one) for one, (a, b, _) in zip(less, parts, strict=True)])
                g_probs.append([dot(vn[h, a:b], dot_[i, h]) for a, b, _ in parts])
            centres = [
                sum(row_sum(x * y) for x, y in zip(prob, g_prob, strict=True))
                for prob, g_prob in zip(probs, g_probs, strict=True)
            ]
            g_scores = [
                [(x * (y - centre)).astype(BF16) for x, y in zip(prob, g_prob, strict=True)]
                for prob, g_prob, centre in zip(probs, g_probs, centres, strict=True)
            ]
            g_values = [[dot(dot_[i, h], x.astype(BF16), NT) for x in prob] for h, prob in zip(group, probs, strict=True)]
            g_keys = [[dot(qt[i, h], x, NT) for x in g_score] for h, g_score in zip(group, g_scores, strict=True)]
            g_queries = [
                sum(dot(kt[h, :, a:b], x) for x, (a, b, _) in zip(g_score, parts, strict=True))
                for h, g_score in zip(group, g_scores, strict=True)
            ]
            for h, g_value, g_key, g_query in zip(group, g_values, g_keys, g_queries, strict=True):
                slot, place = h // hs, h % hs
                for (a, b, _), value, key in zip(parts, g_value, g_key, strict=True):
                    if i == blocks - 1:
                        dv[h, :, a:b] = value
                        dk[h, :, a:b] = key
                    else:
                        dv[h, :, a:b] += value
                        dk[h, :, a:b] += key
                dqkv[slot, 0, place, :, cols] = (g_query * SCALE).astype(BF16)
                dqkv[slot, 1, place, :, cols] = dk[h, :, cols].astype(BF16)
                dqkv[slot, 2, place, :, cols] = dv[h, :, cols].astype(BF16)

        def qkv_back(i):
            three = dqkv[:, :, :, :, at_row(i)].reshape(slots * 3 * part, rows)
            pair_send(1, i, dot(three, wq[...].reshape(slots * 3 * part, width), TN))

        def in_back(i):
            grad, gain_grad = norm_back(pair_sum(1, i), expanded(xbuf[i]), attn_gain)
            sown[0:1, :] += gain_grad
            grad = grad + pool[grad_at(i), :]
            grad = grad - grad[:, width - 1 :]
            keep_out(i, grad)

            @pl.when(last_section)
            def _():
                @pl.when(i < blocks - 2)
                def _():
                    hop_copy(i + 2, cotb).wait_send()

                resb[lax.rem(i, 2)] = grad.astype(BF16)
                hop_copy(i, cotb).start()

        def advance(step, place):
            def body(it, carry):
                reduce(it)
                return carry

            first, stop = 0, 0
            for at, (lo, hi) in EARLY[place].items():
                first = jnp.where(first_section & (step == at), lo, first)
                stop = jnp.where(first_section & (step == at), hi, stop)
            lax.fori_loop(first, stop, body, 0)

        def planned(step, name):
            found = -1
            for at, (first, last) in enumerate(zip(*PLAN[name], strict=True)):
                found = jnp.where(step == at, jnp.where(first_section, first, last), found)
            return found

        def turns(first, stop, body):
            def one(turn, carry):
                body(turn)
                return carry

            lax.fori_loop(first, stop, one, 0)

        def backward(step):
            n_down, n_in, n_rest, n_late = (planned(step, name) for name in ("down", "in", "rest", "late"))
            n_grad = planned(step, "grads")
            last = blocks - 1
            advance(step, 3)

            @pl.when(step == jnp.where(first_section, blocks - 2, 2 * blocks - 1))
            def _():
                loop(blocks, turn_normed)

            @pl.when(last_section & (step == 2 * blocks - 1))
            def _():
                loop(blocks, turn_grad)

            @pl.when(n_down >= 0)
            def _():
                grad_rows(last - n_down)

            early = jnp.where(n_grad == 0, 1, 0)
            turns(0, early, down_grads)

            @pl.when(n_down >= 0)
            def _():
                down_back(last - n_down)

            @pl.when(step == 0)
            def _():
                @pl.when(last_section)
                def _():
                    result_rows(last)

                for copy in act_copies:
                    copy.start()

            @pl.when((n_grad == 0) | (n_grad == 2))
            def _():
                turns(early, 2, down_grads)
                advance(step, 4)

            @pl.when(n_in == 0)
            def _():
                for copy in act_copies:
                    copy.wait()

            @pl.when(n_in >= 0)
            def _():
                in_back(last - n_in)

            @pl.when(n_rest >= 0)
            def _():
                i = last - n_rest
                out_back(i)
                advance(step, 0)

                @pl.when(n_late >= 0)
                def _():
                    in_back(last - n_late)

                @pl.when(n_grad == 1)
                def _():
                    loop(2, up_grads)

                each_block(i, attend_back, HEADS_BACKWARD)
                advance(step, 1)
                qkv_back(i)
                advance(step, 2)

            @pl.when(n_grad == 2)
            def _():
                loop(2, up_grads)

        loop(len(PLAN["in"][0]), backward)
        ones = jnp.ones((8, length), BF16)
        sown[5:6, : 3 * part] = dot(ones, dqkv[0].reshape(3 * part, length), NT)[0:1]
        soth[5:6, : 3 * part] = dot(ones, dqkv[1].reshape(3 * part, length), NT)[0:1]
        soth[0:4, :] = sown[0:4, :]
        small_x.start()

        def attention_grads(turn):
            slot = 1 - turn

            def qkv_part(k):
                first = (2 * width) // CHUNK + k * (part // CHUNK)
                put(turn, first, dot(dqkv[slot, k].reshape(part, length), nrm[...].reshape(length, width)))

            loop(3, qkv_part)
            first = (2 * width + 3 * part) // CHUNK
            context = ctx[pl.ds(slot * hs, hs)].reshape(part, length)
            put(turn, first, dot(context, gat[...].reshape(length, width)))
            start(turn, 2 * (width // CHUNK), chunks - 2 * (width // CHUNK))

        loop(2, attention_grads)
        eg_copies = rows_out(eg, 1)
        for copy in eg_copies:
            copy.start()

        def rest(it, carry):
            reduce(it)
            return carry

        begun = max(hi for place in EARLY for _, hi in place.values())
        lax.fori_loop(jnp.where(first_section, begun, 0), chunks + lag_all, rest, 0)
        small[...] = sfin[...]

        @pl.when(jnp.logical_not(is_mid))
        def _():
            s_in.wait_send()

        @pl.when(has_outer)
        def _():
            s_out.wait_send()

        def drain(k):
            @pl.when(jnp.logical_not(is_mid))
            def _():
                in_copy(k).wait_send()

            @pl.when(is_mid)
            def _():
                cross_copy(k).wait_send()

            @pl.when(has_outer)
            def _():
                out_copy(k).wait_send()

        loop(chunks, drain)
        for _, copy in outs:
            copy.wait()

        @pl.when(last_section)
        def _():
            loop(2, lambda i: hop_copy(i, cotb).wait_send())

        for copy in eg_copies:
            copy.wait()

    return kernel


def per_device(
    block_input,
    segments,
    cotangent,
    attn_gain,
    qkv_weight,
    qv_bias,
    out_weight,
    out_bias,
    mlp_gain,
    up_projection_weight,
    up_bias,
    down_projection_weight,
    down_bias,
):
    micros, rows, _, kept = block_input.shape
    width = qkv_weight.shape[1]
    part = qkv_weight.shape[3]
    units = up_projection_weight.shape[2]
    blocks = lax.axis_size("tensor")
    count = lax.axis_size("dp")
    length = blocks * rows
    slots = 2
    hs = part // HD
    heads = slots * hs
    chunks = (2 * width + 4 * part) // CHUNK

    def features_first(array):
        first = array[:, :, 0, :].transpose(2, 0, 1)
        return jnp.pad(first, ((0, width - kept), (0, 0), (0, 0))).transpose(1, 0, 2)

    inputs = {
        "xin": features_first(block_input),
        "cot": features_first(cotangent),
        "wqh": qkv_weight[0].transpose(1, 2, 0).reshape(3 * part, width),
        "woh": out_weight[0],
        "wuh": up_projection_weight[0],
        "wdh": down_projection_weight[0],
        "attn_gain": attn_gain,
        "mlp_gain": mlp_gain,
        "out_bias": out_bias,
        "down_bias": down_bias,
        "up_bias": up_bias,
        "qv_bias": qv_bias,
        "seg": segments,
    }
    outputs = {
        "act": ((micros, width, rows), BF16),
        "eg": ((micros, width, rows), BF16),
        "down": ((width, units), BF16),
        "up": ((width, units), BF16),
        "qkv": ((3 * part, width), BF16),
        "out": ((part, width), BF16),
        "small": ((8, width), F32),
    }
    scratch = {
        "wq": ((slots, 3 * part, width), BF16),
        "wo": ((slots, part, width), BF16),
        "wud": ((2 * slots * width, units), BF16),
        "mc": ((slots, 8, width), F32),
        "xbuf": ((blocks, rows, width), BF16),
        "cotb": ((blocks, rows, width), BF16),
        "resb": ((2, rows, width), BF16),
        "outt": ((2, width, rows), BF16),
        "pool": ((max(2 * length, chunks * CHUNK), width), F32),
        "nrm": ((blocks, rows, width), BF16),
        "n2t": ((width, length), BF16),
        "qt": ((blocks, heads, HD, rows), BF16),
        "kt": ((heads, HD, length), BF16),
        "vt": ((heads, HD, length), BF16),
        "kn": ((heads, length, HD), BF16),
        "vn": ((heads, length, HD), BF16),
        "ctx": ((heads, HD, length), BF16),
        "lse": ((blocks, heads, 1, rows), F32),
        "segc": ((length, 128), F32),
        "gp": ((slots, blocks, rows, units), BF16),
        "hid": ((slots, blocks, rows, units), BF16),
        "gmt": ((width, length), BF16),
        "gat": ((blocks, rows, width), BF16),
        "dot": ((blocks, heads, HD, rows), BF16),
        "dqkv": ((slots, 3, hs, HD, length), BF16),
        "dk": ((heads, HD, length), F32),
        "dv": ((heads, HD, length), F32),
        "ex": ((4 * length, width), BF16),
        "xrec": ((chunks, CHUNK, width), BF16),
        "cin": ((chunks, CHUNK, width), BF16),
        "sown": ((8, width), F32),
        "soth": ((8, width), F32),
        "srec": ((8, width), F32),
        "scin": ((8, width), F32),
        "sfin": ((8, width), F32),
    }
    dma = pltpu.SemaphoreType.DMA
    semaphores = {
        "sl": dma((8,)),
        "sg": dma((2, 4)),
        "sw": dma((2, 2, 16)),
        "se": dma((2, 2, blocks)),
        "sh": dma((2, 2, blocks)),
        "so": dma((2, 6)),
        "sr": dma((2, chunks)),
        "sc": dma((2, 3, chunks)),
        "ss": dma((2, 4)),
        "ready": pltpu.SemaphoreType.REGULAR,
    }
    in_vmem = {"attn_gain", "mlp_gain", "out_bias", "down_bias", "up_bias", "qv_bias", "seg", "small"}

    def spec(name):
        return pl.BlockSpec(memory_space=pltpu.VMEM if name in in_vmem else pl.ANY)

    names = [*inputs, *outputs, *scratch, *semaphores]
    act, eg, down, up, qkv, out, small = pl.pallas_call(
        make_kernel(names, count),
        out_shape=[jax.ShapeDtypeStruct(*item) for item in outputs.values()],
        in_specs=[spec(name) for name in inputs],
        out_specs=[spec(name) for name in outputs],
        scratch_shapes=[pltpu.VMEM(*item) for item in scratch.values()] + list(semaphores.values()),
        compiler_params=pltpu.CompilerParams(
            collective_id=0, has_side_effects=True, vmem_limit_bytes=63 * 1024 * 1024
        ),
        name="layers",
    )(*inputs.values())

    def positions_first(array):
        return array[:, :kept, :].transpose(0, 2, 1)[None, :, :, None, :]

    qv = small[5, : 3 * part].reshape(3, part)
    return (
        positions_first(act),
        positions_first(eg).astype(F32),
        small[0:1],
        qkv.reshape(3, part, width).transpose(2, 0, 1).astype(F32)[None],
        qv[0::2][None],
        out.astype(F32)[None],
        small[1:2],
        small[2:3],
        up.astype(F32)[None],
        small[4:5, :units],
        down.astype(F32)[None],
        small[3:4],
    )


def solution(mesh):
    in_specs = (
        P(None, "tensor", "dp", None),
        P(None, "dp", None),
        P(None, "tensor", "dp", None),
        P("section", None),
        P("section", None, None, "tensor"),
        P("section", None, "tensor"),
        P("section", "tensor", None),
        P("section", None),
        P("section", None),
        P("section", None, "tensor"),
        P("section", "tensor"),
        P("section", None, "tensor"),
        P("section", None),
    )
    out_specs = (
        P("section", None, "tensor", "dp", None),
        P("section", None, "tensor", "dp", None),
        P("section", None),
        P("section", None, None, "tensor"),
        P("section", None, "tensor"),
        P("section", "tensor", None),
        P("section", None),
        P("section", None),
        P("section", None, "tensor"),
        P("section", "tensor"),
        P("section", None, "tensor"),
        P("section", None),
    )
    return jax.shard_map(
        per_device, mesh=mesh, in_specs=in_specs, out_specs=out_specs, check_vma=False
    )
```
